32 devices in a mesh: dp: 4 (over y, x), fsdp: 8 (over z, core).
Axes of the slice: x: 2, y: 2, z: 4, core: 2. Of those that a mesh axis runs over, the one named last changes fastest.
Arguments:
- tokens: bfloat16 [4, 8192, 512], P('dp', 'fsdp'), may hold values from -6 to 6
- offsets: int32 [4, 5], P('dp'), may hold values from 0 to 8192, as said below
- padding: int32 [4, 8192], P('dp', 'fsdp'), may hold values from 0 to 1, as said below
- feature_bank: float32 [64, 256], replicated, may hold values from -5 to 5
- ln1_gain: bfloat16 [512], P(('dp', 'fsdp')), may hold values from 0.5 to 1.5
- ln1_bias: bfloat16 [512], P(('dp', 'fsdp')), may hold values from -3 to 3
- w_qkv: bfloat16 [512, 1536], P(('dp', 'fsdp')), may hold values from -0.25 to 0.25
- w_out: bfloat16 [512, 512], P(('dp', 'fsdp')), may hold values from -6 to 6
- ln2_gain: bfloat16 [512], P(('dp', 'fsdp')), may hold values from 0.5 to 1.5
- ln2_bias: bfloat16 [512], P(('dp', 'fsdp')), may hold values from -3 to 3
- w_up: bfloat16 [512, 2048], P(('dp', 'fsdp')), may hold values from -0.25 to 0.25
- b_up: bfloat16 [2048], P(('dp', 'fsdp')), may hold values from -3 to 3
- w_down: bfloat16 [2048, 512], P(('dp', 'fsdp')), may hold values from -0.125 to 0.125
- b_down: bfloat16 [512], P(('dp', 'fsdp')), may hold values from -3 to 3
- cotangent: bfloat16 [4, 8192, 512], P('dp', 'fsdp'), may hold values from -6 to 6
Outputs:
- mixed: bfloat16 [4, 8192, 512], P('dp', 'fsdp')
- grad_tokens: float32 [4, 8192, 512], P('dp', 'fsdp')
- grad_ln1_gain: float32 [512], P(('dp', 'fsdp'))
- grad_ln1_bias: float32 [512], P(('dp', 'fsdp'))
- grad_w_qkv: float32 [512, 1536], P(('dp', 'fsdp'))
- grad_w_out: float32 [512, 512], P(('dp', 'fsdp'))
- grad_ln2_gain: float32 [512], P(('dp', 'fsdp'))
- grad_ln2_bias: float32 [512], P(('dp', 'fsdp'))
- grad_w_up: float32 [512, 2048], P(('dp', 'fsdp'))
- grad_b_up: float32 [2048], P(('dp', 'fsdp'))
- grad_w_down: float32 [2048, 512], P(('dp', 'fsdp'))
- grad_b_down: float32 [512], P(('dp', 'fsdp'))
The draws below stay inside these ranges and needn't reach their ends.
Inputs may be any that keep to these rules, and one draw needn't show every extreme that they name: Each row's offsets rise from 0 to 8192; cell c of the row holds slots offsets[c] to offsets[c+1] - 1, at least one slot. `padding`: the first slot of every cell is 1.
All inputs are finite; a program needn't handle non-finite values.
Results may differ from the reference program's by a relative error of at most 0.035.
Values may be sent and summed in bfloat16 or wider, within the bound.
No kernel may reach another device: no remote copies, remote signals or barrier semaphores. Data moves between devices by JAX's collectives and lax.ppermute only.
A program may use at most 192 MiB of HBM per device.

```python
import jax
import jax.numpy as jnp
from jax import lax

D = 512
HEADS = 8
FF = 2048
FEATS = 256
HEAD = 64
CELLS = 4
TOK_DEV = 1024
ROWS = 4
SLOTS = 8192


def cell_layout(key):
    short_cells = jax.random.randint(jax.random.fold_in(key, 21), (ROWS, CELLS - 1), TOK_DEV // 8, TOK_DEV // 4 + 1)
    large_index = jax.random.randint(jax.random.fold_in(key, 22), (ROWS, 1), 0, CELLS)
    column = jnp.arange(CELLS, dtype=jnp.int32)[None, :]
    source = jnp.clip(jnp.where(column < large_index, column, column - 1), 0, CELLS - 2)
    picked = jnp.take_along_axis(short_cells, jnp.broadcast_to(source, (ROWS, CELLS)), 1)
    largest = SLOTS - jnp.sum(short_cells, 1, keepdims=True)
    lengths = jnp.where(column == large_index, largest, picked)
    return jnp.concatenate([jnp.zeros((ROWS, 1), jnp.int32), jnp.cumsum(lengths, 1).astype(jnp.int32)], 1)


def draw_offsets(key, part):
    return cell_layout(key)


def draw_padding(key, part):
    layout = cell_layout(key)
    key = jax.random.fold_in(key, 7)
    coins = jax.random.randint(key, (ROWS, SLOTS), 0, 8)
    place = jnp.arange(SLOTS, dtype=jnp.int32)
    starts = jnp.any(place[None, :, None] == layout[:, None, :CELLS], -1)
    return jnp.where(starts | (coins > 0), 1, 0).astype(jnp.int32)


def levels(rng, shape, split, low, high):
    loudness = 1.0
    for dim, parts in split:
        heights = jax.random.uniform(jax.random.fold_in(jax.random.fold_in(rng, 6), dim), (parts,), jnp.float32, low / len(split), high / len(split))
        loudness = loudness * jnp.repeat(jnp.exp(heights), shape[dim] // parts).reshape((-1,) + (1,) * (len(shape) - 1 - dim))
    return loudness


def bell_draw(own_key, dims, scale, bound, split=(), kind=jnp.bfloat16):
    entries = jax.random.normal(own_key, dims, jnp.float32) * scale
    if len(split) > 0:
        entries = levels(own_key, dims, split, -0.22, 0.18) * entries
    return jnp.clip(entries, min=-bound, max=bound).astype(kind)


def setup_inputs(seed: int = 0) -> dict:
    key_of = jax.random.split(jax.random.key(seed), 16)
    return {
        "tokens": bell_draw(key_of[0], (ROWS, SLOTS, D), 1.0, 6.0, ((0, 4), (1, 8))),
        "offsets": draw_offsets(jax.random.fold_in(key_of[15], 71), 0),
        "padding": draw_padding(jax.random.fold_in(key_of[15], 71), 0),
        "feature_bank": bell_draw(key_of[3], (HEAD, FEATS), 1.0, 5.0, (), jnp.float32),
        "ln1_gain": jnp.clip(1.0 + 0.1 * jax.random.normal(key_of[4], (D,), jnp.float32), 0.5, 1.5).astype(jnp.bfloat16),
        "ln1_bias": bell_draw(key_of[5], (D,), 0.3, 3.0, ((0, 32),)),
        "w_qkv": bell_draw(key_of[6], (D, 3 * D), D ** -0.5, 0.25, ((0, 32),)),
        "w_out": bell_draw(key_of[7], (D, D), (max(1, D // TOK_DEV)) ** -0.5, 6.0, ((0, 32),)),
        "ln2_gain": jnp.clip(1.0 + 0.1 * jax.random.normal(key_of[8], (D,), jnp.float32), 0.5, 1.5).astype(jnp.bfloat16),
        "ln2_bias": bell_draw(key_of[9], (D,), 0.3, 3.0, ((0, 32),)),
        "w_up": bell_draw(key_of[10], (D, FF), D ** -0.5, 0.25, ((0, 32),)),
        "b_up": bell_draw(key_of[11], (FF,), 0.5, 3.0, ((0, 32),)),
        "w_down": bell_draw(key_of[12], (FF, D), FF ** -0.5, 0.125, ((0, 32),)),
        "b_down": bell_draw(key_of[13], (D,), 0.5, 3.0, ((0, 32),)),
        "cotangent": bell_draw(key_of[14], (ROWS, SLOTS, D), 1.0, 6.0, ((0, 4), (1, 8))),
    }


@jax.custom_vjp
def low(v):
    return lax.optimization_barrier(v.astype(jnp.bfloat16)).astype(jnp.float32)

@jax.custom_vjp
def low_back(v):
    return v

def low_keep(v):
    return (low(v), None)

def low_pass(kept, grad):
    return (grad,)

def back_keep(v):
    return (v, None)

def back_low(kept, grad):
    return (low(grad),)
low.defvjp(low_keep, low_pass)
low_back.defvjp(back_keep, back_low)

def matmul_hi(left, right):
    return jnp.dot(left, right, precision=lax.Precision.HIGHEST)

def layer_norm(values, gain, shift):
    center = values - lax.optimization_barrier(jnp.mean(values, -1, keepdims=True))
    spread = lax.optimization_barrier(jnp.mean(center * center, -1, keepdims=True))
    return center * lax.rsqrt(spread + 1e-05) * gain + shift

def feature_map(projected, omega):
    scaled = projected.reshape(projected.shape[0], HEADS, HEAD) * HEAD ** (-0.25)
    lifted = jnp.einsum('nhe,em->nhm', scaled, omega, precision=lax.Precision.HIGHEST)
    return jnp.exp(lifted - 0.5 * lax.optimization_barrier(jnp.sum(scaled * scaled, -1, keepdims=True))) * FEATS ** (-0.5)

def layer_row(params, row_x, row_off, row_pad, omega):
    gain_one, shift_one, qkv_full, out_full, gain_two, shift_two, up_full, up_bias, down_full, down_bias = params
    length = row_x.shape[0]
    place = jnp.arange(length, dtype=jnp.int32)
    member = ((place[:, None] >= row_off[None, :-1]) & (place[:, None] < row_off[None, 1:])).astype(jnp.float32)
    keep = row_pad.astype(jnp.float32)[:, None, None]
    normed = low(layer_norm(row_x, gain_one, shift_one))
    project = low_back(matmul_hi(normed, qkv_full))
    query = project[:, :D]
    key_part = project[:, D:2 * D]
    value_part = project[:, 2 * D:]
    q_feat = low(feature_map(query, omega))
    k_feat = low(keep * feature_map(key_part, omega))
    values = low(value_part.reshape(length, HEADS, HEAD))
    state = jnp.stack([jnp.einsum('nhm,nhe->hme', k_feat * member[:, column, None, None], values, precision=lax.Precision.HIGHEST) for column in range(CELLS)])
    totals = jnp.einsum('nc,nhm->chm', member, k_feat, precision=lax.Precision.HIGHEST)
    state = low(low_back(state))
    totals = low(low_back(totals))
    numer = jnp.zeros((length, HEADS, HEAD), jnp.float32)
    for column in range(CELLS):
        numer = numer + member[:, column, None, None] * jnp.einsum('nhm,hme->nhe', q_feat, state[column], precision=lax.Precision.HIGHEST)
    denom = jnp.einsum('nc,nch->nh', member, jnp.einsum('nhm,chm->nch', q_feat, totals, precision=lax.Precision.HIGHEST), precision=lax.Precision.HIGHEST)
    numer = low_back(numer)
    denom = low_back(denom)
    attend = low(low_back(keep * numer / denom[:, :, None]))
    middle = row_x + low_back(matmul_hi(attend.reshape(length, D), out_full))
    normed_two = low(layer_norm(middle, gain_two, shift_two))
    hidden = low_back(matmul_hi(normed_two, up_full) + up_bias)
    active = low(jax.nn.gelu(hidden))
    return middle + matmul_hi(active, down_full) + down_bias

def reference(tokens, offsets, padding, feature_bank, ln1_gain, ln1_bias, w_qkv, w_out, ln2_gain, ln2_bias, w_up, b_up, w_down, b_down, cotangent):
    omega = feature_bank.astype(jnp.float32)
    params = tuple((weight_item.astype(jnp.float32) for weight_item in (ln1_gain, ln1_bias, w_qkv, w_out, ln2_gain, ln2_bias, w_up, b_up, w_down, b_down)))
    inputs_f = tokens.astype(jnp.float32)

    def forward(weights, activations):

        def one_row(carried, pieces):
            return (carried, layer_row(weights, pieces[0], pieces[1], pieces[2], omega))
        _, result = lax.scan(jax.checkpoint(one_row), jnp.zeros((), jnp.float32), (activations, offsets, padding))
        return result
    mixed, pullback = jax.vjp(forward, params, inputs_f)
    grad_params, grad_tokens = pullback(cotangent.astype(jnp.float32))
    return (mixed.astype(jnp.bfloat16), grad_tokens, grad_params[0], grad_params[1], grad_params[2], grad_params[3], grad_params[4], grad_params[5], grad_params[6], grad_params[7], grad_params[8], grad_params[9])
```

```python
import functools
import math

import jax
import jax.numpy as jnp
from jax import lax
from jax.experimental import pallas as pl
from jax.experimental.pallas import tpu as pltpu
from jax.sharding import PartitionSpec as P

HEADS = 8
FEATS = 256
HEAD = 64
PAIRS = HEADS // 2
SCALE = HEAD ** (-0.25)
LOGF = 0.5 * math.log(FEATS)
BLK = 256
KVROWS = 272
BF = jnp.bfloat16
F32 = jnp.float32
VMEM_LIMIT = 56 * 1024 * 1024


def dot(a, b):
    return jnp.dot(a, b, preferred_element_type=F32)


def dot_nt(a, b):
    return lax.dot_general(a, b, (((1,), (1,)), ((), ())), preferred_element_type=F32)


def dot_tn(a, b):
    return lax.dot_general(a, b, (((0,), (0,)), ((), ())), preferred_element_type=F32)


def norm_stats(x):
    width = x.shape[-1]
    c = x - jnp.sum(x, -1, keepdims=True) * (1.0 / width)
    r = lax.rsqrt(jnp.sum(c * c, -1, keepdims=True) * (1.0 / width) + 1e-05)
    return c * r, r


def lane_low(n):
    return lax.broadcasted_iota(jnp.int32, (n, 128), 1) < HEAD


def phi_pair(u, rhs_main, rhs_rest):
    low = lane_low(u.shape[0])
    s = u * SCALE
    hi = s.astype(BF)
    lo = (s - hi.astype(F32)).astype(BF)
    both = jnp.concatenate([hi, lo], 1)
    s2 = s * s
    feats = []
    for odd in (0, 1):
        lifted = dot(both, rhs_main[odd]) + dot(hi, rhs_rest[odd])
        half = jnp.sum(jnp.where(low, 0.0, s2) if odd else jnp.where(low, s2, 0.0), -1, keepdims=True)
        feats.append(jnp.exp(lifted - (0.5 * half + LOGF)))
    return s, feats


def cell_range(sc, blk, cells):
    first = sc[cells + 1] + blk * BLK
    last = first + BLK - 1
    lo = jnp.int32(0)
    hi = jnp.int32(0)
    for c in range(1, cells):
        lo += (sc[c] <= first).astype(jnp.int32)
        hi += (sc[c] <= last).astype(jnp.int32)
    return lo, hi, first


def cell_mask(sc, c, first, cols):
    place = lax.broadcasted_iota(jnp.int32, (BLK, cols), 0) + first
    return (place >= sc[c]) & (place < sc[c + 1])


def store_sums(acc, keep_ref, send_ref, core, cells, summed):
    rows = lax.broadcasted_iota(jnp.int32, (16, FEATS), 0)
    for slot, out in ((0, keep_ref), (1, send_ref)):
        base = (core ^ slot) * PAIRS
        for c in range(cells):
            tail = jnp.zeros((16, FEATS), F32)
            for i in range(PAIRS):
                part = acc[c, base + i]
                body, rest = (part[HEAD:], part[:HEAD]) if i % 2 else (part[:HEAD], part[HEAD:])
                out[c, i * HEAD : (i + 1) * HEAD, :] = body.astype(BF)
                line = jnp.sum(rest, 0, keepdims=True) if summed else rest[0:1]
                tail = jnp.where(rows == i, line, tail)
            out[c, PAIRS * HEAD :, :] = tail.astype(BF)


def load_sums(own_ref, other_ref, full, core, cells, single):
    rows = lax.broadcasted_iota(jnp.int32, (HEAD, FEATS), 0)
    for slot, src in ((0, own_ref), (1, other_ref)):
        base = (core ^ slot) * PAIRS
        for c in range(cells):
            tail = src[c, PAIRS * HEAD :, :].astype(F32)
            for i in range(PAIRS):
                body = src[c, i * HEAD : (i + 1) * HEAD, :]
                line = jnp.broadcast_to(tail[i : i + 1], (HEAD, FEATS))
                if single:
                    line = jnp.where(rows == 0, line, 0.0)
                line = line.astype(BF)
                if i % 2:
                    full[c, base + i, :HEAD, :] = line
                    full[c, base + i, HEAD:, :] = body
                else:
                    full[c, base + i, :HEAD, :] = body
                    full[c, base + i, HEAD:, :] = line


def key_kernel(
    cells, sc, x, keep, gain, shift, wk, wv, rm, rr, a1_o, sk_o, pk_o, vr_o, kept, sent, acc
):
    blk = pl.program_id(0)

    @pl.when(blk == 0)
    def _():
        acc[...] = jnp.zeros_like(acc)

    z, _ = norm_stats(x[...].astype(F32))
    a1 = (z * gain[...] + shift[...]).astype(BF)
    a1_o[...] = a1
    keys = dot(a1, wk[...])
    vr_o[...] = dot(a1, wv[...]).astype(BF)
    for p in range(PAIRS):
        s, feats = phi_pair(keys[:, 128 * p : 128 * p + 128], rm, rr)
        sk_o[:, 128 * p : 128 * p + 128] = s.astype(BF)
        for odd in (0, 1):
            h = 2 * p + odd
            pk_o[:, FEATS * h : FEATS * (h + 1)] = (keep[...] * feats[odd]).astype(BF)
    lo, hi, first = cell_range(sc, blk, cells)
    low = lane_low(BLK)

    def one(c, carry):
        mask = cell_mask(sc, c, first, 128)
        for p in range(PAIRS):
            v = vr_o[:, 128 * p : 128 * p + 128].astype(F32)
            for odd in (0, 1):
                h = 2 * p + odd
                aug = jnp.where(low, 1.0, v) if odd else jnp.where(low, v, 1.0)
                aug = jnp.where(mask, aug, 0.0).astype(BF)
                acc[c, h] += dot_tn(aug, pk_o[:, FEATS * h : FEATS * (h + 1)])
        return carry

    lax.fori_loop(lo, hi + 1, one, 0)

    @pl.when(blk == pl.num_programs(0) - 1)
    def _():
        store_sums(acc, kept, sent, sc[cells + 2], cells, False)


def rows_spec(cols):
    return pl.BlockSpec((BLK, cols), lambda i: (i, 0))


def whole_spec(shape):
    return pl.BlockSpec(shape, lambda i: (0,) * len(shape))


SMEM = pl.BlockSpec(memory_space=pltpu.SMEM)


def params():
    return pltpu.CompilerParams(vmem_limit_bytes=VMEM_LIMIT, dimension_semantics=("arbitrary",))


def sums_shape(cells):
    return (cells, KVROWS, FEATS)


def run_keys(sc, x, keep, gain, shift, wk, wv, rm, rr, cells):
    n, d = x.shape
    return pl.pallas_call(
        functools.partial(key_kernel, cells),
        grid=(n // BLK,),
        in_specs=[
            SMEM, rows_spec(d), rows_spec(1), whole_spec((1, d)), whole_spec((1, d)),
            whole_spec(wk.shape), whole_spec(wv.shape), whole_spec(rm.shape), whole_spec(rr.shape),
        ],
        out_specs=[
            rows_spec(d), rows_spec(d), rows_spec(HEADS * FEATS), rows_spec(d),
            whole_spec(sums_shape(cells)), whole_spec(sums_shape(cells)),
        ],
        out_shape=[
            jax.ShapeDtypeStruct((n, d), BF),
            jax.ShapeDtypeStruct((n, d), BF),
            jax.ShapeDtypeStruct((n, HEADS * FEATS), BF),
            jax.ShapeDtypeStruct((n, d), BF),
            jax.ShapeDtypeStruct(sums_shape(cells), BF),
            jax.ShapeDtypeStruct(sums_shape(cells), BF),
        ],
        scratch_shapes=[pltpu.VMEM((cells, HEADS, 128, FEATS), F32)],
        compiler_params=params(),
        cost_estimate=pl.CostEstimate(flops=8 * 10**9, bytes_accessed=10 * 10**6, transcendentals=2 * 10**6),
        name="keys",
    )(sc, x, keep, gain, shift, wk, wv, rm, rr)


def query_kernel(a1, wq, rm, rr, sq_o, pq_o):
    q = dot(a1[...], wq[...])
    for p in range(PAIRS):
        s, feats = phi_pair(q[:, 128 * p : 128 * p + 128], rm, rr)
        sq_o[:, 128 * p : 128 * p + 128] = s.astype(BF)
        for odd in (0, 1):
            h = 2 * p + odd
            pq_o[:, FEATS * h : FEATS * (h + 1)] = feats[odd].astype(BF)


def run_queries(a1, wq, rm, rr):
    n, d = a1.shape
    return pl.pallas_call(
        query_kernel,
        grid=(n // BLK,),
        in_specs=[rows_spec(d), whole_spec(wq.shape), whole_spec(rm.shape), whole_spec(rr.shape)],
        out_specs=[rows_spec(d), rows_spec(HEADS * FEATS)],
        out_shape=[
            jax.ShapeDtypeStruct((n, d), BF),
            jax.ShapeDtypeStruct((n, HEADS * FEATS), BF),
        ],
        compiler_params=params(),
        cost_estimate=pl.CostEstimate(flops=5 * 10**9, bytes_accessed=7 * 10**6, transcendentals=2 * 10**6),
        name="queries",
    )(a1, wq, rm, rr)


def spread_kernel(cells, sc, kept, got, out):
    for z in range(out.shape[0]):
        c = sc[8 + z]
        out[z] = (kept[c].astype(F32) + got[c].astype(F32)).astype(BF)


def run_spread(sc, kept, got, chips, cells):
    vm = pl.BlockSpec(memory_space=pltpu.VMEM)
    return pl.pallas_call(
        functools.partial(spread_kernel, cells),
        in_specs=[SMEM, vm, vm],
        out_specs=vm,
        out_shape=jax.ShapeDtypeStruct((chips, KVROWS, FEATS), BF),
        compiler_params=pltpu.CompilerParams(vmem_limit_bytes=VMEM_LIMIT),
        cost_estimate=pl.CostEstimate(flops=10**6, bytes_accessed=2 * 10**6, transcendentals=0),
        name="spread",
    )(sc, kept, got)


def collect_kernel(cells, chips, sc, kept, got, far, out):
    me = sc[16]
    before = jnp.zeros((KVROWS, FEATS), F32)
    after = jnp.zeros((KVROWS, FEATS), F32)
    for z in range(chips):
        part = far[z].astype(F32)
        before += jnp.where(z < me, part, 0.0)
        after += jnp.where(z > me, part, 0.0)
    for c in range(cells):
        total = kept[c].astype(F32) + got[c].astype(F32)
        total += jnp.where(sc[17] == c, before, 0.0) + jnp.where(sc[18] == c, after, 0.0)
        out[c] = total.astype(BF)


def run_collect(sc, kept, got, far, cells):
    vm = pl.BlockSpec(memory_space=pltpu.VMEM)
    return pl.pallas_call(
        functools.partial(collect_kernel, cells, far.shape[0]),
        in_specs=[SMEM, vm, vm, vm],
        out_specs=vm,
        out_shape=jax.ShapeDtypeStruct(kept.shape, BF),
        compiler_params=pltpu.CompilerParams(vmem_limit_bytes=VMEM_LIMIT),
        cost_estimate=pl.CostEstimate(flops=10**6, bytes_accessed=2 * 10**6, transcendentals=0),
        name="collect",
    )(sc, kept, got, far)


def middle_kernel(
    cells, sc, x, dy_r, keep_r, pq, own, other, w_out, gain, shift, w_up, b_up, w_down, b_down,
    mixed_o, gr_o, dpre_o, a2_o, ar_o, do_o, dx_o, grads_o, vec_o, vup_o, kept, sent,
    full, acc, num_s, den_s,
):
    blk = pl.program_id(0)

    @pl.when(blk == 0)
    def _():
        acc[...] = jnp.zeros_like(acc)
        vec_o[...] = jnp.zeros_like(vec_o)
        vup_o[...] = jnp.zeros_like(vup_o)
        load_sums(own, other, full, sc[cells + 2], cells, False)

    lo, hi, first = cell_range(sc, blk, cells)
    low = lane_low(BLK)

    def attend(c, carry):
        mask = cell_mask(sc, c, first, 128)
        for p in range(PAIRS):
            h = 2 * p
            lanes = slice(128 * p, 128 * p + 128)
            r0 = dot_nt(pq[:, FEATS * h : FEATS * (h + 1)], full[c, h])
            r1 = dot_nt(pq[:, FEATS * (h + 1) : FEATS * (h + 2)], full[c, h + 1])
            num = jnp.where(low, r0, r1)
            den = pltpu.roll(jnp.where(low, r1, r0), HEAD, 1)
            num_s[:, lanes] = jnp.where(mask, num, num_s[:, lanes])
            den_s[:, lanes] = jnp.where(mask, den, den_s[:, lanes])
        return carry

    lax.fori_loop(lo, hi + 1, attend, 0)
    keep = keep_r[...]
    inv = 1.0 / den_s[...]
    ar = (keep * num_s[...] * inv).astype(BF)
    ar_o[...] = ar
    x2 = x[...].astype(F32) + dot(ar, w_out[...])
    z2, r2 = norm_stats(x2)
    g2 = gain[...]
    a2 = (z2 * g2 + shift[...]).astype(BF)
    a2_o[...] = a2
    dy = dy_r[...]
    mixed = x2 + b_down[...]
    da2 = jnp.zeros_like(x2)
    width = x2.shape[1]
    k0 = math.sqrt(2.0 / math.pi)
    for j in range(w_up.shape[1] // width):
        cols = slice(j * width, (j + 1) * width)
        pre = dot(a2, w_up[:, cols]) + b_up[:, cols]
        sq = pre * pre
        t = jnp.tanh(k0 * pre * (1.0 + 0.044715 * sq))
        half = 0.5 * (1.0 + t)
        slope = half + 0.5 * pre * (1.0 - t * t) * (k0 + (3.0 * 0.044715 * k0) * sq)
        gr = (pre * half).astype(BF)
        gr_o[:, cols] = gr
        mixed += dot(gr, w_down[cols, :])
        dpre = (dot_nt(dy, w_down[cols, :]) * slope).astype(BF)
        dpre_o[:, cols] = dpre
        da2 += dot_nt(dpre, w_up[:, cols])
        vup_o[:, cols] += jnp.sum(dpre.astype(F32), 0, keepdims=True)
    mixed_o[...] = mixed.astype(BF)
    dyf = dy.astype(F32)
    dz = da2 * g2
    m1 = jnp.sum(dz, -1, keepdims=True) * (1.0 / width)
    m2 = jnp.sum(dz * z2, -1, keepdims=True) * (1.0 / width)
    dx2 = dyf + r2 * (dz - m1 - z2 * m2)
    dx_o[...] = dx2
    vec_o[0:1, :] += jnp.sum(da2 * z2, 0, keepdims=True)
    vec_o[1:2, :] += jnp.sum(da2, 0, keepdims=True)
    vec_o[2:3, :] += jnp.sum(dyf, 0, keepdims=True)
    do = dx2.astype(BF)
    do_o[...] = do
    dattn = keep * dot_nt(do, w_out[...]).astype(BF).astype(F32)
    dnum = dattn * inv
    dden = -dnum * num_s[...] * inv
    for p in range(PAIRS):
        lanes = slice(128 * p, 128 * p + 128)
        mine = dnum[:, lanes]
        swap = pltpu.roll(dden[:, lanes], HEAD, 1)
        h = 2 * p
        grads_o[:, 128 * h : 128 * h + 128] = jnp.where(low, mine, swap).astype(BF)
        grads_o[:, 128 * h + 128 : 128 * h + 256] = jnp.where(low, swap, mine).astype(BF)

    def gather(c, carry):
        mask = cell_mask(sc, c, first, 128)
        for h in range(HEADS):
            part = grads_o[:, 128 * h : 128 * h + 128]
            part = jnp.where(mask, part.astype(F32), 0.0).astype(BF)
            acc[c, h] += dot_tn(part, pq[:, FEATS * h : FEATS * (h + 1)])
        return carry

    lax.fori_loop(lo, hi + 1, gather, 0)

    @pl.when(blk == pl.num_programs(0) - 1)
    def _():
        store_sums(acc, kept, sent, sc[cells + 2], cells, True)


def run_middle(sc, x, dy, keep, pq, own, other, w_out, gain, shift, w_up, b_up, w_down, b_down, cells):
    n, d = x.shape
    ff = w_up.shape[1]
    wide = HEADS * 128
    return pl.pallas_call(
        functools.partial(middle_kernel, cells),
        grid=(n // BLK,),
        in_specs=[
            SMEM, rows_spec(d), rows_spec(d), rows_spec(1), rows_spec(HEADS * FEATS),
            whole_spec(own.shape), whole_spec(other.shape), whole_spec((d, d)), whole_spec((1, d)), whole_spec((1, d)),
            whole_spec((d, ff)), whole_spec((1, ff)), whole_spec((ff, d)), whole_spec((1, d)),
        ],
        out_specs=[
            rows_spec(d), rows_spec(ff), rows_spec(ff), rows_spec(d), rows_spec(d), rows_spec(d),
            rows_spec(d), rows_spec(wide), whole_spec((8, d)), whole_spec((1, ff)),
            whole_spec(sums_shape(cells)), whole_spec(sums_shape(cells)),
        ],
        out_shape=[
            jax.ShapeDtypeStruct((n, d), BF),
            jax.ShapeDtypeStruct((n, ff), BF),
            jax.ShapeDtypeStruct((n, ff), BF),
            jax.ShapeDtypeStruct((n, d), BF),
            jax.ShapeDtypeStruct((n, d), BF),
            jax.ShapeDtypeStruct((n, d), BF),
            jax.ShapeDtypeStruct((n, d), F32),
            jax.ShapeDtypeStruct((n, wide), BF),
            jax.ShapeDtypeStruct((8, d), F32),
            jax.ShapeDtypeStruct((1, ff), F32),
            jax.ShapeDtypeStruct(sums_shape(cells), BF),
            jax.ShapeDtypeStruct(sums_shape(cells), BF),
        ],
        scratch_shapes=[
            pltpu.VMEM((cells, HEADS, 128, FEATS), BF),
            pltpu.VMEM((cells, HEADS, 128, FEATS), F32),
            pltpu.VMEM((BLK, d), F32),
            pltpu.VMEM((BLK, d), F32),
        ],
        compiler_params=params(),
        cost_estimate=pl.CostEstimate(flops=14 * 10**9, bytes_accessed=30 * 10**6, transcendentals=2 * 10**6),
        name="middle",
    )(sc, x, dy, keep, pq, own, other, w_out, gain, shift, w_up, b_up, w_down, b_down)


def phi_back(s, feats, rhs, low):
    r0 = dot(feats[0].astype(BF), rhs[0])
    r1 = dot(feats[1].astype(BF), rhs[1])
    total = pltpu.roll(jnp.where(low, r1, r0), HEAD, 1)
    return (jnp.where(low, r0, r1) - s * total) * SCALE


def query_back_kernel(cells, sc, grads, pq, sq, own, other, rhs, dq_o, full, g_s):
    blk = pl.program_id(0)

    @pl.when(blk == 0)
    def _():
        load_sums(own, other, full, sc[cells + 2], cells, False)

    lo, hi, first = cell_range(sc, blk, cells)
    low = lane_low(BLK)

    def one(c, carry):
        mask = cell_mask(sc, c, first, FEATS)
        for h in range(HEADS):
            cols = slice(FEATS * h, FEATS * (h + 1))
            g = dot(grads[:, 128 * h : 128 * h + 128], full[c, h])
            g_s[:, cols] = jnp.where(mask, g, g_s[:, cols])
        return carry

    lax.fori_loop(lo, hi + 1, one, 0)
    for p in range(PAIRS):
        lanes = slice(128 * p, 128 * p + 128)
        feats = []
        for odd in (0, 1):
            cols = slice(FEATS * (2 * p + odd), FEATS * (2 * p + odd + 1))
            feats.append(g_s[:, cols] * pq[:, cols].astype(F32))
        dq_o[:, lanes] = phi_back(sq[:, lanes].astype(F32), feats, rhs, low).astype(BF)


def run_query_back(sc, grads, pq, sq, own, other, rhs, cells):
    n, d = sq.shape
    return pl.pallas_call(
        functools.partial(query_back_kernel, cells),
        grid=(n // BLK,),
        in_specs=[
            SMEM, rows_spec(HEADS * 128), rows_spec(HEADS * FEATS), rows_spec(d),
            whole_spec(own.shape), whole_spec(other.shape), whole_spec(rhs.shape),
        ],
        out_specs=rows_spec(d),
        out_shape=jax.ShapeDtypeStruct((n, d), BF),
        scratch_shapes=[
            pltpu.VMEM((cells, HEADS, 128, FEATS), BF),
            pltpu.VMEM((BLK, HEADS * FEATS), F32),
        ],
        compiler_params=params(),
        cost_estimate=pl.CostEstimate(flops=3 * 10**9, bytes_accessed=8 * 10**6, transcendentals=0),
        name="query_back",
    )(sc, grads, pq, sq, own, other, rhs)


def key_back_kernel(
    cells, sc, x, a1, gain, pk, vr, sk, dq, dx, own, other, rhs, wq, wk, wv, gt_o, dk_o, dv_o, vec_o, full, g_s, v_s
):
    blk = pl.program_id(0)

    @pl.when(blk == 0)
    def _():
        vec_o[...] = jnp.zeros_like(vec_o)
        load_sums(own, other, full, sc[cells + 2], cells, True)

    lo, hi, first = cell_range(sc, blk, cells)
    low = lane_low(BLK)

    def one(c, carry):
        mask = cell_mask(sc, c, first, FEATS)
        narrow = cell_mask(sc, c, first, 128)
        for p in range(PAIRS):
            lanes = slice(128 * p, 128 * p + 128)
            v = vr[:, lanes].astype(F32)
            outs = []
            for odd in (0, 1):
                h = 2 * p + odd
                cols = slice(FEATS * h, FEATS * (h + 1))
                aug = (jnp.where(low, 1.0, v) if odd else jnp.where(low, v, 1.0)).astype(BF)
                g = dot(aug, full[c, h])
                g_s[:, cols] = jnp.where(mask, g, g_s[:, cols])
                outs.append(dot_nt(pk[:, cols], full[c, h]))
            v_s[:, lanes] = jnp.where(narrow, jnp.where(low, outs[0], outs[1]), v_s[:, lanes])
        return carry

    lax.fori_loop(lo, hi + 1, one, 0)
    for p in range(PAIRS):
        lanes = slice(128 * p, 128 * p + 128)
        feats = []
        for odd in (0, 1):
            cols = slice(FEATS * (2 * p + odd), FEATS * (2 * p + odd + 1))
            feats.append(g_s[:, cols] * pk[:, cols].astype(F32))
        dk_o[:, lanes] = phi_back(sk[:, lanes].astype(F32), feats, rhs, low).astype(BF)
    dv = v_s[...].astype(BF)
    dv_o[...] = dv
    da1 = dot_nt(dq[...], wq[...]) + dot_nt(dk_o[...], wk[...]) + dot_nt(dv, wv[...])
    z, r = norm_stats(x[...].astype(F32))
    width = z.shape[1]
    dz = da1 * gain[...]
    m1 = jnp.sum(dz, -1, keepdims=True) * (1.0 / width)
    m2 = jnp.sum(dz * z, -1, keepdims=True) * (1.0 / width)
    gt_o[...] = dx[...] + r * (dz - m1 - z * m2)
    vec_o[0:1, :] += jnp.sum(da1 * z, 0, keepdims=True)
    vec_o[1:2, :] += jnp.sum(da1, 0, keepdims=True)


def run_key_back(sc, x, a1, gain, pk, vr, sk, dq, dx, own, other, rhs, wq, wk, wv, cells):
    n, d = x.shape
    return pl.pallas_call(
        functools.partial(key_back_kernel, cells),
        grid=(n // BLK,),
        in_specs=[
            SMEM, rows_spec(d), rows_spec(d), whole_spec((1, d)), rows_spec(HEADS * FEATS), rows_spec(d),
            rows_spec(d), rows_spec(d), rows_spec(d), whole_spec(own.shape), whole_spec(other.shape),
            whole_spec(rhs.shape), whole_spec(wq.shape), whole_spec(wk.shape), whole_spec(wv.shape),
        ],
        out_specs=[rows_spec(d), rows_spec(d), rows_spec(d), whole_spec((8, d))],
        out_shape=[
            jax.ShapeDtypeStruct((n, d), F32),
            jax.ShapeDtypeStruct((n, d), BF),
            jax.ShapeDtypeStruct((n, d), BF),
            jax.ShapeDtypeStruct((8, d), F32),
        ],
        scratch_shapes=[
            pltpu.VMEM((cells, HEADS, 128, FEATS), BF),
            pltpu.VMEM((BLK, HEADS * FEATS), F32),
            pltpu.VMEM((BLK, d), F32),
        ],
        compiler_params=params(),
        cost_estimate=pl.CostEstimate(flops=5 * 10**9, bytes_accessed=12 * 10**6, transcendentals=0),
        name="key_back",
    )(sc, x, a1, gain, pk, vr, sk, dq, dx, own, other, rhs, wq, wk, wv)


AXES = ("dp", "fsdp")


def pair_axis(x, size, flip, axis):
    return lax.ppermute(x, axis, [(i, i ^ flip) for i in range(size)])


def same_core_groups(dp, fsdp):
    return [[d * fsdp + 2 * z + c for d in range(dp) for z in range(fsdp // 2)] for c in range(2)]


def chip_groups(fsdp):
    return [[2 * z + c for z in range(fsdp // 2)] for c in range(2)]


def local(dp, fsdp, tokens, offsets, padding, feature_bank, ln1_gain, ln1_bias, w_qkv, w_out, ln2_gain, ln2_bias,
          w_up, b_up, w_down, b_down, cotangent):
    ndev = dp * fsdp
    x = tokens[0]
    dy = cotangent[0]
    n, d = x.shape
    ff = w_up.shape[1]
    cells = offsets.shape[1] - 1
    chips = fsdp // 2
    rows = d // ndev
    wide = ff // d
    frow = ff // ndev
    spot = lax.axis_index("fsdp")
    core = spot % 2
    zpos = spot // 2
    bounds = offsets[0]

    starts = jnp.arange(chips, dtype=jnp.int32) * (2 * n)
    inner = bounds[1:cells]
    first_cell = jnp.sum((inner[None, :] <= starts[:, None]).astype(jnp.int32), 1)
    last_cell = jnp.sum((inner[None, :] <= starts[:, None] + (2 * n - 1)).astype(jnp.int32), 1)
    asked = jnp.where(jnp.arange(chips) > zpos, first_cell, last_cell)
    one = lambda v: jnp.reshape(v, (1,)).astype(jnp.int32)
    own_first = jnp.sum((inner <= zpos * (2 * n)).astype(jnp.int32))
    own_last = jnp.sum((inner <= zpos * (2 * n) + (2 * n - 1)).astype(jnp.int32))

    whi = feature_bank.astype(BF)
    wlo = (feature_bank - whi.astype(F32)).astype(BF)
    none = jnp.zeros_like(whi)
    rm = jnp.stack([jnp.concatenate([whi, none, whi, none], 0), jnp.concatenate([none, whi, none, whi], 0)])
    rr = jnp.stack([jnp.concatenate([wlo, none], 0), jnp.concatenate([none, wlo], 0)])
    ones = jnp.ones((FEATS, HEAD), BF)
    rback = jnp.stack([jnp.concatenate([whi.T, ones], 1), jnp.concatenate([ones, whi.T], 1)])
    keep = padding[0].astype(F32)[:, None]

    vecs = jnp.concatenate(
        [v.reshape(rows, -1) for v in (ln1_gain, ln1_bias, ln2_gain, ln2_bias, b_down, b_up)]
        + [jnp.zeros((rows, 128 - 5 - wide), BF)], 1
    )
    paired = dp == 4 and fsdp == 8
    lead = jnp.concatenate([w_qkv[:, d:], vecs], 1)
    rest = (w_qkv[:, :d], w_out, w_up)
    if paired:
        mine = lax.all_to_all(
            jnp.broadcast_to(lead[None], (ndev // 2,) + lead.shape), AXES, 0, 0,
            axis_index_groups=same_core_groups(dp, fsdp), tiled=True,
        )
        theirs = pair_axis(mine, fsdp, 1, "fsdp")
        lead_all = jnp.stack(
            [jnp.where(core == 0, mine, theirs), jnp.where(core == 0, theirs, mine)], 1
        ).reshape(d, -1)
    else:
        lead_all = lax.all_gather(lead, AXES, axis=0, tiled=True)
    body = jnp.concatenate(
        [w_qkv[:, :d], w_out] + [w_up[:, j * d : (j + 1) * d] for j in range(wide)] + [w_down], 0
    )
    body_all = lax.all_gather(body, AXES, axis=0, tiled=True).reshape(ndev, -1, d)
    take = lambda lo, size: body_all[:, lo : lo + size].reshape(ndev * size, d)
    wq = take(0, rows)
    wo = take(rows, rows)
    wup = jnp.concatenate([take((2 + j) * rows, rows) for j in range(wide)], 1)
    wdn = take((2 + wide) * rows, frow)
    wk, wv = lead_all[:, :d], lead_all[:, d : 2 * d]
    vt = lead_all[:, 2 * d :].astype(F32)
    line = lambda i: vt[:, i].reshape(1, d)
    up_bias = vt[:, 5 : 5 + wide].reshape(1, ff)

    sc = jnp.concatenate([bounds, one(spot * n), one(core if paired else jnp.int32(0)), jnp.zeros((1,), jnp.int32)])
    if paired:
        sc = jnp.concatenate([sc, jnp.pad(asked, (0, 8 - chips)), one(zpos), one(own_first), one(own_last)])
    sc = sc.astype(jnp.int32)

    def exchange(kept, sent):
        if not paired:
            total = lax.psum(jnp.stack([kept, sent]), "fsdp")
            return total[0], total[1]
        got = pair_axis(sent, fsdp, 1, "fsdp")
        out = run_spread(sc, kept, got, chips, cells)
        far = lax.all_to_all(out, "fsdp", 0, 0, axis_index_groups=chip_groups(fsdp), tiled=True)
        done = run_collect(sc, kept, got, far, cells)
        return done, pair_axis(done, fsdp, 1, "fsdp")

    a1, sk, pk, vr, kept, sent = run_keys(sc, x, keep, line(0), line(1), wk, wv, rm, rr, cells)
    own, other = exchange(kept, sent)
    sq, pq = run_queries(a1, wq, rm, rr)
    mixed, gr, dpre, a2, ar, do, dx2, grads, vec2, vup, kept, sent = run_middle(
        sc, x, dy, keep, pq, own, other, wo, line(2), line(3), wup, up_bias, wdn, line(4), cells
    )
    d_own, d_other = exchange(kept, sent)
    dq = run_query_back(sc, grads, pq, sq, own, other, rback, cells)

    def blocks(g, size):
        return g.astype(BF).reshape(ndev, size, d)

    gup = dot_tn(a2, dpre)
    gbody = jnp.concatenate(
        [blocks(dot_tn(a1, dq), rows), blocks(dot_tn(ar, do), rows)]
        + [blocks(gup[:, j * d : (j + 1) * d], rows) for j in range(wide)]
        + [blocks(dot_tn(gr, dy), frow)], 1
    )

    def scatter(g, split):
        if not paired:
            return lax.psum_scatter(g.astype(F32), AXES, scatter_dimension=0, tiled=True)[0]
        g = g.reshape((ndev // 2, 2) + g.shape[1:])
        pick = lambda c: lax.dynamic_index_in_dim(g, c, 1, keepdims=False)
        got = pair_axis(pick(1 - core), fsdp, 1, "fsdp")
        half = (pick(core).astype(F32) + got.astype(F32)).astype(BF)
        if split:
            part = lax.all_to_all(half, "dp", 0, 0, tiled=True).reshape((dp, chips) + g.shape[2:])
            half = jnp.sum(part.astype(F32), 0).astype(BF)
            part = lax.all_to_all(half, "fsdp", 0, 0, axis_index_groups=chip_groups(fsdp), tiled=True)
        else:
            part = lax.all_to_all(half, AXES, 0, 0, axis_index_groups=same_core_groups(dp, fsdp), tiled=True)
        return jnp.sum(part.astype(F32), 0)

    gbody = scatter(gbody, True)
    gt, dk, dv, vec1 = run_key_back(
        sc, x, a1, line(0), pk, vr, sk, dq, dx2, d_own, d_other, rback, wq, wk, wv, cells
    )
    vgrads = jnp.concatenate(
        [vec1[0:2].T, vec2[0:3].T, vup.reshape(d, wide), jnp.zeros((d, 128 - 5 - wide), F32)], 1
    )
    glead = jnp.concatenate([dot_tn(a1, dk), dot_tn(a1, dv), vgrads], 1).astype(BF)
    glead = scatter(glead.reshape(ndev, rows, -1), False)
    gvec = glead[:, 2 * d :]
    flat = lambda i: gvec[:, i]
    return (
        mixed[None],
        gt[None],
        flat(0),
        flat(1),
        jnp.concatenate([gbody[:rows], glead[:, : 2 * d]], 1),
        gbody[rows : 2 * rows],
        flat(2),
        flat(3),
        jnp.concatenate([gbody[(2 + j) * rows : (3 + j) * rows] for j in range(wide)], 1),
        gvec[:, 5 : 5 + wide].reshape(-1),
        gbody[(2 + wide) * rows :],
        flat(4),
    )


def solution(mesh):
    both = P(("dp", "fsdp"))
    mat = P(("dp", "fsdp"), None)
    act = P("dp", "fsdp", None)
    return jax.shard_map(
        functools.partial(local, mesh.shape["dp"], mesh.shape["fsdp"]),
        mesh=mesh,
        in_specs=(act, P("dp", None), P("dp", "fsdp"), P(), both, both, mat, mat, both, both, mat, both, mat, both, act),
        out_specs=(act, act, both, both, mat, mat, both, both, mat, both, mat, both),
        check_vma=False,
    )
```

```python
import functools
import math

import jax
import jax.numpy as jnp
from jax import lax
from jax.experimental import pallas as pl
from jax.experimental.pallas import tpu as pltpu
from jax.sharding import PartitionSpec as P

HEADS = 8
FEATS = 256
HEAD = 64
PAIRS = HEADS // 2
SCALE = HEAD ** (-0.25)
LOGF = 0.5 * math.log(FEATS)
BLK = 256
KVROWS = 272
BF = jnp.bfloat16
F32 = jnp.float32
VMEM_LIMIT = 56 * 1024 * 1024


def dot(a, b):
    return jnp.dot(a, b, preferred_element_type=F32)


def dot_nt(a, b):
    return lax.dot_general(a, b, (((1,), (1,)), ((), ())), preferred_element_type=F32)


def dot_tn(a, b):
    return lax.dot_general(a, b, (((0,), (0,)), ((), ())), preferred_element_type=F32)


def norm_stats(x):
    width = x.shape[-1]
    c = x - jnp.sum(x, -1, keepdims=True) * (1.0 / width)
    r = lax.rsqrt(jnp.sum(c * c, -1, keepdims=True) * (1.0 / width) + 1e-05)
    return c * r, r


def lane_low(n):
    return lax.broadcasted_iota(jnp.int32, (n, 128), 1) < HEAD


def phi_pair(u, rhs_main, rhs_rest):
    low = lane_low(u.shape[0])
    s = u * SCALE
    hi = s.astype(BF)
    lo = (s - hi.astype(F32)).astype(BF)
    both = jnp.concatenate([hi, lo], 1)
    s2 = s * s
    feats = []
    for odd in (0, 1):
        lifted = dot(both, rhs_main[odd]) + dot(hi, rhs_rest[odd])
        half = jnp.sum(jnp.where(low, 0.0, s2) if odd else jnp.where(low, s2, 0.0), -1, keepdims=True)
        feats.append(jnp.exp(lifted - (0.5 * half + LOGF)))
    return s, feats


def cell_range(bounds, blk, cells):
    first = lax.axis_index("fsdp") * (pl.num_programs(0) * BLK) + blk * BLK
    return cell_at(bounds, first, cells), cell_at(bounds, first + BLK - 1, cells), first


def cell_at(bounds, slot, cells):
    cell = jnp.int32(0)
    for c in range(1, cells):
        cell += (bounds[0, c] <= slot).astype(jnp.int32)
    return cell


def cell_mask(bounds, c, first, cols):
    place = lax.broadcasted_iota(jnp.int32, (BLK, cols), 0) + first
    return (place >= bounds[0, c]) & (place < bounds[0, c + 1])


def store_sums(acc, out, cells, summed):
    rows = lax.broadcasted_iota(jnp.int32, (16, FEATS), 0)
    for half in (0, 1):
        for c in range(cells):
            tail = jnp.zeros((16, FEATS), F32)
            for i in range(PAIRS):
                part = acc[c, half * PAIRS + i]
                body, rest = (part[HEAD:], part[:HEAD]) if i % 2 else (part[:HEAD], part[HEAD:])
                out[half, c, i * HEAD : (i + 1) * HEAD, :] = body.astype(BF)
                line = jnp.sum(rest, 0, keepdims=True) if summed else rest[0:1]
                tail = jnp.where(rows == i, line, tail)
            out[half, c, PAIRS * HEAD :, :] = tail.astype(BF)


def load_sums(bounds, sums, full, slots, cells, single):
    rows = lax.broadcasted_iota(jnp.int32, (HEAD, FEATS), 0)
    spot = lax.axis_index("fsdp")
    if len(sums) > 1:
        own, got, far_own, far_other = sums
        core = spot % 2
        start = (spot // 2) * (2 * slots)
        first, last = cell_at(bounds, start, cells), cell_at(bounds, start + 2 * slots - 1, cells)
    for slot in (0, 1):
        if len(sums) > 1:
            half = core ^ slot
            far = far_other if slot else far_own
            before = jnp.zeros(far.shape[1:], F32)
            after = jnp.zeros(far.shape[1:], F32)
            for z in range(far.shape[0]):
                part = far[z].astype(F32)
                before += jnp.where(z < spot // 2, part, 0.0)
                after += jnp.where(z > spot // 2, part, 0.0)
        else:
            half = slot
        for c in range(cells):
            if len(sums) > 1:
                total = own[half, c].astype(F32) + got[half, c].astype(F32)
                total += jnp.where(first == c, before, 0.0) + jnp.where(last == c, after, 0.0)
            else:
                total = sums[0][half, c].astype(F32)
            for i in range(PAIRS):
                body = total[i * HEAD : (i + 1) * HEAD].astype(BF)
                line = jnp.broadcast_to(total[PAIRS * HEAD + i : PAIRS * HEAD + i + 1], (HEAD, FEATS))
                if single:
                    line = jnp.where(rows == 0, line, 0.0)
                line = line.astype(BF)
                h = half * PAIRS + i
                full[c, h, :HEAD, :] = line if i % 2 else body
                full[c, h, HEAD:, :] = body if i % 2 else line


def feature_parts(bank, main, rest):
    w = bank[...]
    hi = w.astype(BF)
    lo = (w - hi.astype(F32)).astype(BF)
    none = jnp.zeros_like(hi)
    main[0] = jnp.concatenate([hi, none, hi, none], 0)
    main[1] = jnp.concatenate([none, hi, none, hi], 0)
    rest[0] = jnp.concatenate([lo, none], 0)
    rest[1] = jnp.concatenate([none, lo], 0)


def back_parts(bank, rhs):
    hi = bank[...].astype(BF)
    ones = jnp.ones_like(hi)
    rhs[0] = jnp.concatenate([hi, ones], 0)
    rhs[1] = jnp.concatenate([ones, hi], 0)


FEATURE_SCRATCH = [pltpu.VMEM((2, 4 * HEAD, FEATS), BF), pltpu.VMEM((2, 2 * HEAD, FEATS), BF)]


def copies(pieces, places, target, sems):
    spot = lax.axis_index("fsdp")
    core = spot % 2
    chip = lax.axis_index("dp") * (target.shape[0] // lax.axis_size("dp")) + spot // 2
    made = []
    for i, (masks, lo, hi) in enumerate(places):
        for side in (0, 1):
            src = pieces[i + side * len(places)]
            for k, mask in enumerate(masks):
                dst = target.at[chip ^ mask, core ^ side, lo:hi]
                made.append(pltpu.make_async_copy(src.at[k], dst, sems.at[len(made)]))
    return made


def both_cores(value):
    mine = lax.axis_index("fsdp") % 2 == 0
    a, b = value[:, 0], value[:, 1]
    return jnp.where(mine, a, b), jnp.where(mine, b, a)


def columns(ref, lo, hi):
    value = ref[..., lo:hi]
    return value.reshape(-1, value.shape[-1])


def key_kernel(cells, places, bounds, x, keep, bank, *refs):
    count = 2 * len(places) if places else 1
    pieces, (a1_o, sk_o, pk_o, vr_o, sums_o, vec_o), refs = refs[:count], refs[count : count + 6], refs[count + 6 :]
    if places:
        w, acc, rm, rr, sems = refs
    else:
        w = pieces[0]
        acc, rm, rr = refs
    blk = pl.program_id(0)
    d = x.shape[1]

    @pl.when(blk == 0)
    def _():
        if places:
            made = copies(pieces, places, w, sems)
            for copy in made:
                copy.start()
        acc[...] = jnp.zeros_like(acc)
        feature_parts(bank, rm, rr)
        if places:
            for copy in made:
                copy.wait()
        vec_o[...] = columns(w, 3 * d, 3 * d + 128).astype(F32).T[:16]

    z, _ = norm_stats(x[...].astype(F32))
    a1 = (z * vec_o[0:1] + vec_o[1:2]).astype(BF)
    a1_o[...] = a1
    keys = dot(a1, columns(w, d, 2 * d))
    vr_o[...] = dot(a1, columns(w, 2 * d, 3 * d)).astype(BF)
    for p in range(PAIRS):
        s, feats = phi_pair(keys[:, 128 * p : 128 * p + 128], rm, rr)
        sk_o[:, 128 * p : 128 * p + 128] = s.astype(BF)
        for odd in (0, 1):
            h = 2 * p + odd
            pk_o[:, FEATS * h : FEATS * (h + 1)] = (keep[...] * feats[odd]).astype(BF)
    lo, hi, first = cell_range(bounds, blk, cells)
    low = lane_low(BLK)

    def one(c, carry):
        mask = cell_mask(bounds, c, first, 128)
        for p in range(PAIRS):
            v = vr_o[:, 128 * p : 128 * p + 128].astype(F32)
            for odd in (0, 1):
                h = 2 * p + odd
                aug = jnp.where(low, 1.0, v) if odd else jnp.where(low, v, 1.0)
                aug = jnp.where(mask, aug, 0.0).astype(BF)
                acc[c, h] += dot_tn(aug, pk_o[:, FEATS * h : FEATS * (h + 1)])
        return carry

    lax.fori_loop(lo, hi + 1, one, 0)

    @pl.when(blk == pl.num_programs(0) - 1)
    def _():
        store_sums(acc, sums_o, cells, False)


def rows_spec(cols):
    return pl.BlockSpec((BLK, cols), lambda i: (i, 0))


def whole_spec(shape):
    return pl.BlockSpec(shape, lambda i: (0,) * len(shape))


def whole_specs(arrays):
    return [whole_spec(v.shape) for v in arrays]


SMEM = pl.BlockSpec(memory_space=pltpu.SMEM)
ANY = pl.BlockSpec(memory_space=pl.ANY)
VM = pl.BlockSpec(memory_space=pltpu.VMEM)


def params():
    return pltpu.CompilerParams(vmem_limit_bytes=VMEM_LIMIT, dimension_semantics=("arbitrary",))


def cost(gflop, mb):
    return pl.CostEstimate(flops=int(gflop * 1e3), bytes_accessed=int(mb * 1e3), transcendentals=0)


def sums_shape(cells):
    return (2, cells, KVROWS, FEATS)


def shape(*dims, kind=BF):
    return jax.ShapeDtypeStruct(dims, kind)


def run_keys(bounds, x, keep, bank, pieces, places, cells):
    n, d = x.shape
    out_specs = [
        rows_spec(d), rows_spec(d), rows_spec(HEADS * FEATS), rows_spec(d), whole_spec(sums_shape(cells)), whole_spec((16, d)),
    ]
    out_shape = [
        shape(n, d), shape(n, d), shape(n, HEADS * FEATS), shape(n, d), shape(*sums_shape(cells)), shape(16, d, kind=F32),
    ]
    scratch = [pltpu.VMEM((cells, HEADS, 128, FEATS), F32)] + FEATURE_SCRATCH
    if places:
        piece = pieces[0].shape
        w = (d // (2 * piece[1]), 2) + piece[1:]
        out_specs.append(whole_spec(w))
        out_shape.append(shape(*w))
        scratch.append(pltpu.SemaphoreType.DMA((d // piece[1],)))
    return pl.pallas_call(
        functools.partial(key_kernel, cells, places),
        grid=(n // BLK,),
        in_specs=[SMEM, rows_spec(d), rows_spec(1), whole_spec(bank.shape)]
        + ([ANY] * len(pieces) if places else whole_specs(pieces)),
        out_specs=out_specs,
        out_shape=out_shape,
        scratch_shapes=scratch,
        compiler_params=params(),
        cost_estimate=cost(8, 10),
        name="keys",
    )(bounds, x, keep, bank, *pieces)


def shuffle(j, rows, wide, d):
    a = lax.broadcasted_iota(jnp.int32, (d, d // wide), 0)
    b = lax.broadcasted_iota(jnp.int32, (d, d // wide), 1)
    hit = (a // (rows * wide) == b // rows) & (a % (rows * wide) == rows * j + b % rows)
    return jnp.where(hit, 1.0, 0.0).astype(BF)


def pad_rows(lines, count):
    return jnp.concatenate(lines + [jnp.zeros((count - len(lines), lines[0].shape[1]), lines[0].dtype)], 0)


def in_order(table, rows, wide):
    d = table.shape[1]
    part = d // wide
    total = jnp.zeros((8, d), F32)
    for j in range(wide):
        lines = pad_rows([table[5 + j : 6 + j, part * k : part * (k + 1)] for k in range(wide)], 8)
        total += dot_nt(lines.astype(BF), shuffle(j, rows, wide, d))
    return total


def by_owner(lines, rows, wide):
    d = lines.shape[1]
    out = []
    for j in range(wide):
        got = dot(lines.astype(BF), shuffle(j, rows, wide, d))
        out.append(jnp.concatenate([got[k : k + 1] for k in range(wide)], 1))
    return out


def query_kernel(rows, wide, a1, wq, bank, vec, sq_o, pq_o, up_o, rm, rr):
    @pl.when(pl.program_id(0) == 0)
    def _():
        feature_parts(bank, rm, rr)
        up_o[...] = in_order(vec[...], rows, wide)

    q = dot(a1[...], wq[...])
    for p in range(PAIRS):
        s, feats = phi_pair(q[:, 128 * p : 128 * p + 128], rm, rr)
        sq_o[:, 128 * p : 128 * p + 128] = s.astype(BF)
        for odd in (0, 1):
            h = 2 * p + odd
            pq_o[:, FEATS * h : FEATS * (h + 1)] = feats[odd].astype(BF)


def run_queries(a1, w, bank, vec, rows, wide):
    n, d = a1.shape
    return pl.pallas_call(
        functools.partial(query_kernel, rows, wide),
        grid=(n // BLK,),
        in_specs=[rows_spec(d), whole_spec((d, d)), whole_spec(bank.shape), whole_spec(vec.shape)],
        out_specs=[rows_spec(d), rows_spec(HEADS * FEATS), whole_spec((8, d))],
        out_shape=[shape(n, d), shape(n, HEADS * FEATS), shape(8, d, kind=F32)],
        scratch_shapes=FEATURE_SCRATCH,
        compiler_params=params(),
        cost_estimate=cost(5, 7),
        name="queries",
    )(a1, w, bank, vec)


def spread_kernel(cells, slots, bounds, own, got, out):
    spot = lax.axis_index("fsdp")
    core = spot % 2
    for z in range(out.shape[0]):
        c = cell_at(bounds, z * (2 * slots) + jnp.where(z > spot // 2, 0, 2 * slots - 1), cells)
        out[z] = (own[core, c].astype(F32) + got[core, c].astype(F32)).astype(BF)


def run_spread(bounds, own, got, chips, slots, cells):
    return pl.pallas_call(
        functools.partial(spread_kernel, cells, slots),
        in_specs=[SMEM, VM, VM],
        out_specs=VM,
        out_shape=shape(chips, KVROWS, FEATS),
        compiler_params=pltpu.CompilerParams(vmem_limit_bytes=VMEM_LIMIT),
        cost_estimate=cost(0.001, 2),
        name="spread",
    )(bounds, own, got)


def middle_kernel(cells, slots, nsums, places, bounds, x, dy_r, keep_r, pq, vec, b_up, *refs):
    sums, refs = refs[:nsums], refs[nsums:]
    count = 2 * len(places) if places else 3
    pieces, refs = refs[:count], refs[count:]
    mixed_o, gr_o, dpre_o, a2_o, ar_o, do_o, dx_o, grads_o, vec_o, vup_o, sums_o, full = refs[:12]
    acc, num_s, den_s = refs[12:15]
    blk = pl.program_id(0)
    width = x.shape[1]
    wide = gr_o.shape[1] // width
    if places:
        w, sems = refs[15:]
        rows = width // (2 * w.shape[0])
        base = rows * (1 + wide)
        w_out = lambda: w[:, :, 0:rows, :].reshape(width, width)
        w_up = lambda j: w[:, :, rows * (1 + j) : rows * (2 + j), :].reshape(width, width)
        w_down = lambda j: w[j * (w.shape[0] // wide) : (j + 1) * (w.shape[0] // wide), :, base:, :].reshape(width, width)
    else:
        w_out = lambda: pieces[0][...]
        w_up = lambda j: pieces[1][:, j * width : (j + 1) * width]
        w_down = lambda j: pieces[2][j * width : (j + 1) * width, :]

    @pl.when(blk == 0)
    def _():
        if places:
            for copy in copies(pieces, places, w, sems):
                copy.start()
        acc[...] = jnp.zeros_like(acc)
        vec_o[...] = jnp.zeros_like(vec_o)
        vup_o[...] = jnp.zeros_like(vup_o)
        load_sums(bounds, sums, full, slots, cells, False)

    lo, hi, first = cell_range(bounds, blk, cells)
    low = lane_low(BLK)

    def attend(c, carry):
        mask = cell_mask(bounds, c, first, 128)
        for p in range(PAIRS):
            h = 2 * p
            lanes = slice(128 * p, 128 * p + 128)
            r0 = dot_nt(pq[:, FEATS * h : FEATS * (h + 1)], full[c, h])
            r1 = dot_nt(pq[:, FEATS * (h + 1) : FEATS * (h + 2)], full[c, h + 1])
            num = jnp.where(low, r0, r1)
            den = pltpu.roll(jnp.where(low, r1, r0), HEAD, 1)
            num_s[:, lanes] = jnp.where(mask, num, num_s[:, lanes])
            den_s[:, lanes] = jnp.where(mask, den, den_s[:, lanes])
        return carry

    lax.fori_loop(lo, hi + 1, attend, 0)
    if places:
        @pl.when(blk == 0)
        def _():
            for copy in copies(pieces, places, w, sems):
                copy.wait()

    keep = keep_r[...]
    inv = 1.0 / den_s[...]
    ar = (keep * num_s[...] * inv).astype(BF)
    ar_o[...] = ar
    x2 = x[...].astype(F32) + dot(ar, w_out())
    z2, r2 = norm_stats(x2)
    g2 = vec[2:3]
    a2 = (z2 * g2 + vec[3:4]).astype(BF)
    a2_o[...] = a2
    dy = dy_r[...]
    mixed = x2 + vec[4:5]
    da2 = jnp.zeros_like(x2)
    k0 = math.sqrt(2.0 / math.pi)
    k1 = 0.044715 * k0
    for j in range(wide):
        cols = slice(j * width, (j + 1) * width)
        pre = dot(a2, w_up(j)) + b_up[j : j + 1]
        sq = pre * pre
        t = jnp.tanh(pre * (k0 + k1 * sq))
        half = 0.5 + 0.5 * t
        act = pre * half
        slope = half + act * (1.0 - t) * (k0 + (3.0 * k1) * sq)
        gr = act.astype(BF)
        gr_o[:, cols] = gr
        mixed += dot(gr, w_down(j))
        dpre = (dot_nt(dy, w_down(j)) * slope).astype(BF)
        dpre_o[:, cols] = dpre
        da2 += dot_nt(dpre, w_up(j))
        vup_o[j : j + 1] += jnp.sum(dpre.astype(F32), 0, keepdims=True)
    mixed_o[...] = mixed.astype(BF)
    dyf = dy.astype(F32)
    dz = da2 * g2
    m1 = jnp.sum(dz, -1, keepdims=True) * (1.0 / width)
    m2 = jnp.sum(dz * z2, -1, keepdims=True) * (1.0 / width)
    dx2 = dyf + r2 * (dz - m1 - z2 * m2)
    dx_o[...] = dx2
    vec_o[2:3, :] += jnp.sum(da2 * z2, 0, keepdims=True)
    vec_o[3:4, :] += jnp.sum(da2, 0, keepdims=True)
    vec_o[4:5, :] += jnp.sum(dyf, 0, keepdims=True)
    do = dx2.astype(BF)
    do_o[...] = do
    dattn = keep * dot_nt(do, w_out()).astype(BF).astype(F32)
    dnum = dattn * inv
    dden = -dnum * num_s[...] * inv
    for p in range(PAIRS):
        lanes = slice(128 * p, 128 * p + 128)
        mine = dnum[:, lanes]
        swap = pltpu.roll(dden[:, lanes], HEAD, 1)
        h = 2 * p
        grads_o[:, 128 * h : 128 * h + 128] = jnp.where(low, mine, swap).astype(BF)
        grads_o[:, 128 * h + 128 : 128 * h + 256] = jnp.where(low, swap, mine).astype(BF)

    def gather(c, carry):
        mask = cell_mask(bounds, c, first, 128)
        for h in range(HEADS):
            part = grads_o[:, 128 * h : 128 * h + 128]
            part = jnp.where(mask, part.astype(F32), 0.0).astype(BF)
            acc[c, h] += dot_tn(part, pq[:, FEATS * h : FEATS * (h + 1)])
        return carry

    lax.fori_loop(lo, hi + 1, gather, 0)

    @pl.when(blk == pl.num_programs(0) - 1)
    def _():
        store_sums(acc, sums_o, cells, True)


def run_middle(bounds, x, dy, keep, pq, vec, b_up, sums, pieces, places, ff, cells):
    n, d = x.shape
    wide = HEADS * 128
    full = (cells, HEADS, 128, FEATS)
    scratch = [pltpu.VMEM(full, F32), pltpu.VMEM((BLK, d), F32), pltpu.VMEM((BLK, d), F32)]
    if places:
        rows = max(hi for _, _, hi in places)
        chips = 1 + max(m for masks, _, _ in places for m in masks)
        number = 2 * sum(len(masks) for masks, _, _ in places)
        scratch += [pltpu.VMEM((chips, 2, rows, d), BF), pltpu.SemaphoreType.DMA((number,))]
    return pl.pallas_call(
        functools.partial(middle_kernel, cells, n, len(sums), places),
        grid=(n // BLK,),
        in_specs=[
            SMEM, rows_spec(d), rows_spec(d), rows_spec(1), rows_spec(HEADS * FEATS), whole_spec(vec.shape), whole_spec(b_up.shape),
        ]
        + whole_specs(sums)
        + ([ANY] * len(pieces) if places else whole_specs(pieces)),
        out_specs=[
            rows_spec(d), rows_spec(ff), rows_spec(ff), rows_spec(d), rows_spec(d), rows_spec(d),
            rows_spec(d), rows_spec(wide), whole_spec((16, d)), whole_spec((8, d)),
            whole_spec(sums_shape(cells)), whole_spec(full),
        ],
        out_shape=[
            shape(n, d), shape(n, ff), shape(n, ff), shape(n, d), shape(n, d), shape(n, d),
            shape(n, d, kind=F32), shape(n, wide), shape(16, d, kind=F32), shape(8, d, kind=F32),
            shape(*sums_shape(cells)), shape(*full),
        ],
        scratch_shapes=scratch,
        compiler_params=params(),
        cost_estimate=cost(14, 30),
        name="middle",
    )(bounds, x, dy, keep, pq, vec, b_up, *sums, *pieces)


def phi_back(s, feats, rhs, low):
    r0 = dot_nt(feats[0].astype(BF), rhs[0])
    r1 = dot_nt(feats[1].astype(BF), rhs[1])
    total = pltpu.roll(jnp.where(low, r1, r0), HEAD, 1)
    return (jnp.where(low, r0, r1) - s * total) * SCALE


def query_back_kernel(cells, bounds, grads, pq, sq, full, bank, a1, dq_o, gq_o, g_s, acc, rhs):
    blk = pl.program_id(0)

    @pl.when(blk == 0)
    def _():
        back_parts(bank, rhs)
        acc[...] = jnp.zeros_like(acc)

    lo, hi, first = cell_range(bounds, blk, cells)
    low = lane_low(BLK)

    def one(c, carry):
        mask = cell_mask(bounds, c, first, FEATS)
        for h in range(HEADS):
            cols = slice(FEATS * h, FEATS * (h + 1))
            g = dot(grads[:, 128 * h : 128 * h + 128], full[c, h])
            g_s[:, cols] = jnp.where(mask, g, g_s[:, cols])
        return carry

    lax.fori_loop(lo, hi + 1, one, 0)
    for p in range(PAIRS):
        lanes = slice(128 * p, 128 * p + 128)
        feats = []
        for odd in (0, 1):
            cols = slice(FEATS * (2 * p + odd), FEATS * (2 * p + odd + 1))
            feats.append(g_s[:, cols] * pq[:, cols].astype(F32))
        dq_o[:, lanes] = phi_back(sq[:, lanes].astype(F32), feats, rhs, low).astype(BF)
    acc[...] += dot_tn(a1[...], dq_o[...])

    @pl.when(blk == pl.num_programs(0) - 1)
    def _():
        gq_o[...] = acc[...].astype(BF)


def run_query_back(bounds, grads, pq, sq, full, bank, a1, cells):
    n, d = sq.shape
    return pl.pallas_call(
        functools.partial(query_back_kernel, cells),
        grid=(n // BLK,),
        in_specs=[
            SMEM, rows_spec(HEADS * 128), rows_spec(HEADS * FEATS), rows_spec(d),
            whole_spec(full.shape), whole_spec(bank.shape), rows_spec(d),
        ],
        out_specs=[rows_spec(d), whole_spec((d, d))],
        out_shape=[shape(n, d), shape(d, d)],
        scratch_shapes=[
            pltpu.VMEM((BLK, HEADS * FEATS), F32), pltpu.VMEM((d, d), F32), pltpu.VMEM((2, 128, FEATS), BF),
        ],
        compiler_params=params(),
        cost_estimate=cost(3, 8),
        name="query_back",
    )(bounds, grads, pq, sq, full, bank, a1)


def weight_kernel(rows, a2, dpre, gr, dy, ar, do, keep_o, send_o):
    j = pl.program_id(0)
    d = a2.shape[1]

    def put(value, block, lo, size):
        count = d // (2 * size)
        kept, sent = both_cores(value.reshape(count, 2, size, d))
        at = (pl.ds(block * count, count), pl.ds(lo, size))
        keep_o[at] = kept.astype(BF)
        send_o[at] = sent.astype(BF)

    @pl.when(j == 0)
    def _():
        put(dot_tn(ar[...], do[...]), 0, 0, rows)

    put(dot_tn(a2[...], dpre[...]), 0, pl.multiple_of(rows * (1 + j), rows), rows)
    wide = (keep_o.shape[1] // rows - 1) // 2
    put(dot_tn(gr[...], dy[...]), j, rows * (1 + wide), rows * wide)


def run_weights(a2, dpre, gr, dy, ar, do, rows):
    n, d = a2.shape
    wide = dpre.shape[1] // d
    out = (d // (2 * rows), rows * (1 + 2 * wide), d)
    cols = pl.BlockSpec((n, d), lambda j: (0, j))
    whole = whole_spec((n, d))
    return pl.pallas_call(
        functools.partial(weight_kernel, rows),
        grid=(wide,),
        in_specs=[whole, cols, cols, whole, whole, whole],
        out_specs=[whole_spec(out), whole_spec(out)],
        out_shape=[shape(*out), shape(*out)],
        compiler_params=params(),
        cost_estimate=cost(5, 20),
        name="weights",
    )(a2, dpre, gr, dy, ar, do)


def key_back_kernel(cells, slots, nsums, paired, rows, wide, bounds, x, a1, pk, vr, sk, dq, dx, vec, gvec, vup, bank, w, gq, *refs):
    sums, refs = refs[:nsums], refs[nsums:]
    outs, refs = refs[: 3 if paired else 2], refs[3 if paired else 2 :]
    gt_o = outs[0]
    full, g_s, v_s, rhs, dk_s, dv_s, vec_s, gk_s, gv_s = refs
    blk = pl.program_id(0)
    d = x.shape[1]

    @pl.when(blk == 0)
    def _():
        vec_s[...] = gvec[...]
        gk_s[...] = jnp.zeros_like(gk_s)
        gv_s[...] = jnp.zeros_like(gv_s)
        back_parts(bank, rhs)
        load_sums(bounds, sums, full, slots, cells, True)

    lo, hi, first = cell_range(bounds, blk, cells)
    low = lane_low(BLK)

    def one(c, carry):
        mask = cell_mask(bounds, c, first, FEATS)
        narrow = cell_mask(bounds, c, first, 128)
        for p in range(PAIRS):
            lanes = slice(128 * p, 128 * p + 128)
            v = vr[:, lanes].astype(F32)
            outs = []
            for odd in (0, 1):
                h = 2 * p + odd
                cols = slice(FEATS * h, FEATS * (h + 1))
                aug = (jnp.where(low, 1.0, v) if odd else jnp.where(low, v, 1.0)).astype(BF)
                g = dot(aug, full[c, h])
                g_s[:, cols] = jnp.where(mask, g, g_s[:, cols])
                outs.append(dot_nt(pk[:, cols], full[c, h]))
            v_s[:, lanes] = jnp.where(narrow, jnp.where(low, outs[0], outs[1]), v_s[:, lanes])
        return carry

    lax.fori_loop(lo, hi + 1, one, 0)
    for p in range(PAIRS):
        lanes = slice(128 * p, 128 * p + 128)
        feats = []
        for odd in (0, 1):
            cols = slice(FEATS * (2 * p + odd), FEATS * (2 * p + odd + 1))
            feats.append(g_s[:, cols] * pk[:, cols].astype(F32))
        dk_s[:, lanes] = phi_back(sk[:, lanes].astype(F32), feats, rhs, low).astype(BF)
    dv_s[...] = v_s[...].astype(BF)
    dk, dv = dk_s[...], dv_s[...]
    gk_s[...] += dot_tn(a1[...], dk)
    gv_s[...] += dot_tn(a1[...], dv)
    da1 = dot_nt(dq[...], w[:, :d]) + dot_nt(dk, w[:, d : 2 * d]) + dot_nt(dv, w[:, 2 * d : 3 * d])
    z, r = norm_stats(x[...].astype(F32))
    dz = da1 * vec[0:1]
    m1 = jnp.sum(dz, -1, keepdims=True) * (1.0 / d)
    m2 = jnp.sum(dz * z, -1, keepdims=True) * (1.0 / d)
    gt_o[...] = dx[...] + r * (dz - m1 - z * m2)
    vec_s[0:1, :] += jnp.sum(da1 * z, 0, keepdims=True)
    vec_s[1:2, :] += jnp.sum(da1, 0, keepdims=True)

    @pl.when(blk == pl.num_programs(0) - 1)
    def _():
        vt = pad_rows([vec_s[i : i + 1] for i in range(5)] + by_owner(vup[...], rows, wide), 128).T
        for lo, value in ((0, gq[...].astype(F32)), (d, gk_s[...]), (2 * d, gv_s[...]), (3 * d, vt)):
            cols = slice(lo, lo + value.shape[1])
            if paired:
                kept, sent = both_cores(value.reshape(outs[1].shape[0], 2, rows, value.shape[1]))
                outs[1][:, :, cols] = kept.astype(BF)
                outs[2][:, :, cols] = sent.astype(BF)
            else:
                outs[1][:, cols] = value.astype(BF)


def run_key_back(bounds, x, a1, pk, vr, sk, dq, dx, vec, gvec, vup, bank, w, gq, sums, rows, wide, paired, cells):
    n, d = x.shape
    total = w.shape[1]
    gout = [(d // (2 * rows), rows, total)] * 2 if paired else [(d, total)]
    square = pltpu.VMEM((d, d), F32)
    return pl.pallas_call(
        functools.partial(key_back_kernel, cells, n, len(sums), paired, rows, wide),
        grid=(n // BLK,),
        in_specs=[
            SMEM, rows_spec(d), rows_spec(d), rows_spec(HEADS * FEATS), rows_spec(d), rows_spec(d), rows_spec(d), rows_spec(d),
        ]
        + whole_specs((vec, gvec, vup, bank, w, gq))
        + whole_specs(sums),
        out_specs=[rows_spec(d)] + [whole_spec(g) for g in gout],
        out_shape=[shape(n, d, kind=F32)] + [shape(*g) for g in gout],
        scratch_shapes=[
            pltpu.VMEM((cells, HEADS, 128, FEATS), BF),
            pltpu.VMEM((BLK, HEADS * FEATS), F32),
            pltpu.VMEM((BLK, d), F32),
            pltpu.VMEM((2, 128, FEATS), BF),
            pltpu.VMEM((BLK, d), BF),
            pltpu.VMEM((BLK, d), BF),
            pltpu.VMEM((16, d), F32),
            square,
            square,
        ],
        compiler_params=params(),
        cost_estimate=cost(6, 14),
        name="key_back",
    )(bounds, x, a1, pk, vr, sk, dq, dx, vec, gvec, vup, bank, w, gq, *sums)


AXES = ("dp", "fsdp")
Z_ALL = (0, 1, 2, 3)
LEAD_MASKS = (Z_ALL, (4, 5, 6, 7), (8, 9, 10, 11), (12, 13, 14, 15))


def flip(x, axis, size, mask):
    return lax.ppermute(x, axis, [(i, i ^ mask) for i in range(size)])


def to_core(x, fsdp):
    return flip(x, "fsdp", fsdp, 1)


def to_z(x, fsdp, mask):
    return flip(x, "fsdp", fsdp, 2 * mask)


def tie(*values):
    return lax.optimization_barrier(values)


def same_core_groups(dp, fsdp):
    return [[d * fsdp + 2 * z + c for d in range(dp) for z in range(fsdp // 2)] for c in range(2)]


def chip_groups(fsdp):
    return [[2 * z + c for z in range(fsdp // 2)] for c in range(2)]


def pack_kernel(wide, w_qkv, g1, s1, w_out, g2, s2, w_up, b_up, w_down, b_down, lead, body):
    rows = w_qkv.shape[0]
    d = w_out.shape[1]
    total = w_qkv.shape[1]
    place = lax.broadcasted_iota(jnp.int32, (128, rows), 0)
    up = b_up[...].astype(F32).reshape(1, -1)
    lines = [v[...].astype(F32).reshape(1, -1) for v in (g1, s1, g2, s2, b_down)]
    lines += [up[:, j * rows : (j + 1) * rows] for j in range(wide)]
    table = jnp.zeros((128, rows), F32)
    for i, line in enumerate(lines):
        table = jnp.where(place == i, line, table)
    across = lax.broadcasted_iota(jnp.int32, (rows, rows), 0) == lax.broadcasted_iota(jnp.int32, (rows, rows), 1)
    lead[:, :total] = w_qkv[...]
    lead[:, total:] = dot_nt(jnp.where(across, 1.0, 0.0).astype(BF), table.astype(BF)).astype(BF)
    body[:rows] = w_out[...]
    for j in range(wide):
        body[rows * (1 + j) : rows * (2 + j)] = w_up[:, j * d : (j + 1) * d]
    body[rows * (1 + wide) :] = w_down[...]


def lead_sum_kernel(wide, part, wqkv, *lines):
    total = part[0].astype(F32)
    for k in range(1, part.shape[0]):
        total += part[k].astype(F32)
    cols = wqkv.shape[1]
    wqkv[...] = total[:, :cols]
    table = total[:, cols:].T
    for i in range(5):
        lines[i][...] = table[i]
    lines[5][...] = jnp.concatenate([table[5 + j : 6 + j] for j in range(wide)], 1)[0]


def run_lead_sum(part, cols, wide):
    rows = part.shape[1]
    return pl.pallas_call(
        functools.partial(lead_sum_kernel, wide),
        in_specs=[VM],
        out_specs=[VM] * 7,
        out_shape=[shape(rows, cols, kind=F32)] + [shape(rows, kind=F32)] * 5 + [shape(rows * wide, kind=F32)],
        name="lead_sum",
    )(part)


def body_sum_kernel(rows, wide, *refs):
    parts, (wout, wup, wdown) = refs[:-3], refs[-3:]
    d = wout.shape[1]
    total = parts[0][...].astype(F32)
    for part in parts[1:]:
        total += part[...].astype(F32)
    wout[...] = total[:rows]
    for j in range(wide):
        wup[:, j * d : (j + 1) * d] = total[rows * (1 + j) : rows * (2 + j)]
    wdown[...] = total[rows * (1 + wide) :]


def run_body_sum(parts, rows, wide):
    d = parts[0].shape[1]
    return pl.pallas_call(
        functools.partial(body_sum_kernel, rows, wide),
        in_specs=[VM] * len(parts),
        out_specs=[VM] * 3,
        out_shape=[shape(rows, d, kind=F32), shape(rows, wide * d, kind=F32), shape(rows * wide, d, kind=F32)],
        name="body_sum",
    )(*parts)


def local(dp, fsdp, tokens, bounds, padding, bank, ln1_gain, ln1_bias, w_qkv, w_out, ln2_gain, ln2_bias,
          w_up, b_up, w_down, b_down, cotangent):
    ndev = dp * fsdp
    x = tokens[0]
    dy = cotangent[0]
    n, d = x.shape
    ff = w_up.shape[1]
    cells = bounds.shape[1] - 1
    chips = fsdp // 2
    rows = d // ndev
    wide = ff // d
    frow = ff // ndev
    paired = dp == 4 and fsdp == 8

    shards = (w_qkv, ln1_gain, ln1_bias, w_out, ln2_gain, ln2_bias, w_up, b_up, w_down, b_down)
    if paired:
        lead, body = pl.pallas_call(
            functools.partial(pack_kernel, wide),
            in_specs=[VM] * len(shards),
            out_specs=[VM, VM],
            out_shape=[shape(rows, 3 * d + 128), shape(rows * (1 + wide) + frow, d)],
            name="pack",
        )(*shards)
    else:
        vecs = jnp.concatenate([ln1_gain, ln1_bias, ln2_gain, ln2_bias, b_down, b_up]).reshape(5 + wide, rows)
        lead = jnp.concatenate([w_qkv, jnp.pad(vecs, ((0, 128 - 5 - wide), (0, 0))).T], 1)
        body = jnp.concatenate([w_out] + [w_up[:, j * d : (j + 1) * d] for j in range(wide)] + [w_down], 0)
    keep = padding[0].astype(F32)[:, None]
    cut = rows * (1 + wide)

    if paired:
        lead, body, keep = tie(lead, body, keep)
        first = jnp.stack([lead] + [to_z(lead, fsdp, k) for k in (1, 2, 3)])
        lead_own = [first] + [flip(first, "dp", dp, k) for k in (1, 2, 3)]
        pair = jnp.stack([body, to_z(body, fsdp, 1)])
        pair, *lead_own = tie(pair, *lead_own)
        lead_pieces = lead_own + [to_core(v, fsdp) for v in lead_own]
        four = jnp.concatenate([pair, to_z(pair, fsdp, 2)])
        lead_places = tuple((m, 0, rows) for m in LEAD_MASKS)
    else:
        lead_pieces = [lax.all_gather(lead, AXES, axis=0, tiled=True)]
        parts = lax.all_gather(body, AXES, axis=0)
        take = lambda lo, size: parts[:, lo : lo + size].reshape(ndev * size, d)
        body_pieces = [
            take(0, rows), jnp.concatenate([take((1 + j) * rows, rows) for j in range(wide)], 1), take(cut, frow),
        ]
        lead_places = body_places = None

    def far_sums(out):
        return lax.all_to_all(out, "fsdp", 0, 0, axis_index_groups=chip_groups(fsdp), tiled=True)

    a1, sk, pk, vr, sums, vec, *w = run_keys(bounds, x, keep, bank, lead_pieces, lead_places, cells)
    w = w[0].reshape(d, -1) if paired else lead_pieces[0]
    if paired:
        sums, four = tie(sums, four)
        sums = [sums, to_core(sums, fsdp)]
        out = run_spread(bounds, *sums, chips, n, cells)
        a1_q, four, out = tie(a1, four, out)
        far = far_sums(out)
        up, down = four[:, :cut], four[:, cut:]
        up_x, down_y = flip(up, "dp", dp, 1), flip(down, "dp", dp, 2)
        up_y = flip(jnp.concatenate([up, up_x]), "dp", dp, 2)
        down_x = flip(jnp.concatenate([down, down_y]), "dp", dp, 1)
        sq, pq, up_line = run_queries(a1_q, w, bank, vec, rows, wide)
        up_y, down_x, pq, up_line = tie(up_y, down_x, pq, up_line)
        body_own = [four, up_x, down_y, up_y, down_x]
        body_pieces = body_own + [to_core(v, fsdp) for v in body_own]
        body_places = (
            (Z_ALL, 0, cut + frow), ((4, 5, 6, 7), 0, cut), ((8, 9, 10, 11), cut, cut + frow),
            ((8, 9, 10, 11, 12, 13, 14, 15), 0, cut), ((4, 5, 6, 7, 12, 13, 14, 15), cut, cut + frow),
        )
        sums = sums + [far, to_core(far, fsdp)]
    else:
        sums = [lax.psum(sums, "fsdp")]
        sq, pq, up_line = run_queries(a1, w, bank, vec, rows, wide)
    mixed, gr, dpre, a2, ar, do, dx2, grads, gvec, vup, sums, full = run_middle(
        bounds, x, dy, keep, pq, vec, up_line, sums, body_pieces, body_places, ff, cells
    )
    back = lambda dq, gq, sums: run_key_back(
        bounds, x, a1, pk, vr, sk, dq, dx2, vec, gvec, vup, bank, w, gq, sums, rows, wide, paired, cells
    )
    if paired:
        kept, sent = run_weights(a2, dpre, gr, dy, ar, do, rows)
        got, kept, sent = tie(to_core(sums, fsdp), kept, sent)
        sums = [sums, got]
        out = run_spread(bounds, *sums, chips, n, cells)
        grads, out = tie(grads, out)
        far = far_sums(out)
        dq, gq = run_query_back(bounds, grads, pq, sq, full, bank, a1, cells)
        plus = lambda *parts: functools.reduce(lambda a, b: a + b, [v.astype(F32) for v in parts]).astype(BF)
        half = plus(kept, to_core(sent, fsdp)).reshape((2, 2, chips) + kept.shape[1:])
        ypos, xpos = lax.axis_index("dp") // 2, lax.axis_index("dp") % 2
        pick = lambda value, at, dim: lax.dynamic_index_in_dim(value, at, dim, keepdims=False)
        up, down = half[:, :, :, :cut], half[:, :, :, cut:]
        far, dq, gq, up, down = tie(far, dq, gq, up, down)
        up_got = flip(pick(up, 1 - xpos, 1), "dp", dp, 1)
        down_got = flip(pick(down, 1 - ypos, 0), "dp", dp, 2)
        gt, kept, sent = back(dq, gq, sums + [far, to_core(far, fsdp)])
        kept, sent, up_got, down_got = tie(kept, sent, up_got, down_got)
        up = plus(pick(up, xpos, 1), up_got)
        down = plus(pick(down, ypos, 0), down_got)
        up = plus(pick(up, ypos, 0), flip(pick(up, 1 - ypos, 0), "dp", dp, 2))
        down = plus(pick(down, xpos, 0), flip(pick(down, 1 - xpos, 0), "dp", dp, 1))
        whole = jnp.concatenate([up, down], 1)
        zpos = lax.axis_index("fsdp") // 2
        parts = [pick(whole, zpos, 0)] + [to_z(pick(whole, zpos ^ k, 0), fsdp, k) for k in (1, 2, 3)]
        half = plus(kept, to_core(sent, fsdp))
        part = lax.all_to_all(half, AXES, 0, 0, axis_index_groups=same_core_groups(dp, fsdp), tiled=True)
        wqkv, *vecs = run_lead_sum(part, 3 * d, wide)
        wout, wup, wdown = run_body_sum(parts, rows, wide)
    else:
        dq, gq = run_query_back(bounds, grads, pq, sq, full, bank, a1, cells)
        gt, glead = back(dq, gq, [lax.psum(sums, "fsdp")])
        gup = dot_tn(a2, dpre)
        blocks = lambda g, size: g.reshape(ndev, size, d)
        gbody = jnp.concatenate(
            [blocks(dot_tn(ar, do), rows)]
            + [blocks(gup[:, j * d : (j + 1) * d], rows) for j in range(wide)]
            + [blocks(dot_tn(gr, dy), frow)], 1
        )
        gbody = lax.psum_scatter(gbody, AXES, scatter_dimension=0, tiled=True)[0]
        glead = lax.psum_scatter(glead.astype(F32), AXES, scatter_dimension=0, tiled=True)
        gvec = glead[:, 3 * d :].T
        vecs = [gvec[i] for i in range(5)] + [gvec[5 : 5 + wide].reshape(-1)]
        wqkv, wout, wdown = glead[:, : 3 * d], gbody[:rows], gbody[cut:]
        wup = jnp.concatenate([gbody[(1 + j) * rows : (2 + j) * rows] for j in range(wide)], 1)
    return (
        mixed[None], gt[None], vecs[0], vecs[1], wqkv, wout, vecs[2], vecs[3], wup, vecs[5], wdown, vecs[4],
    )


def solution(mesh):
    both = P(("dp", "fsdp"))
    mat = P(("dp", "fsdp"), None)
    act = P("dp", "fsdp", None)
    return jax.shard_map(
        functools.partial(local, mesh.shape["dp"], mesh.shape["fsdp"]),
        mesh=mesh,
        in_specs=(act, P("dp", None), P("dp", "fsdp"), P(), both, both, mat, mat, both, both, mat, both, mat, both, act),
        out_specs=(act, act, both, both, mat, mat, both, both, mat, both, mat, both),
        check_vma=False,
    )
```

```python
import functools
import math

import jax
import jax.numpy as jnp
from jax import lax
from jax.experimental import pallas as pl
from jax.experimental.pallas import tpu as pltpu
from jax.sharding import PartitionSpec as P

HEADS = 8
FEATS = 256
HEAD = 64
PAIRS = HEADS // 2
SCALE = HEAD ** (-0.25)
LOGF = 0.5 * math.log(FEATS)
BLK = 256
WIDE_BLK = 512
SUB = 256
KVROWS = 272
BF = jnp.bfloat16
F32 = jnp.float32
VMEM_LIMIT = 56 * 1024 * 1024


def dot(a, b):
    return jnp.dot(a, b, preferred_element_type=F32)


def dot_nt(a, b):
    return lax.dot_general(a, b, (((1,), (1,)), ((), ())), preferred_element_type=F32)


def dot_tn(a, b):
    return lax.dot_general(a, b, (((0,), (0,)), ((), ())), preferred_element_type=F32)


def norm_stats(x):
    width = x.shape[-1]
    c = x - jnp.sum(x, -1, keepdims=True) * (1.0 / width)
    r = lax.rsqrt(jnp.sum(c * c, -1, keepdims=True) * (1.0 / width) + 1e-05)
    return c * r, r


def lane_low(n):
    return lax.broadcasted_iota(jnp.int32, (n, 128), 1) < HEAD


def phi_pair(u, rhs_main, rhs_rest):
    low = lane_low(u.shape[0])
    s = u * SCALE
    hi = s.astype(BF)
    lo = (s - hi.astype(F32)).astype(BF)
    both = jnp.concatenate([hi, lo], 1)
    s2 = s * s
    feats = []
    for odd in (0, 1):
        lifted = dot(both, rhs_main[odd]) + dot(hi, rhs_rest[odd])
        half = jnp.sum(jnp.where(low, 0.0, s2) if odd else jnp.where(low, s2, 0.0), -1, keepdims=True)
        feats.append(jnp.exp(lifted - (0.5 * half + LOGF)))
    return s, feats


def over_cells(bounds, blk, cells, block, body):
    for sub in range(block // SUB):
        first = lax.axis_index("fsdp") * (pl.num_programs(0) * block) + blk * block + sub * SUB
        rows = slice(sub * SUB, (sub + 1) * SUB)

        def one(c, carry):
            body(c, rows, first)
            return carry

        lax.fori_loop(cell_at(bounds, first, cells), cell_at(bounds, first + SUB - 1, cells) + 1, one, 0)


def cell_at(bounds, slot, cells):
    cell = jnp.int32(0)
    for c in range(1, cells):
        cell += (bounds[0, c] <= slot).astype(jnp.int32)
    return cell


def cell_mask(bounds, c, first, cols):
    place = lax.broadcasted_iota(jnp.int32, (SUB, cols), 0) + first
    return (place >= bounds[0, c]) & (place < bounds[0, c + 1])


def store_sums(acc, out, cells, summed):
    rows = lax.broadcasted_iota(jnp.int32, (16, FEATS), 0)
    for half in (0, 1):
        for c in range(cells):
            tail = jnp.zeros((16, FEATS), F32)
            for i in range(PAIRS):
                part = acc[c, half * PAIRS + i]
                body, rest = (part[HEAD:], part[:HEAD]) if i % 2 else (part[:HEAD], part[HEAD:])
                out[half, c, i * HEAD : (i + 1) * HEAD, :] = body.astype(BF)
                line = jnp.sum(rest, 0, keepdims=True) if summed else rest[0:1]
                tail = jnp.where(rows == i, line, tail)
            out[half, c, PAIRS * HEAD :, :] = tail.astype(BF)


def load_sums(bounds, sums, full, slots, cells, single):
    rows = lax.broadcasted_iota(jnp.int32, (HEAD, FEATS), 0)
    spot = lax.axis_index("fsdp")
    if len(sums) > 1:
        own, got, far_own, far_other = sums
        core = spot % 2
        start = (spot // 2) * (2 * slots)
        first, last = cell_at(bounds, start, cells), cell_at(bounds, start + 2 * slots - 1, cells)
    for slot in (0, 1):
        if len(sums) > 1:
            half = core ^ slot
            far = far_other if slot else far_own
            before = jnp.zeros(far.shape[1:], F32)
            after = jnp.zeros(far.shape[1:], F32)
            for z in range(far.shape[0]):
                part = far[z].astype(F32)
                before += jnp.where(z < spot // 2, part, 0.0)
                after += jnp.where(z > spot // 2, part, 0.0)
        else:
            half = slot
        for c in range(cells):
            if len(sums) > 1:
                total = own[half, c].astype(F32) + got[half, c].astype(F32)
                total += jnp.where(first == c, before, 0.0) + jnp.where(last == c, after, 0.0)
            else:
                total = sums[0][half, c].astype(F32)
            for i in range(PAIRS):
                body = total[i * HEAD : (i + 1) * HEAD].astype(BF)
                line = jnp.broadcast_to(total[PAIRS * HEAD + i : PAIRS * HEAD + i + 1], (HEAD, FEATS))
                if single:
                    line = jnp.where(rows == 0, line, 0.0)
                line = line.astype(BF)
                h = half * PAIRS + i
                full[c, h, :HEAD, :] = line if i % 2 else body
                full[c, h, HEAD:, :] = body if i % 2 else line


def keep_lanes(pad):
    return jnp.broadcast_to(pad[...].astype(F32), (128, pad.shape[1])).T


def feature_parts(bank, main, rest):
    w = bank[...]
    hi = w.astype(BF)
    lo = (w - hi.astype(F32)).astype(BF)
    none = jnp.zeros_like(hi)
    main[0] = jnp.concatenate([hi, none, hi, none], 0)
    main[1] = jnp.concatenate([none, hi, none, hi], 0)
    rest[0] = jnp.concatenate([lo, none], 0)
    rest[1] = jnp.concatenate([none, lo], 0)


def back_parts(bank, rhs):
    hi = bank[...].astype(BF)
    ones = jnp.ones_like(hi)
    rhs[0] = jnp.concatenate([hi, ones], 0)
    rhs[1] = jnp.concatenate([ones, hi], 0)


FEATURE_SCRATCH = [pltpu.VMEM((2, 4 * HEAD, FEATS), BF), pltpu.VMEM((2, 2 * HEAD, FEATS), BF)]


def copies(pieces, places, target, sems):
    spot = lax.axis_index("fsdp")
    core = spot % 2
    chip = lax.axis_index("dp") * (target.shape[0] // lax.axis_size("dp")) + spot // 2
    made = []
    for i, (masks, lo, hi) in enumerate(places):
        for side in (0, 1):
            src = pieces[i + side * len(places)]
            for k, mask in enumerate(masks):
                dst = target.at[chip ^ mask, core ^ side, lo:hi]
                made.append(pltpu.make_async_copy(src.at[k], dst, sems.at[len(made)]))
    return made


def both_cores(value):
    mine = lax.axis_index("fsdp") % 2 == 0
    a, b = value[:, 0], value[:, 1]
    return jnp.where(mine, a, b), jnp.where(mine, b, a)


def columns(ref, lo, hi):
    value = ref[..., lo:hi]
    return value.reshape(-1, value.shape[-1])


def key_kernel(cells, places, bounds, x, pad, bank, *refs):
    count = 2 * len(places) if places else 1
    pieces, (a1_o, sk_o, pk_o, vr_o, sums_o, vec_o), refs = refs[:count], refs[count : count + 6], refs[count + 6 :]
    if places:
        w, acc, rm, rr, sems = refs
    else:
        w = pieces[0]
        acc, rm, rr = refs
    blk = pl.program_id(0)
    d = x.shape[1]

    @pl.when(blk == 0)
    def _():
        if places:
            made = copies(pieces, places, w, sems)
            for copy in made:
                copy.start()
        acc[...] = jnp.zeros_like(acc)
        feature_parts(bank, rm, rr)
        if places:
            for copy in made:
                copy.wait()
        vec_o[...] = columns(w, 3 * d, 3 * d + 128).astype(F32).T[:16]

    keep = keep_lanes(pad)
    keep = jnp.concatenate([keep, keep], 1)
    z, _ = norm_stats(x[...].astype(F32))
    a1 = (z * vec_o[0:1] + vec_o[1:2]).astype(BF)
    a1_o[...] = a1
    keys = dot(a1, columns(w, d, 2 * d))
    vr_o[...] = dot(a1, columns(w, 2 * d, 3 * d)).astype(BF)
    for p in range(PAIRS):
        s, feats = phi_pair(keys[:, 128 * p : 128 * p + 128], rm, rr)
        sk_o[:, 128 * p : 128 * p + 128] = s.astype(BF)
        for odd in (0, 1):
            h = 2 * p + odd
            pk_o[:, FEATS * h : FEATS * (h + 1)] = (keep * feats[odd]).astype(BF)
    low = lane_low(SUB)

    def one(c, rows, first):
        mask = cell_mask(bounds, c, first, 128)
        for p in range(PAIRS):
            v = vr_o[rows, 128 * p : 128 * p + 128].astype(F32)
            for odd in (0, 1):
                h = 2 * p + odd
                aug = jnp.where(low, 1.0, v) if odd else jnp.where(low, v, 1.0)
                aug = jnp.where(mask, aug, 0.0).astype(BF)
                acc[c, h] += dot_tn(aug, pk_o[rows, FEATS * h : FEATS * (h + 1)])

    over_cells(bounds, blk, cells, BLK, one)

    @pl.when(blk == pl.num_programs(0) - 1)
    def _():
        store_sums(acc, sums_o, cells, False)


PAD = pl.BlockSpec((1, BLK), lambda i: (0, i))


def rows_spec(cols):
    return pl.BlockSpec((BLK, cols), lambda i: (i, 0))


def wide_spec(cols):
    return pl.BlockSpec((WIDE_BLK, cols), lambda i: (i, 0))


def whole_spec(shape):
    return pl.BlockSpec(shape, lambda i: (0,) * len(shape))


def whole_specs(arrays):
    return [whole_spec(v.shape) for v in arrays]


SMEM = pl.BlockSpec(memory_space=pltpu.SMEM)
ANY = pl.BlockSpec(memory_space=pl.ANY)
HBM = pl.BlockSpec(memory_space=pltpu.HBM)
VM = pl.BlockSpec(memory_space=pltpu.VMEM)


def params():
    return pltpu.CompilerParams(vmem_limit_bytes=VMEM_LIMIT, dimension_semantics=("arbitrary",))


def cost(gflop, mb):
    return pl.CostEstimate(flops=int(gflop * 1e3), bytes_accessed=int(mb * 1e3), transcendentals=0)


def sums_shape(cells):
    return (2, cells, KVROWS, FEATS)


def shape(*dims, kind=BF):
    return jax.ShapeDtypeStruct(dims, kind)


def run_keys(bounds, x, padding, bank, pieces, places, cells):
    n, d = x.shape
    out_specs = [
        rows_spec(d), rows_spec(d), rows_spec(HEADS * FEATS), rows_spec(d), whole_spec(sums_shape(cells)), whole_spec((16, d)),
    ]
    out_shape = [
        shape(n, d), shape(n, d), shape(n, HEADS * FEATS), shape(n, d), shape(*sums_shape(cells)), shape(16, d, kind=F32),
    ]
    scratch = [pltpu.VMEM((cells, HEADS, 128, FEATS), F32)] + FEATURE_SCRATCH
    if places:
        piece = pieces[0].shape
        w = (d // (2 * piece[1]), 2) + piece[1:]
        out_specs.append(whole_spec(w))
        out_shape.append(shape(*w))
        scratch.append(pltpu.SemaphoreType.DMA((d // piece[1],)))
    return pl.pallas_call(
        functools.partial(key_kernel, cells, places),
        grid=(n // BLK,),
        in_specs=[SMEM, rows_spec(d), PAD, whole_spec(bank.shape)]
        + ([ANY] * len(pieces) if places else whole_specs(pieces)),
        out_specs=out_specs,
        out_shape=out_shape,
        scratch_shapes=scratch,
        compiler_params=params(),
        cost_estimate=cost(8, 10),
        name="keys",
    )(bounds, x, padding, bank, *pieces)


def shuffle(j, rows, wide, d):
    a = lax.broadcasted_iota(jnp.int32, (d, d // wide), 0)
    b = lax.broadcasted_iota(jnp.int32, (d, d // wide), 1)
    hit = (a // (rows * wide) == b // rows) & (a % (rows * wide) == rows * j + b % rows)
    return jnp.where(hit, 1.0, 0.0).astype(BF)


def pad_rows(lines, count):
    return jnp.concatenate(lines + [jnp.zeros((count - len(lines), lines[0].shape[1]), lines[0].dtype)], 0)


def in_order(table, rows, wide):
    d = table.shape[1]
    part = d // wide
    total = jnp.zeros((8, d), F32)
    for j in range(wide):
        lines = pad_rows([table[5 + j : 6 + j, part * k : part * (k + 1)] for k in range(wide)], 8)
        total += dot_nt(lines.astype(BF), shuffle(j, rows, wide, d))
    return total


def by_owner(lines, rows, wide):
    d = lines.shape[1]
    out = []
    for j in range(wide):
        got = dot(lines.astype(BF), shuffle(j, rows, wide, d))
        out.append(jnp.concatenate([got[k : k + 1] for k in range(wide)], 1))
    return out


def query_kernel(rows, wide, a1, wq, bank, vec, sq_o, pq_o, up_o, rm, rr):
    @pl.when(pl.program_id(0) == 0)
    def _():
        feature_parts(bank, rm, rr)
        up_o[...] = in_order(vec[...], rows, wide)

    q = dot(a1[...], wq[...])
    for p in range(PAIRS):
        s, feats = phi_pair(q[:, 128 * p : 128 * p + 128], rm, rr)
        sq_o[:, 128 * p : 128 * p + 128] = s.astype(BF)
        for odd in (0, 1):
            h = 2 * p + odd
            pq_o[:, FEATS * h : FEATS * (h + 1)] = feats[odd].astype(BF)


def run_queries(a1, w, bank, vec, rows, wide):
    n, d = a1.shape
    return pl.pallas_call(
        functools.partial(query_kernel, rows, wide),
        grid=(n // BLK,),
        in_specs=[rows_spec(d), whole_spec((d, d)), whole_spec(bank.shape), whole_spec(vec.shape)],
        out_specs=[rows_spec(d), rows_spec(HEADS * FEATS), whole_spec((8, d))],
        out_shape=[shape(n, d), shape(n, HEADS * FEATS), shape(8, d, kind=F32)],
        scratch_shapes=FEATURE_SCRATCH,
        compiler_params=params(),
        cost_estimate=cost(5, 7),
        name="queries",
    )(a1, w, bank, vec)


def spread_kernel(cells, slots, bounds, own, got, out, mine, theirs, sems):
    spot = lax.axis_index("fsdp")
    core = spot % 2
    made = []
    for z in range(out.shape[0]):
        c = cell_at(bounds, z * (2 * slots) + jnp.where(z > spot // 2, 0, 2 * slots - 1), cells)
        made.append(pltpu.make_async_copy(own.at[core, c], mine.at[z], sems.at[0, z]))
        made.append(pltpu.make_async_copy(got.at[core, c], theirs.at[z], sems.at[1, z]))
    for copy in made:
        copy.start()
    for z in range(out.shape[0]):
        made[2 * z].wait()
        made[2 * z + 1].wait()
        out[z] = (mine[z].astype(F32) + theirs[z].astype(F32)).astype(BF)


def run_spread(bounds, own, got, chips, slots, cells):
    part = pltpu.VMEM((chips, KVROWS, FEATS), BF)
    return pl.pallas_call(
        functools.partial(spread_kernel, cells, slots),
        in_specs=[SMEM, ANY, ANY],
        out_specs=VM,
        out_shape=shape(chips, KVROWS, FEATS),
        scratch_shapes=[part, part, pltpu.SemaphoreType.DMA((2, chips))],
        compiler_params=pltpu.CompilerParams(vmem_limit_bytes=4 * 1024 * 1024),
        cost_estimate=cost(0.001, 2),
        name="spread",
    )(bounds, own, got)


def middle_kernel(cells, slots, nsums, places, bounds, x, dy_r, pad, pq, vec, b_up, *refs):
    sums, refs = refs[:nsums], refs[nsums:]
    count = 2 * len(places) if places else 3
    pieces, refs = refs[:count], refs[count:]
    mixed_o, gr_o, dpre_o, a2_o, ar_o, do_o, dx_o, grads_o, vec_o, vup_o, sums_o, full = refs[:12]
    acc, num_s, den_s = refs[12:15]
    blk = pl.program_id(0)
    width = x.shape[1]
    wide = gr_o.shape[1] // width
    if places:
        w, sems = refs[15:]
        rows = width // (2 * w.shape[0])
        base = rows * (1 + wide)
        w_out = lambda: w[:, :, 0:rows, :].reshape(width, width)
        w_up = lambda j: w[:, :, rows * (1 + j) : rows * (2 + j), :].reshape(width, width)
        w_down = lambda j: w[j * (w.shape[0] // wide) : (j + 1) * (w.shape[0] // wide), :, base:, :].reshape(width, width)
    else:
        w_out = lambda: pieces[0][...]
        w_up = lambda j: pieces[1][:, j * width : (j + 1) * width]
        w_down = lambda j: pieces[2][j * width : (j + 1) * width, :]

    @pl.when(blk == 0)
    def _():
        if places:
            for copy in copies(pieces, places, w, sems):
                copy.start()
        acc[...] = jnp.zeros_like(acc)
        vec_o[...] = jnp.zeros_like(vec_o)
        vup_o[...] = jnp.zeros_like(vup_o)
        load_sums(bounds, sums, full, slots, cells, False)

    low = lane_low(SUB)

    def attend(c, rows, first):
        mask = cell_mask(bounds, c, first, 128)
        for p in range(PAIRS):
            h = 2 * p
            lanes = slice(128 * p, 128 * p + 128)
            r0 = dot_nt(pq[rows, FEATS * h : FEATS * (h + 1)], full[c, h])
            r1 = dot_nt(pq[rows, FEATS * (h + 1) : FEATS * (h + 2)], full[c, h + 1])
            num = jnp.where(low, r0, r1)
            den = pltpu.roll(jnp.where(low, r1, r0), HEAD, 1)
            num_s[rows, lanes] = jnp.where(mask, num, num_s[rows, lanes])
            den_s[rows, lanes] = jnp.where(mask, den, den_s[rows, lanes])

    over_cells(bounds, blk, cells, x.shape[0], attend)
    if places:
        @pl.when(blk == 0)
        def _():
            for copy in copies(pieces, places, w, sems):
                copy.wait()

    keep = keep_lanes(pad)
    keep = jnp.concatenate([keep] * (width // 128), 1)
    inv = 1.0 / den_s[...]
    ar = (keep * num_s[...] * inv).astype(BF)
    ar_o[...] = ar
    x2 = x[...].astype(F32) + dot(ar, w_out())
    z2, r2 = norm_stats(x2)
    g2 = vec[2:3]
    a2 = (z2 * g2 + vec[3:4]).astype(BF)
    a2_o[...] = a2
    dy = dy_r[...]
    mixed = x2 + vec[4:5]
    da2 = jnp.zeros_like(x2)
    k0 = math.sqrt(2.0 / math.pi)
    k1 = 0.044715 * k0
    for j in range(wide):
        cols = slice(j * width, (j + 1) * width)
        pre = dot(a2, w_up(j)) + b_up[j : j + 1]
        sq = pre * pre
        t = jnp.tanh(pre * (k0 + k1 * sq))
        half = 0.5 + 0.5 * t
        act = pre * half
        slope = half + act * (1.0 - t) * (k0 + (3.0 * k1) * sq)
        gr = act.astype(BF)
        gr_o[:, cols] = gr
        mixed += dot(gr, w_down(j))
        dpre = (dot_nt(dy, w_down(j)) * slope).astype(BF)
        dpre_o[:, cols] = dpre
        da2 += dot_nt(dpre, w_up(j))
        vup_o[j : j + 1] += jnp.sum(dpre.astype(F32), 0, keepdims=True)
    mixed_o[...] = mixed.astype(BF)
    dyf = dy.astype(F32)
    dz = da2 * g2
    m1 = jnp.sum(dz, -1, keepdims=True) * (1.0 / width)
    m2 = jnp.sum(dz * z2, -1, keepdims=True) * (1.0 / width)
    dx2 = dyf + r2 * (dz - m1 - z2 * m2)
    dx_o[...] = dx2
    vec_o[2:3, :] += jnp.sum(da2 * z2, 0, keepdims=True)
    vec_o[3:4, :] += jnp.sum(da2, 0, keepdims=True)
    vec_o[4:5, :] += jnp.sum(dyf, 0, keepdims=True)
    do = dx2.astype(BF)
    do_o[...] = do
    dattn = keep * dot_nt(do, w_out()).astype(BF).astype(F32)
    dnum = dattn * inv
    dden = -dnum * num_s[...] * inv
    low = lane_low(x.shape[0])
    for p in range(PAIRS):
        lanes = slice(128 * p, 128 * p + 128)
        mine = dnum[:, lanes]
        swap = pltpu.roll(dden[:, lanes], HEAD, 1)
        h = 2 * p
        grads_o[:, 128 * h : 128 * h + 128] = jnp.where(low, mine, swap).astype(BF)
        grads_o[:, 128 * h + 128 : 128 * h + 256] = jnp.where(low, swap, mine).astype(BF)

    def gather(c, rows, first):
        mask = cell_mask(bounds, c, first, 128)
        for h in range(HEADS):
            part = grads_o[rows, 128 * h : 128 * h + 128]
            part = jnp.where(mask, part.astype(F32), 0.0).astype(BF)
            acc[c, h] += dot_tn(part, pq[rows, FEATS * h : FEATS * (h + 1)])

    over_cells(bounds, blk, cells, x.shape[0], gather)

    @pl.when(blk == pl.num_programs(0) - 1)
    def _():
        store_sums(acc, sums_o, cells, True)


def run_middle(bounds, x, dy, padding, pq, vec, b_up, sums, pieces, places, ff, cells):
    n, d = x.shape
    wide = HEADS * 128
    full = (cells, HEADS, 128, FEATS)
    scratch = [pltpu.VMEM(full, F32), pltpu.VMEM((WIDE_BLK, d), F32), pltpu.VMEM((WIDE_BLK, d), F32)]
    if places:
        rows = max(hi for _, _, hi in places)
        chips = 1 + max(m for masks, _, _ in places for m in masks)
        number = 2 * sum(len(masks) for masks, _, _ in places)
        scratch += [pltpu.VMEM((chips, 2, rows, d), BF), pltpu.SemaphoreType.DMA((number,))]
    return pl.pallas_call(
        functools.partial(middle_kernel, cells, n, len(sums), places),
        grid=(n // WIDE_BLK,),
        in_specs=[
            SMEM, wide_spec(d), wide_spec(d), pl.BlockSpec((1, WIDE_BLK), lambda i: (0, i)), wide_spec(HEADS * FEATS), whole_spec(vec.shape), whole_spec(b_up.shape),
        ]
        + whole_specs(sums)
        + ([ANY] * len(pieces) if places else whole_specs(pieces)),
        out_specs=[
            wide_spec(d), wide_spec(ff), wide_spec(ff), wide_spec(d), wide_spec(d), wide_spec(d),
            wide_spec(d), wide_spec(wide), whole_spec((16, d)), whole_spec((8, d)),
            whole_spec(sums_shape(cells)), whole_spec(full),
        ],
        out_shape=[
            shape(n, d), shape(n, ff), shape(n, ff), shape(n, d), shape(n, d), shape(n, d),
            shape(n, d, kind=F32), shape(n, wide), shape(16, d, kind=F32), shape(8, d, kind=F32),
            shape(*sums_shape(cells)), shape(*full),
        ],
        scratch_shapes=scratch,
        compiler_params=params(),
        cost_estimate=cost(14, 30),
        name="middle",
    )(bounds, x, dy, padding, pq, vec, b_up, *sums, *pieces)


def phi_back(s, feats, rhs, low):
    r0 = dot_nt(feats[0].astype(BF), rhs[0])
    r1 = dot_nt(feats[1].astype(BF), rhs[1])
    total = pltpu.roll(jnp.where(low, r1, r0), HEAD, 1)
    return (jnp.where(low, r0, r1) - s * total) * SCALE


def query_back_kernel(cells, bounds, grads, pq, sq, full, bank, a1, dq_o, gq_o, sum_o, g_s, rhs):
    blk = pl.program_id(0)

    @pl.when(blk == 0)
    def _():
        back_parts(bank, rhs)
        gq_o[...] = jnp.zeros_like(gq_o)
        sum_o[...] = jnp.zeros_like(sum_o)

    low = lane_low(BLK)

    def one(c, rows, first):
        mask = cell_mask(bounds, c, first, FEATS)
        for h in range(HEADS):
            cols = slice(FEATS * h, FEATS * (h + 1))
            g = dot(grads[rows, 128 * h : 128 * h + 128], full[c, h])
            g_s[rows, cols] = jnp.where(mask, g, g_s[rows, cols])

    over_cells(bounds, blk, cells, BLK, one)
    for p in range(PAIRS):
        lanes = slice(128 * p, 128 * p + 128)
        feats = []
        for odd in (0, 1):
            cols = slice(FEATS * (2 * p + odd), FEATS * (2 * p + odd + 1))
            feats.append(g_s[:, cols] * pq[:, cols].astype(F32))
        dq_o[:, lanes] = phi_back(sq[:, lanes].astype(F32), feats, rhs, low).astype(BF)
    dq = dq_o[...]
    gq_o[...] += dot_tn(a1[...], dq)
    sum_o[0:1] += jnp.sum(dq.astype(F32), 0, keepdims=True)


def run_query_back(bounds, grads, pq, sq, full, bank, a1, cells):
    n, d = sq.shape
    return pl.pallas_call(
        functools.partial(query_back_kernel, cells),
        grid=(n // BLK,),
        in_specs=[
            SMEM, rows_spec(HEADS * 128), rows_spec(HEADS * FEATS), rows_spec(d),
            whole_spec(full.shape), whole_spec(bank.shape), rows_spec(d),
        ],
        out_specs=[rows_spec(d), whole_spec((d, d)), whole_spec((8, d))],
        out_shape=[shape(n, d), shape(d, d, kind=F32), shape(8, d, kind=F32)],
        scratch_shapes=[pltpu.VMEM((BLK, HEADS * FEATS), F32), pltpu.VMEM((2, 128, FEATS), BF)],
        compiler_params=params(),
        cost_estimate=cost(3, 8),
        name="query_back",
    )(bounds, grads, pq, sq, full, bank, a1)


def weight_kernel(rows, a2, dpre, gr, dy, ar, do, top_k, top_s, low_k, low_s, ar_s, do_s, sems):
    j = pl.program_id(0)
    last = pl.num_programs(0) - 1
    d = a2.shape[1]
    made = [pltpu.make_async_copy(src, dst, sems.at[i]) for i, (src, dst) in enumerate(((ar, ar_s), (do, do_s)))]

    def put(value, kept, sent):
        count, size = kept.shape[:2]
        mine, theirs = both_cores(value.reshape(count, 2, size, d))
        kept[...] = mine.astype(BF)
        sent[...] = theirs.astype(BF)

    @pl.when(j == 0)
    def _():
        for copy in made:
            copy.start()

    @pl.when(j < last)
    def _():
        put(dot_tn(a2[...], dpre[...]), top_k, top_s)
        put(dot_tn(gr[...], dy[...]), low_k, low_s)

    @pl.when(j == last)
    def _():
        for copy in made:
            copy.wait()
        put(dot_tn(ar_s[...], do_s[...]), top_k, top_s)


def run_weights(a2, dpre, gr, dy, ar, do, rows):
    n, d = a2.shape
    wide = dpre.shape[1] // d
    chips = d // (2 * rows)
    cols = pl.BlockSpec((n, d), lambda j: (0, jnp.minimum(j, wide - 1)))
    whole = whole_spec((n, d))
    top = pl.BlockSpec((chips, rows, d), lambda j: (0, j, 0))
    low = pl.BlockSpec((chips // wide, rows * wide, d), lambda j: (jnp.minimum(j, wide - 1), 0, 0))
    tops, lows = shape(chips, rows * (wide + 1), d), shape(chips, rows * wide, d)
    return pl.pallas_call(
        functools.partial(weight_kernel, rows),
        grid=(wide + 1,),
        in_specs=[whole, cols, cols, whole, HBM, HBM],
        out_specs=[top, top, low, low],
        out_shape=[tops, tops, lows, lows],
        scratch_shapes=[pltpu.VMEM((n, d), BF), pltpu.VMEM((n, d), BF), pltpu.SemaphoreType.DMA((2,))],
        compiler_params=params(),
        cost_estimate=cost(5, 20),
        name="weights",
    )(a2, dpre, gr, dy, ar, do)


def key_back_kernel(cells, slots, nsums, paired, rows, wide, bounds, a1, pk, vr, sk, gvec, vup, bank, w, gq, qsum, *refs):
    sums, refs = refs[:nsums], refs[nsums:]
    dk_o, dv_o, outs = refs[0], refs[1], refs[2 : 4 if paired else 3]
    full, g_s, v_s, rhs, gk_s, gv_s, sum_s = refs[4 if paired else 3 :]
    blk = pl.program_id(0)
    d = a1.shape[1]

    @pl.when(blk == 0)
    def _():
        gk_s[...] = jnp.zeros_like(gk_s)
        gv_s[...] = jnp.zeros_like(gv_s)
        sum_s[...] = qsum[...]
        back_parts(bank, rhs)
        load_sums(bounds, sums, full, slots, cells, True)

    low = lane_low(BLK)

    def one(c, rows, first):
        mask = cell_mask(bounds, c, first, FEATS)
        narrow = cell_mask(bounds, c, first, 128)
        low = lane_low(SUB)
        for p in range(PAIRS):
            lanes = slice(128 * p, 128 * p + 128)
            v = vr[rows, lanes].astype(F32)
            outs = []
            for odd in (0, 1):
                h = 2 * p + odd
                cols = slice(FEATS * h, FEATS * (h + 1))
                aug = (jnp.where(low, 1.0, v) if odd else jnp.where(low, v, 1.0)).astype(BF)
                g = dot(aug, full[c, h])
                g_s[rows, cols] = jnp.where(mask, g, g_s[rows, cols])
                outs.append(dot_nt(pk[rows, cols], full[c, h]))
            v_s[rows, lanes] = jnp.where(narrow, jnp.where(low, outs[0], outs[1]), v_s[rows, lanes])

    over_cells(bounds, blk, cells, BLK, one)
    for p in range(PAIRS):
        lanes = slice(128 * p, 128 * p + 128)
        feats = []
        for odd in (0, 1):
            cols = slice(FEATS * (2 * p + odd), FEATS * (2 * p + odd + 1))
            feats.append(g_s[:, cols] * pk[:, cols].astype(F32))
        dk_o[:, lanes] = phi_back(sk[:, lanes].astype(F32), feats, rhs, low).astype(BF)
    dk = dk_o[...]
    dv = v_s[...].astype(BF)
    dv_o[...] = dv
    gk_s[...] += dot_tn(a1[...], dk)
    gv_s[...] += dot_tn(a1[...], dv)
    sum_s[1:2] += jnp.sum(dk.astype(F32), 0, keepdims=True)
    sum_s[2:3] += jnp.sum(dv.astype(F32), 0, keepdims=True)

    @pl.when(blk == pl.num_programs(0) - 1)
    def _():
        gain = w[:, 3 * d : 3 * d + 1].astype(F32)
        shift = w[:, 3 * d + 1 : 3 * d + 2].astype(F32)
        total = jnp.zeros((d, 1), F32)
        plain = jnp.zeros((d, 1), F32)

        def put(lo, value):
            cols = slice(lo, lo + value.shape[1])
            if paired:
                kept, sent = both_cores(value.reshape(outs[0].shape[0], 2, rows, value.shape[1]))
                outs[0][:, :, cols] = kept.astype(BF)
                outs[1][:, :, cols] = sent.astype(BF)
            else:
                outs[0][:, cols] = value.astype(BF)

        for i, grad in enumerate((gq, gk_s, gv_s)):
            weight = w[:, i * d : (i + 1) * d].astype(F32)
            line = sum_s[i : i + 1]
            total += jnp.sum(weight * grad[...], -1, keepdims=True)
            plain += jnp.sum(weight * line, -1, keepdims=True)
            put(i * d, grad[...])
        lines = [gvec[i : i + 1] for i in range(5)] + by_owner(vup[...], rows, wide)
        vt = pad_rows(lines, 128).T
        lane = lax.broadcasted_iota(jnp.int32, vt.shape, 1)
        vt = jnp.where(lane == 0, (total - shift * plain) / gain, jnp.where(lane == 1, plain, vt))
        put(3 * d, vt)


def run_key_back(bounds, a1, pk, vr, sk, gvec, vup, bank, w, gq, qsum, sums, rows, wide, paired, cells):
    n, d = a1.shape
    total = w.shape[1]
    gout = [(d // (2 * rows), rows, total)] * 2 if paired else [(d, total)]
    square = pltpu.VMEM((d, d), F32)
    return pl.pallas_call(
        functools.partial(key_back_kernel, cells, n, len(sums), paired, rows, wide),
        grid=(n // BLK,),
        in_specs=[SMEM, rows_spec(d), rows_spec(HEADS * FEATS), rows_spec(d), rows_spec(d)]
        + whole_specs((gvec, vup, bank, w, gq, qsum))
        + whole_specs(sums),
        out_specs=[rows_spec(d), rows_spec(d)] + [whole_spec(g) for g in gout],
        out_shape=[shape(n, d), shape(n, d)] + [shape(*g) for g in gout],
        scratch_shapes=[
            pltpu.VMEM((cells, HEADS, 128, FEATS), BF),
            pltpu.VMEM((BLK, HEADS * FEATS), F32),
            pltpu.VMEM((BLK, d), F32),
            pltpu.VMEM((2, 128, FEATS), BF),
            square,
            square,
            pltpu.VMEM((8, d), F32),
        ],
        compiler_params=params(),
        cost_estimate=cost(6, 14),
        name="key_back",
    )(bounds, a1, pk, vr, sk, gvec, vup, bank, w, gq, qsum, *sums)


def token_back_kernel(x, dq, dk, dv, dx, vec, w, gt_o):
    d = x.shape[1]
    da1 = dot_nt(dq[...], w[:, :d]) + dot_nt(dk[...], w[:, d : 2 * d]) + dot_nt(dv[...], w[:, 2 * d : 3 * d])
    z, r = norm_stats(x[...].astype(F32))
    dz = da1 * vec[0:1]
    m1 = jnp.sum(dz, -1, keepdims=True) * (1.0 / d)
    m2 = jnp.sum(dz * z, -1, keepdims=True) * (1.0 / d)
    gt_o[...] = dx[...] + r * (dz - m1 - z * m2)


def run_token_back(x, dq, dk, dv, dx, vec, w):
    n, d = x.shape
    return pl.pallas_call(
        token_back_kernel,
        grid=(n // BLK,),
        in_specs=[rows_spec(d)] * 5 + whole_specs((vec, w)),
        out_specs=rows_spec(d),
        out_shape=shape(n, d, kind=F32),
        compiler_params=params(),
        cost_estimate=cost(2, 8),
        name="token_back",
    )(x, dq, dk, dv, dx, vec, w)


AXES = ("dp", "fsdp")
Z_ALL = (0, 1, 2, 3)
LEAD_MASKS = (Z_ALL, (4, 5, 6, 7), (8, 9, 10, 11), (12, 13, 14, 15))


def flip(x, axis, size, mask):
    return lax.ppermute(x, axis, [(i, i ^ mask) for i in range(size)])


def to_core(x, fsdp):
    return flip(x, "fsdp", fsdp, 1)


def to_z(x, fsdp, mask):
    return flip(x, "fsdp", fsdp, 2 * mask)


def tie(*values):
    return lax.optimization_barrier(values)


def same_core_groups(dp, fsdp):
    return [[d * fsdp + 2 * z + c for d in range(dp) for z in range(fsdp // 2)] for c in range(2)]


def chip_groups(fsdp):
    return [[2 * z + c for z in range(fsdp // 2)] for c in range(2)]


def pack_kernel(wide, w_qkv, g1, s1, w_out, g2, s2, w_up, b_up, w_down, b_down, lead, body):
    rows = w_qkv.shape[0]
    d = w_out.shape[1]
    total = w_qkv.shape[1]
    place = lax.broadcasted_iota(jnp.int32, (128, rows), 0)
    up = b_up[...].astype(F32).reshape(1, -1)
    lines = [v[...].astype(F32).reshape(1, -1) for v in (g1, s1, g2, s2, b_down)]
    lines += [up[:, j * rows : (j + 1) * rows] for j in range(wide)]
    table = jnp.zeros((128, rows), F32)
    for i, line in enumerate(lines):
        table = jnp.where(place == i, line, table)
    across = lax.broadcasted_iota(jnp.int32, (rows, rows), 0) == lax.broadcasted_iota(jnp.int32, (rows, rows), 1)
    lead[:, :total] = w_qkv[...]
    lead[:, total:] = dot_nt(jnp.where(across, 1.0, 0.0).astype(BF), table.astype(BF)).astype(BF)
    body[:rows] = w_out[...]
    for j in range(wide):
        body[rows * (1 + j) : rows * (2 + j)] = w_up[:, j * d : (j + 1) * d]
    body[rows * (1 + wide) :] = w_down[...]


def lead_sum_kernel(wide, *refs):
    parts, wqkv, lines = refs[:-7], refs[-7], refs[-6:]
    total = parts[0][...].astype(F32)
    for part in parts[1:]:
        total += part[...].astype(F32)
    cols = wqkv.shape[1]
    wqkv[...] = total[:, :cols]
    table = total[:, cols:].T
    for i in range(5):
        lines[i][...] = table[i]
    lines[5][...] = jnp.concatenate([table[5 + j : 6 + j] for j in range(wide)], 1)[0]


def run_lead_sum(parts, cols, wide):
    rows = parts[0].shape[0]
    return pl.pallas_call(
        functools.partial(lead_sum_kernel, wide),
        in_specs=[VM] * len(parts),
        out_specs=[VM] * 7,
        out_shape=[shape(rows, cols, kind=F32)] + [shape(rows, kind=F32)] * 5 + [shape(rows * wide, kind=F32)],
        name="lead_sum",
    )(*parts)


def body_sum_kernel(rows, wide, *refs):
    parts, (wout, wup, wdown) = refs[:-3], refs[-3:]
    d = wout.shape[1]
    total = parts[0][...].astype(F32)
    for part in parts[1:]:
        total += part[...].astype(F32)
    for j in range(wide):
        wup[:, j * d : (j + 1) * d] = total[rows * j : rows * (j + 1)]
    wout[...] = total[rows * wide : rows * (1 + wide)]
    wdown[...] = total[rows * (1 + wide) :]


def run_body_sum(parts, rows, wide):
    d = parts[0].shape[1]
    return pl.pallas_call(
        functools.partial(body_sum_kernel, rows, wide),
        in_specs=[VM] * len(parts),
        out_specs=[VM] * 3,
        out_shape=[shape(rows, d, kind=F32), shape(rows, wide * d, kind=F32), shape(rows * wide, d, kind=F32)],
        name="body_sum",
    )(*parts)


def local(dp, fsdp, tokens, bounds, padding, bank, ln1_gain, ln1_bias, w_qkv, w_out, ln2_gain, ln2_bias,
          w_up, b_up, w_down, b_down, cotangent):
    ndev = dp * fsdp
    x = tokens[0]
    dy = cotangent[0]
    n, d = x.shape
    ff = w_up.shape[1]
    cells = bounds.shape[1] - 1
    chips = fsdp // 2
    rows = d // ndev
    wide = ff // d
    frow = ff // ndev
    paired = dp == 4 and fsdp == 8

    shards = (w_qkv, ln1_gain, ln1_bias, w_out, ln2_gain, ln2_bias, w_up, b_up, w_down, b_down)
    if paired:
        lead, body = pl.pallas_call(
            functools.partial(pack_kernel, wide),
            in_specs=[VM] * len(shards),
            out_specs=[VM, VM],
            out_shape=[shape(rows, 3 * d + 128), shape(rows * (1 + wide) + frow, d)],
            name="pack",
        )(*shards)
    else:
        vecs = jnp.concatenate([ln1_gain, ln1_bias, ln2_gain, ln2_bias, b_down, b_up]).reshape(5 + wide, rows)
        lead = jnp.concatenate([w_qkv, jnp.pad(vecs, ((0, 128 - 5 - wide), (0, 0))).T], 1)
        body = jnp.concatenate([w_out] + [w_up[:, j * d : (j + 1) * d] for j in range(wide)] + [w_down], 0)
    cut = rows * (1 + wide)

    if paired:
        first = jnp.stack([lead] + [to_z(lead, fsdp, k) for k in (1, 2, 3)])
        lead_own = [first] + [flip(first, "dp", dp, k) for k in (1, 2, 3)]
        pair = jnp.stack([body, to_z(body, fsdp, 1)])
        pair, *lead_own = tie(pair, *lead_own)
        lead_pieces = lead_own + [to_core(v, fsdp) for v in lead_own]
        four = jnp.concatenate([pair, to_z(pair, fsdp, 2)])
        lead_places = tuple((m, 0, rows) for m in LEAD_MASKS)
    else:
        lead_pieces = [lax.all_gather(lead, AXES, axis=0, tiled=True)]
        parts = lax.all_gather(body, AXES, axis=0)
        take = lambda lo, size: parts[:, lo : lo + size].reshape(ndev * size, d)
        body_pieces = [
            take(0, rows), jnp.concatenate([take((1 + j) * rows, rows) for j in range(wide)], 1), take(cut, frow),
        ]
        lead_places = body_places = None

    def far_sums(out):
        return lax.all_to_all(out, "fsdp", 0, 0, axis_index_groups=chip_groups(fsdp), tiled=True)

    a1, sk, pk, vr, sums, vec, *w = run_keys(bounds, x, padding, bank, lead_pieces, lead_places, cells)
    w = w[0].reshape(d, -1) if paired else lead_pieces[0]
    if paired:
        sums, four = tie(sums, four)
        sums = [sums, to_core(sums, fsdp)]
        out = run_spread(bounds, *sums, chips, n, cells)
        a1_q, out = tie(a1, out)
        far = far_sums(out)
        up, down = four[:, :cut], four[:, cut:]
        up_x, down_y = flip(up, "dp", dp, 1), flip(down, "dp", dp, 2)
        up_y = flip(jnp.concatenate([up, up_x]), "dp", dp, 2)
        down_x = flip(jnp.concatenate([down, down_y]), "dp", dp, 1)
        sq, pq, up_line = run_queries(a1_q, w, bank, vec, rows, wide)
        up_y, down_x, pq, up_line = tie(up_y, down_x, pq, up_line)
        body_own = [four, up_x, down_y, up_y, down_x]
        body_pieces = body_own + [to_core(v, fsdp) for v in body_own]
        body_places = (
            (Z_ALL, 0, cut + frow), ((4, 5, 6, 7), 0, cut), ((8, 9, 10, 11), cut, cut + frow),
            ((8, 9, 10, 11, 12, 13, 14, 15), 0, cut), ((4, 5, 6, 7, 12, 13, 14, 15), cut, cut + frow),
        )
        sums = sums + [far, to_core(far, fsdp)]
    else:
        sums = [lax.psum(sums, "fsdp")]
        sq, pq, up_line = run_queries(a1, w, bank, vec, rows, wide)
    mixed, gr, dpre, a2, ar, do, dx2, grads, gvec, vup, sums, full = run_middle(
        bounds, x, dy, padding, pq, vec, up_line, sums, body_pieces, body_places, ff, cells
    )
    back = lambda gq, qsum, sums: run_key_back(
        bounds, a1, pk, vr, sk, gvec, vup, bank, w, gq, qsum, sums, rows, wide, paired, cells
    )
    if paired:
        top, top_sent, low, low_sent = run_weights(a2, dpre, gr, dy, ar, do, rows)
        got, top_sent, low_sent = tie(to_core(sums, fsdp), top_sent, low_sent)
        sums = [sums, got]
        out = run_spread(bounds, *sums, chips, n, cells)
        far = far_sums(out)
        plus = lambda *parts: functools.reduce(lambda a, b: a + b, [v.astype(F32) for v in parts]).astype(BF)
        ypos, xpos = lax.axis_index("dp") // 2, lax.axis_index("dp") % 2
        pick = lambda value, at, dim: lax.dynamic_index_in_dim(value, at, dim, keepdims=False)
        by_chip = lambda v: v.reshape((2, 2, chips) + v.shape[1:])
        tops = [by_chip(v) for v in (top, to_core(top_sent, fsdp))]
        lows = [by_chip(v) for v in (low, to_core(low_sent, fsdp))]
        top_sent = plus(*[pick(v, 1 - xpos, 1) for v in tops])
        low_sent = plus(*[pick(v, 1 - ypos, 0) for v in lows])
        grads, top_sent, low_sent = tie(grads, top_sent, low_sent)
        top_got, low_got = flip(top_sent, "dp", dp, 1), flip(low_sent, "dp", dp, 2)
        dq, gq, qsum = run_query_back(bounds, grads, pq, sq, full, bank, a1, cells)
        far, gq, qsum, top_got, low_got = tie(far, gq, qsum, top_got, low_got)
        far_got = to_core(far, fsdp)
        tops = [pick(v, xpos, 1) for v in tops] + [top_got]
        lows = [pick(v, ypos, 0) for v in lows] + [low_got]
        both = lambda y, x: ([pick(v, y, 0) for v in tops], [pick(v, x, 0) for v in lows])
        top_sent, low_sent = [plus(*v) for v in both(1 - ypos, 1 - xpos)]
        top_more, low_more = flip(top_sent, "dp", dp, 2), flip(low_sent, "dp", dp, 1)
        dk, dv, kept, sent = back(gq, qsum, sums + [far, far_got])
        kept, sent, top_more, low_more = tie(kept, sent, top_more, low_more)
        tops, lows = both(ypos, xpos)
        whole = jnp.concatenate([plus(*tops, top_more), plus(*lows, low_more)], 1)
        zpos = lax.axis_index("fsdp") // 2
        parts = [pick(whole, zpos, 0)] + [to_z(pick(whole, zpos ^ k, 0), fsdp, k) for k in (1, 2, 3)]
        half = plus(kept, to_core(sent, fsdp)).reshape((dp, chips) + kept.shape[1:])
        dpos = lax.axis_index("dp")
        half = plus(pick(half, dpos, 0), *[flip(pick(half, dpos ^ k, 0), "dp", dp, k) for k in (1, 2, 3)])
        lead_parts = [pick(half, zpos, 0)] + [to_z(pick(half, zpos ^ k, 0), fsdp, k) for k in (1, 2, 3)]
        wqkv, *vecs = run_lead_sum(lead_parts, 3 * d, wide)
        wout, wup, wdown = run_body_sum(parts, rows, wide)
    else:
        dq, gq, qsum = run_query_back(bounds, grads, pq, sq, full, bank, a1, cells)
        dk, dv, glead = back(gq, qsum, [lax.psum(sums, "fsdp")])
        gup = dot_tn(a2, dpre)
        blocks = lambda g, size: g.reshape(ndev, size, d)
        gbody = jnp.concatenate(
            [blocks(dot_tn(ar, do), rows)]
            + [blocks(gup[:, j * d : (j + 1) * d], rows) for j in range(wide)]
            + [blocks(dot_tn(gr, dy), frow)], 1
        )
        gbody = lax.psum_scatter(gbody, AXES, scatter_dimension=0, tiled=True)[0]
        glead = lax.psum_scatter(glead.astype(F32), AXES, scatter_dimension=0, tiled=True)
        gvec = glead[:, 3 * d :].T
        vecs = [gvec[i] for i in range(5)] + [gvec[5 : 5 + wide].reshape(-1)]
        wqkv, wout, wdown = glead[:, : 3 * d], gbody[:rows], gbody[cut:]
        wup = jnp.concatenate([gbody[(1 + j) * rows : (2 + j) * rows] for j in range(wide)], 1)
    gt = run_token_back(x, dq, dk, dv, dx2, vec, w)
    return (
        mixed[None], gt[None], vecs[0], vecs[1], wqkv, wout, vecs[2], vecs[3], wup, vecs[5], wdown, vecs[4],
    )


def solution(mesh):
    both = P(("dp", "fsdp"))
    mat = P(("dp", "fsdp"), None)
    act = P("dp", "fsdp", None)
    return jax.shard_map(
        functools.partial(local, mesh.shape["dp"], mesh.shape["fsdp"]),
        mesh=mesh,
        in_specs=(act, P("dp", None), P("dp", "fsdp"), P(), both, both, mat, mat, both, both, mat, both, mat, both, act),
        out_specs=(act, act, both, both, mat, mat, both, both, mat, both, mat, both),
        check_vma=False,
    )
```

```python
import functools
import math

import jax
import jax.numpy as jnp
from jax import lax
from jax.experimental import pallas as pl
from jax.experimental.pallas import tpu as pltpu
from jax.sharding import PartitionSpec as P

HEADS = 8
FEATS = 256
HEAD = 64
PAIRS = HEADS // 2
SCALE = HEAD ** (-0.25)
LOGF = 0.5 * math.log(FEATS)
BLK = 256
WIDE_BLK = 512
SUB = 256
KVROWS = 272
BF = jnp.bfloat16
F32 = jnp.float32
VMEM_LIMIT = 56 * 1024 * 1024


def dot(a, b):
    return jnp.dot(a, b, preferred_element_type=F32)


def dot_nt(a, b):
    return lax.dot_general(a, b, (((1,), (1,)), ((), ())), preferred_element_type=F32)


def dot_tn(a, b):
    return lax.dot_general(a, b, (((0,), (0,)), ((), ())), preferred_element_type=F32)


def norm_stats(x):
    width = x.shape[-1]
    c = x - jnp.sum(x, -1, keepdims=True) * (1.0 / width)
    r = lax.rsqrt(jnp.sum(c * c, -1, keepdims=True) * (1.0 / width) + 1e-05)
    return c * r, r


def lane_low(n):
    return lax.broadcasted_iota(jnp.int32, (n, 128), 1) < HEAD


def phi_pair(u, rhs_main, rhs_rest):
    low = lane_low(u.shape[0])
    s = u * SCALE
    hi = s.astype(BF)
    lo = (s - hi.astype(F32)).astype(BF)
    both = jnp.concatenate([hi, lo], 1)
    s2 = s * s
    feats = []
    for odd in (0, 1):
        lifted = dot(both, rhs_main[odd]) + dot(hi, rhs_rest[odd])
        half = jnp.sum(jnp.where(low, 0.0, s2) if odd else jnp.where(low, s2, 0.0), -1, keepdims=True)
        feats.append(jnp.exp(lifted - (0.5 * half + LOGF)))
    return s, feats


def over_cells(bounds, blk, cells, block, body):
    for sub in range(block // SUB):
        first = lax.axis_index("fsdp") * (pl.num_programs(0) * block) + blk * block + sub * SUB
        rows = slice(sub * SUB, (sub + 1) * SUB)

        def one(c, carry):
            body(c, rows, first)
            return carry

        lax.fori_loop(cell_at(bounds, first, cells), cell_at(bounds, first + SUB - 1, cells) + 1, one, 0)


def cell_at(bounds, slot, cells):
    cell = jnp.int32(0)
    for c in range(1, cells):
        cell += (bounds[0, c] <= slot).astype(jnp.int32)
    return cell


def cell_mask(bounds, c, first, cols):
    place = lax.broadcasted_iota(jnp.int32, (SUB, cols), 0) + first
    return (place >= bounds[0, c]) & (place < bounds[0, c + 1])


def store_sums(acc, out, cells, summed):
    rows = lax.broadcasted_iota(jnp.int32, (16, FEATS), 0)
    for half in (0, 1):
        for c in range(cells):
            tail = jnp.zeros((16, FEATS), F32)
            for i in range(PAIRS):
                part = acc[c, half * PAIRS + i]
                body, rest = (part[HEAD:], part[:HEAD]) if i % 2 else (part[:HEAD], part[HEAD:])
                out[half, c, i * HEAD : (i + 1) * HEAD, :] = body.astype(BF)
                line = jnp.sum(rest, 0, keepdims=True) if summed else rest[0:1]
                tail = jnp.where(rows == i, line, tail)
            out[half, c, PAIRS * HEAD :, :] = tail.astype(BF)


def load_sums(bounds, sums, full, slots, cells, single):
    rows = lax.broadcasted_iota(jnp.int32, (HEAD, FEATS), 0)
    spot = lax.axis_index("fsdp")
    if len(sums) > 1:
        own, got, far_own, far_other = sums
        core = spot % 2
        start = (spot // 2) * (2 * slots)
        first, last = cell_at(bounds, start, cells), cell_at(bounds, start + 2 * slots - 1, cells)
    for slot in (0, 1):
        if len(sums) > 1:
            half = core ^ slot
            far = far_other if slot else far_own
            before = jnp.zeros(far.shape[1:], F32)
            after = jnp.zeros(far.shape[1:], F32)
            for z in range(far.shape[0]):
                part = far[z].astype(F32)
                before += jnp.where(z < spot // 2, part, 0.0)
                after += jnp.where(z > spot // 2, part, 0.0)
        else:
            half = slot
        for c in range(cells):
            if len(sums) > 1:
                total = own[half, c].astype(F32) + got[half, c].astype(F32)
                total += jnp.where(first == c, before, 0.0) + jnp.where(last == c, after, 0.0)
            else:
                total = sums[0][half, c].astype(F32)
            for i in range(PAIRS):
                body = total[i * HEAD : (i + 1) * HEAD].astype(BF)
                line = jnp.broadcast_to(total[PAIRS * HEAD + i : PAIRS * HEAD + i + 1], (HEAD, FEATS))
                if single:
                    line = jnp.where(rows == 0, line, 0.0)
                line = line.astype(BF)
                h = half * PAIRS + i
                full[c, h, :HEAD, :] = line if i % 2 else body
                full[c, h, HEAD:, :] = body if i % 2 else line


def keep_lanes(pad):
    return jnp.broadcast_to(pad[...].astype(F32), (128, pad.shape[1])).T


def feature_parts(bank, main, rest):
    w = bank[...]
    hi = w.astype(BF)
    lo = (w - hi.astype(F32)).astype(BF)
    none = jnp.zeros_like(hi)
    main[0] = jnp.concatenate([hi, none, hi, none], 0)
    main[1] = jnp.concatenate([none, hi, none, hi], 0)
    rest[0] = jnp.concatenate([lo, none], 0)
    rest[1] = jnp.concatenate([none, lo], 0)


def back_parts(bank, rhs):
    hi = bank[...].astype(BF)
    ones = jnp.ones_like(hi)
    rhs[0] = jnp.concatenate([hi, ones], 0)
    rhs[1] = jnp.concatenate([ones, hi], 0)


FEATURE_SCRATCH = [pltpu.VMEM((2, 4 * HEAD, FEATS), BF), pltpu.VMEM((2, 2 * HEAD, FEATS), BF)]


def copies(pieces, places, target, sems):
    spot = lax.axis_index("fsdp")
    core = spot % 2
    chip = lax.axis_index("dp") * (target.shape[0] // lax.axis_size("dp")) + spot // 2
    made = []
    for i, (masks, lo, hi) in enumerate(places):
        for side in (0, 1):
            src = pieces[i + side * len(places)]
            for k, mask in enumerate(masks):
                dst = target.at[chip ^ mask, core ^ side, lo:hi]
                made.append(pltpu.make_async_copy(src.at[k], dst, sems.at[len(made)]))
    return made


def both_cores(value):
    mine = lax.axis_index("fsdp") % 2 == 0
    a, b = value[:, 0], value[:, 1]
    return jnp.where(mine, a, b), jnp.where(mine, b, a)


def columns(ref, lo, hi):
    value = ref[..., lo:hi]
    return value.reshape(-1, value.shape[-1])


def key_kernel(cells, places, bounds, x, pad, bank, *refs):
    count = 2 * len(places) if places else 1
    pieces, (a1_o, sk_o, pk_o, vr_o, sums_o, vec_o), refs = refs[:count], refs[count : count + 6], refs[count + 6 :]
    if places:
        w, acc, rm, rr, sems = refs
    else:
        w = pieces[0]
        acc, rm, rr = refs
    blk = pl.program_id(0)
    d = x.shape[1]

    @pl.when(blk == 0)
    def _():
        if places:
            made = copies(pieces, places, w, sems)
            for copy in made:
                copy.start()
        acc[...] = jnp.zeros_like(acc)
        feature_parts(bank, rm, rr)
        if places:
            for copy in made:
                copy.wait()
        vec_o[...] = columns(w, 3 * d, 3 * d + 128).astype(F32).T[:16]

    keep = keep_lanes(pad)
    keep = jnp.concatenate([keep, keep], 1)
    z, _ = norm_stats(x[...].astype(F32))
    a1 = (z * vec_o[0:1] + vec_o[1:2]).astype(BF)
    a1_o[...] = a1
    keys = dot(a1, columns(w, d, 2 * d))
    vr_o[...] = dot(a1, columns(w, 2 * d, 3 * d)).astype(BF)
    for p in range(PAIRS):
        s, feats = phi_pair(keys[:, 128 * p : 128 * p + 128], rm, rr)
        sk_o[:, 128 * p : 128 * p + 128] = s.astype(BF)
        for odd in (0, 1):
            h = 2 * p + odd
            pk_o[:, FEATS * h : FEATS * (h + 1)] = (keep * feats[odd]).astype(BF)
    low = lane_low(SUB)

    def one(c, rows, first):
        mask = cell_mask(bounds, c, first, 128)
        for p in range(PAIRS):
            v = vr_o[rows, 128 * p : 128 * p + 128].astype(F32)
            for odd in (0, 1):
                h = 2 * p + odd
                aug = jnp.where(low, 1.0, v) if odd else jnp.where(low, v, 1.0)
                aug = jnp.where(mask, aug, 0.0).astype(BF)
                acc[c, h] += dot_tn(aug, pk_o[rows, FEATS * h : FEATS * (h + 1)])

    over_cells(bounds, blk, cells, BLK, one)

    @pl.when(blk == pl.num_programs(0) - 1)
    def _():
        store_sums(acc, sums_o, cells, False)


PAD = pl.BlockSpec((1, BLK), lambda i: (0, i))


def rows_spec(cols):
    return pl.BlockSpec((BLK, cols), lambda i: (i, 0))


def wide_spec(cols):
    return pl.BlockSpec((WIDE_BLK, cols), lambda i: (i, 0))


def whole_spec(shape):
    return pl.BlockSpec(shape, lambda i: (0,) * len(shape))


def whole_specs(arrays):
    return [whole_spec(v.shape) for v in arrays]


SMEM = pl.BlockSpec(memory_space=pltpu.SMEM)
ANY = pl.BlockSpec(memory_space=pl.ANY)
HBM = pl.BlockSpec(memory_space=pltpu.HBM)
VM = pl.BlockSpec(memory_space=pltpu.VMEM)


def params():
    return pltpu.CompilerParams(vmem_limit_bytes=VMEM_LIMIT, dimension_semantics=("arbitrary",))


def cost(gflop, mb):
    return pl.CostEstimate(flops=int(gflop * 1e3), bytes_accessed=int(mb * 1e3), transcendentals=0)


def sums_shape(cells):
    return (2, cells, KVROWS, FEATS)


def shape(*dims, kind=BF):
    return jax.ShapeDtypeStruct(dims, kind)


def run_keys(bounds, x, padding, bank, pieces, places, cells):
    n, d = x.shape
    out_specs = [
        rows_spec(d), rows_spec(d), rows_spec(HEADS * FEATS), rows_spec(d), whole_spec(sums_shape(cells)), whole_spec((16, d)),
    ]
    out_shape = [
        shape(n, d), shape(n, d), shape(n, HEADS * FEATS), shape(n, d), shape(*sums_shape(cells)), shape(16, d, kind=F32),
    ]
    scratch = [pltpu.VMEM((cells, HEADS, 128, FEATS), F32)] + FEATURE_SCRATCH
    if places:
        piece = pieces[0].shape
        w = (d // (2 * piece[1]), 2) + piece[1:]
        out_specs.append(whole_spec(w))
        out_shape.append(shape(*w))
        scratch.append(pltpu.SemaphoreType.DMA((d // piece[1],)))
    return pl.pallas_call(
        functools.partial(key_kernel, cells, places),
        grid=(n // BLK,),
        in_specs=[SMEM, rows_spec(d), PAD, whole_spec(bank.shape)]
        + ([ANY] * len(pieces) if places else whole_specs(pieces)),
        out_specs=out_specs,
        out_shape=out_shape,
        scratch_shapes=scratch,
        compiler_params=params(),
        cost_estimate=cost(8, 10),
        name="keys",
    )(bounds, x, padding, bank, *pieces)


def shuffle(j, rows, wide, d):
    a = lax.broadcasted_iota(jnp.int32, (d, d // wide), 0)
    b = lax.broadcasted_iota(jnp.int32, (d, d // wide), 1)
    hit = (a // (rows * wide) == b // rows) & (a % (rows * wide) == rows * j + b % rows)
    return jnp.where(hit, 1.0, 0.0).astype(BF)


def pad_rows(lines, count):
    return jnp.concatenate(lines + [jnp.zeros((count - len(lines), lines[0].shape[1]), lines[0].dtype)], 0)


def in_order(table, rows, wide):
    d = table.shape[1]
    part = d // wide
    total = jnp.zeros((8, d), F32)
    for j in range(wide):
        lines = pad_rows([table[5 + j : 6 + j, part * k : part * (k + 1)] for k in range(wide)], 8)
        total += dot_nt(lines.astype(BF), shuffle(j, rows, wide, d))
    return total


def by_owner(lines, rows, wide):
    d = lines.shape[1]
    out = []
    for j in range(wide):
        got = dot(lines.astype(BF), shuffle(j, rows, wide, d))
        out.append(jnp.concatenate([got[k : k + 1] for k in range(wide)], 1))
    return out


def query_kernel(rows, wide, a1, wq, bank, vec, sq_o, pq_o, up_o, rm, rr):
    @pl.when(pl.program_id(0) == 0)
    def _():
        feature_parts(bank, rm, rr)
        up_o[...] = in_order(vec[...], rows, wide)

    q = dot(a1[...], wq[...])
    for p in range(PAIRS):
        s, feats = phi_pair(q[:, 128 * p : 128 * p + 128], rm, rr)
        sq_o[:, 128 * p : 128 * p + 128] = s.astype(BF)
        for odd in (0, 1):
            h = 2 * p + odd
            pq_o[:, FEATS * h : FEATS * (h + 1)] = feats[odd].astype(BF)


def run_queries(a1, w, bank, vec, rows, wide):
    n, d = a1.shape
    return pl.pallas_call(
        functools.partial(query_kernel, rows, wide),
        grid=(n // BLK,),
        in_specs=[rows_spec(d), whole_spec((d, d)), whole_spec(bank.shape), whole_spec(vec.shape)],
        out_specs=[rows_spec(d), rows_spec(HEADS * FEATS), whole_spec((8, d))],
        out_shape=[shape(n, d), shape(n, HEADS * FEATS), shape(8, d, kind=F32)],
        scratch_shapes=FEATURE_SCRATCH,
        compiler_params=params(),
        cost_estimate=cost(5, 7),
        name="queries",
    )(a1, w, bank, vec)


def spread_kernel(cells, slots, bounds, own, got, out, mine, theirs, sems):
    spot = lax.axis_index("fsdp")
    core = spot % 2
    made = []
    for z in range(out.shape[0]):
        c = cell_at(bounds, z * (2 * slots) + jnp.where(z > spot // 2, 0, 2 * slots - 1), cells)
        made.append(pltpu.make_async_copy(own.at[core, c], mine.at[z], sems.at[0, z]))
        made.append(pltpu.make_async_copy(got.at[core, c], theirs.at[z], sems.at[1, z]))
    for copy in made:
        copy.start()
    for z in range(out.shape[0]):
        made[2 * z].wait()
        made[2 * z + 1].wait()
        out[z] = (mine[z].astype(F32) + theirs[z].astype(F32)).astype(BF)


def run_spread(bounds, own, got, chips, slots, cells):
    part = pltpu.VMEM((chips, KVROWS, FEATS), BF)
    return pl.pallas_call(
        functools.partial(spread_kernel, cells, slots),
        in_specs=[SMEM, ANY, ANY],
        out_specs=VM,
        out_shape=shape(chips, KVROWS, FEATS),
        scratch_shapes=[part, part, pltpu.SemaphoreType.DMA((2, chips))],
        compiler_params=pltpu.CompilerParams(vmem_limit_bytes=4 * 1024 * 1024),
        cost_estimate=cost(0.001, 2),
        name="spread",
    )(bounds, own, got)


def middle_kernel(cells, slots, nsums, places, bounds, x, dy_r, pad, pq, vec, b_up, *refs):
    sums, refs = refs[:nsums], refs[nsums:]
    count = 2 * len(places) if places else 3
    pieces, refs = refs[:count], refs[count:]
    mixed_o, gr_o, dpre_o, a2_o, ar_o, do_o, dx_o, grads_o, vec_o, vup_o, sums_o, full = refs[:12]
    acc, num_s, den_s = refs[12:15]
    blk = pl.program_id(0)
    width = x.shape[1]
    wide = gr_o.shape[1] // width
    if places:
        w, sems = refs[15:]
        rows = width // (2 * w.shape[0])
        base = rows * (1 + wide)
        w_out = lambda: w[:, :, 0:rows, :].reshape(width, width)
        w_up = lambda j: w[:, :, rows * (1 + j) : rows * (2 + j), :].reshape(width, width)
        w_down = lambda j: w[j * (w.shape[0] // wide) : (j + 1) * (w.shape[0] // wide), :, base:, :].reshape(width, width)
    else:
        w_out = lambda: pieces[0][...]
        w_up = lambda j: pieces[1][:, j * width : (j + 1) * width]
        w_down = lambda j: pieces[2][j * width : (j + 1) * width, :]

    @pl.when(blk == 0)
    def _():
        if places:
            for copy in copies(pieces, places, w, sems):
                copy.start()
        acc[...] = jnp.zeros_like(acc)
        vec_o[...] = jnp.zeros_like(vec_o)
        vup_o[...] = jnp.zeros_like(vup_o)
        load_sums(bounds, sums, full, slots, cells, False)

    low = lane_low(SUB)

    def attend(c, rows, first):
        mask = cell_mask(bounds, c, first, 128)
        for p in range(PAIRS):
            h = 2 * p
            lanes = slice(128 * p, 128 * p + 128)
            r0 = dot_nt(pq[rows, FEATS * h : FEATS * (h + 1)], full[c, h])
            r1 = dot_nt(pq[rows, FEATS * (h + 1) : FEATS * (h + 2)], full[c, h + 1])
            num = jnp.where(low, r0, r1)
            den = pltpu.roll(jnp.where(low, r1, r0), HEAD, 1)
            num_s[rows, lanes] = jnp.where(mask, num, num_s[rows, lanes])
            den_s[rows, lanes] = jnp.where(mask, den, den_s[rows, lanes])

    over_cells(bounds, blk, cells, x.shape[0], attend)
    if places:
        @pl.when(blk == 0)
        def _():
            for copy in copies(pieces, places, w, sems):
                copy.wait()

    keep = keep_lanes(pad)
    keep = jnp.concatenate([keep] * (width // 128), 1)
    inv = 1.0 / den_s[...]
    ar = (keep * num_s[...] * inv).astype(BF)
    ar_o[...] = ar
    x2 = x[...].astype(F32) + dot(ar, w_out())
    z2, r2 = norm_stats(x2)
    g2 = vec[2:3]
    a2 = (z2 * g2 + vec[3:4]).astype(BF)
    a2_o[...] = a2
    dy = dy_r[...]
    mixed = x2 + vec[4:5]
    da2 = jnp.zeros_like(x2)
    k0 = math.sqrt(2.0 / math.pi)
    k1 = 0.044715 * k0
    for j in range(wide):
        cols = slice(j * width, (j + 1) * width)
        pre = dot(a2, w_up(j)) + b_up[j : j + 1]
        sq = pre * pre
        t = jnp.tanh(pre * (k0 + k1 * sq))
        half = 0.5 + 0.5 * t
        act = pre * half
        slope = half + act * (1.0 - t) * (k0 + (3.0 * k1) * sq)
        gr = act.astype(BF)
        gr_o[:, cols] = gr
        mixed += dot(gr, w_down(j))
        dpre = (dot_nt(dy, w_down(j)) * slope).astype(BF)
        dpre_o[:, cols] = dpre
        da2 += dot_nt(dpre, w_up(j))
        vup_o[j : j + 1] += jnp.sum(dpre.astype(F32), 0, keepdims=True)
    mixed_o[...] = mixed.astype(BF)
    dyf = dy.astype(F32)
    dz = da2 * g2
    m1 = jnp.sum(dz, -1, keepdims=True) * (1.0 / width)
    m2 = jnp.sum(dz * z2, -1, keepdims=True) * (1.0 / width)
    dx2 = dyf + r2 * (dz - m1 - z2 * m2)
    dx_o[...] = dx2
    vec_o[2:3, :] += jnp.sum(da2 * z2, 0, keepdims=True)
    vec_o[3:4, :] += jnp.sum(da2, 0, keepdims=True)
    vec_o[4:5, :] += jnp.sum(dyf, 0, keepdims=True)
    do = dx2.astype(BF)
    do_o[...] = do
    dattn = keep * dot_nt(do, w_out()).astype(BF).astype(F32)
    dnum = dattn * inv
    dden = -dnum * num_s[...] * inv
    low = lane_low(x.shape[0])
    for p in range(PAIRS):
        lanes = slice(128 * p, 128 * p + 128)
        mine = dnum[:, lanes]
        swap = pltpu.roll(dden[:, lanes], HEAD, 1)
        h = 2 * p
        grads_o[:, 128 * h : 128 * h + 128] = jnp.where(low, mine, swap).astype(BF)
        grads_o[:, 128 * h + 128 : 128 * h + 256] = jnp.where(low, swap, mine).astype(BF)

    def gather(c, rows, first):
        mask = cell_mask(bounds, c, first, 128)
        for h in range(HEADS):
            part = grads_o[rows, 128 * h : 128 * h + 128]
            part = jnp.where(mask, part.astype(F32), 0.0).astype(BF)
            acc[c, h] += dot_tn(part, pq[rows, FEATS * h : FEATS * (h + 1)])

    over_cells(bounds, blk, cells, x.shape[0], gather)

    @pl.when(blk == pl.num_programs(0) - 1)
    def _():
        store_sums(acc, sums_o, cells, True)


def run_middle(bounds, x, dy, padding, pq, vec, b_up, sums, pieces, places, ff, cells):
    n, d = x.shape
    wide = HEADS * 128
    full = (cells, HEADS, 128, FEATS)
    scratch = [pltpu.VMEM(full, F32), pltpu.VMEM((WIDE_BLK, d), F32), pltpu.VMEM((WIDE_BLK, d), F32)]
    if places:
        rows = max(hi for _, _, hi in places)
        chips = 1 + max(m for masks, _, _ in places for m in masks)
        number = 2 * sum(len(masks) for masks, _, _ in places)
        scratch += [pltpu.VMEM((chips, 2, rows, d), BF), pltpu.SemaphoreType.DMA((number,))]
    return pl.pallas_call(
        functools.partial(middle_kernel, cells, n, len(sums), places),
        grid=(n // WIDE_BLK,),
        in_specs=[
            SMEM, wide_spec(d), wide_spec(d), pl.BlockSpec((1, WIDE_BLK), lambda i: (0, i)), wide_spec(HEADS * FEATS), whole_spec(vec.shape), whole_spec(b_up.shape),
        ]
        + whole_specs(sums)
        + ([ANY] * len(pieces) if places else whole_specs(pieces)),
        out_specs=[
            wide_spec(d), wide_spec(ff), wide_spec(ff), wide_spec(d), wide_spec(d), wide_spec(d),
            wide_spec(d), wide_spec(wide), whole_spec((16, d)), whole_spec((8, d)),
            whole_spec(sums_shape(cells)), whole_spec(full),
        ],
        out_shape=[
            shape(n, d), shape(n, ff), shape(n, ff), shape(n, d), shape(n, d), shape(n, d),
            shape(n, d, kind=F32), shape(n, wide), shape(16, d, kind=F32), shape(8, d, kind=F32),
            shape(*sums_shape(cells)), shape(*full),
        ],
        scratch_shapes=scratch,
        compiler_params=params(),
        cost_estimate=cost(14, 30),
        name="middle",
    )(bounds, x, dy, padding, pq, vec, b_up, *sums, *pieces)


def phi_back(s, feats, rhs, low):
    r0 = dot_nt(feats[0].astype(BF), rhs[0])
    r1 = dot_nt(feats[1].astype(BF), rhs[1])
    total = pltpu.roll(jnp.where(low, r1, r0), HEAD, 1)
    return (jnp.where(low, r0, r1) - s * total) * SCALE


def query_back_kernel(cells, bounds, grads, pq, sq, full, bank, a1, dq_o, gq_o, sum_o, g_s, rhs):
    blk = pl.program_id(0)

    @pl.when(blk == 0)
    def _():
        back_parts(bank, rhs)
        gq_o[...] = jnp.zeros_like(gq_o)
        sum_o[...] = jnp.zeros_like(sum_o)

    low = lane_low(BLK)

    def one(c, rows, first):
        mask = cell_mask(bounds, c, first, FEATS)
        for h in range(HEADS):
            cols = slice(FEATS * h, FEATS * (h + 1))
            g = dot(grads[rows, 128 * h : 128 * h + 128], full[c, h])
            g_s[rows, cols] = jnp.where(mask, g, g_s[rows, cols])

    over_cells(bounds, blk, cells, BLK, one)
    for p in range(PAIRS):
        lanes = slice(128 * p, 128 * p + 128)
        feats = []
        for odd in (0, 1):
            cols = slice(FEATS * (2 * p + odd), FEATS * (2 * p + odd + 1))
            feats.append(g_s[:, cols] * pq[:, cols].astype(F32))
        dq_o[:, lanes] = phi_back(sq[:, lanes].astype(F32), feats, rhs, low).astype(BF)
    dq = dq_o[...]
    gq_o[...] += dot_tn(a1[...], dq)
    sum_o[0:1] += jnp.sum(dq.astype(F32), 0, keepdims=True)


def run_query_back(bounds, grads, pq, sq, full, bank, a1, cells):
    n, d = sq.shape
    return pl.pallas_call(
        functools.partial(query_back_kernel, cells),
        grid=(n // BLK,),
        in_specs=[
            SMEM, rows_spec(HEADS * 128), rows_spec(HEADS * FEATS), rows_spec(d),
            whole_spec(full.shape), whole_spec(bank.shape), rows_spec(d),
        ],
        out_specs=[rows_spec(d), whole_spec((d, d)), whole_spec((8, d))],
        out_shape=[shape(n, d), shape(d, d, kind=F32), shape(8, d, kind=F32)],
        scratch_shapes=[pltpu.VMEM((BLK, HEADS * FEATS), F32), pltpu.VMEM((2, 128, FEATS), BF)],
        compiler_params=params(),
        cost_estimate=cost(3, 8),
        name="query_back",
    )(bounds, grads, pq, sq, full, bank, a1)


def weight_kernel(rows, a2, dpre, gr, dy, ar, do, top_k, top_s, low_k, low_s, ar_s, do_s, sems):
    j = pl.program_id(0)
    last = pl.num_programs(0) - 1
    d = a2.shape[1]
    made = [pltpu.make_async_copy(src, dst, sems.at[i]) for i, (src, dst) in enumerate(((ar, ar_s), (do, do_s)))]

    def put(value, kept, sent):
        count, size = kept.shape[:2]
        mine, theirs = both_cores(value.reshape(count, 2, size, d))
        kept[...] = mine.astype(BF)
        sent[...] = theirs.astype(BF)

    @pl.when(j == 0)
    def _():
        for copy in made:
            copy.start()

    @pl.when(j < last)
    def _():
        put(dot_tn(a2[...], dpre[...]), top_k, top_s)
        put(dot_tn(gr[...], dy[...]), low_k, low_s)

    @pl.when(j == last)
    def _():
        for copy in made:
            copy.wait()
        put(dot_tn(ar_s[...], do_s[...]), top_k, top_s)


def run_weights(a2, dpre, gr, dy, ar, do, rows):
    n, d = a2.shape
    wide = dpre.shape[1] // d
    chips = d // (2 * rows)
    cols = pl.BlockSpec((n, d), lambda j: (0, jnp.minimum(j, wide - 1)))
    whole = whole_spec((n, d))
    top = pl.BlockSpec((chips, rows, d), lambda j: (0, j, 0))
    low = pl.BlockSpec((chips // wide, rows * wide, d), lambda j: (jnp.minimum(j, wide - 1), 0, 0))
    tops, lows = shape(chips, rows * (wide + 1), d), shape(chips, rows * wide, d)
    return pl.pallas_call(
        functools.partial(weight_kernel, rows),
        grid=(wide + 1,),
        in_specs=[whole, cols, cols, whole, HBM, HBM],
        out_specs=[top, top, low, low],
        out_shape=[tops, tops, lows, lows],
        scratch_shapes=[pltpu.VMEM((n, d), BF), pltpu.VMEM((n, d), BF), pltpu.SemaphoreType.DMA((2,))],
        compiler_params=params(),
        cost_estimate=cost(5, 20),
        name="weights",
    )(a2, dpre, gr, dy, ar, do)


def fold_kernel(parts, *refs):
    ins, outs, bufs, sems = refs[:4], refs[4 : 4 + parts], refs[4 + parts : 8 + parts], refs[8 + parts]
    me = lax.axis_index("dp")
    size = ins[0].shape[0] // parts
    made = []
    for k in range(parts):
        rows = pl.ds((me ^ k) * size, size)
        for i in range(4):
            made.append(pltpu.make_async_copy(ins[i].at[rows], bufs[i].at[k], sems.at[k, i]))
    for copy in made:
        copy.start()
    cut = ins[0].shape[1]
    for k in range(parts):
        for copy in made[4 * k : 4 * k + 4]:
            copy.wait()
        outs[k][:, :cut] = (bufs[0][k].astype(F32) + bufs[1][k].astype(F32)).astype(BF)
        outs[k][:, cut:] = (bufs[2][k].astype(F32) + bufs[3][k].astype(F32)).astype(BF)


def run_fold(top, top_got, low, low_got, parts):
    size, d = top.shape[0] // parts, top.shape[2]
    out = shape(size, top.shape[1] + low.shape[1], d)
    bufs = [pltpu.VMEM((parts, size) + v.shape[1:], BF) for v in (top, top_got, low, low_got)]
    return pl.pallas_call(
        functools.partial(fold_kernel, parts),
        in_specs=[ANY] * 4,
        out_specs=[VM] * parts,
        out_shape=[out] * parts,
        scratch_shapes=bufs + [pltpu.SemaphoreType.DMA((parts, 4))],
        compiler_params=pltpu.CompilerParams(vmem_limit_bytes=16 * 1024 * 1024),
        cost_estimate=cost(0.001, 7),
        name="fold",
    )(top, top_got, low, low_got)


def key_back_kernel(cells, slots, nsums, paired, rows, wide, bounds, a1, pk, vr, sk, gvec, vup, bank, w, gq, qsum, *refs):
    sums, refs = refs[:nsums], refs[nsums:]
    dk_o, dv_o, outs = refs[0], refs[1], refs[2 : 4 if paired else 3]
    full, g_s, v_s, rhs, gk_s, gv_s, sum_s, w_s, gq_s, sems = refs[4 if paired else 3 :]
    made = [pltpu.make_async_copy(a, b, sems.at[i]) for i, (a, b) in enumerate(((w, w_s), (gq, gq_s)))]
    blk = pl.program_id(0)
    d = a1.shape[1]

    @pl.when(blk == 0)
    def _():
        for copy in made:
            copy.start()
        gk_s[...] = jnp.zeros_like(gk_s)
        gv_s[...] = jnp.zeros_like(gv_s)
        sum_s[...] = qsum[...]
        back_parts(bank, rhs)
        load_sums(bounds, sums, full, slots, cells, True)

    low = lane_low(BLK)

    def one(c, rows, first):
        mask = cell_mask(bounds, c, first, FEATS)
        narrow = cell_mask(bounds, c, first, 128)
        low = lane_low(SUB)
        for p in range(PAIRS):
            lanes = slice(128 * p, 128 * p + 128)
            v = vr[rows, lanes].astype(F32)
            outs = []
            for odd in (0, 1):
                h = 2 * p + odd
                cols = slice(FEATS * h, FEATS * (h + 1))
                aug = (jnp.where(low, 1.0, v) if odd else jnp.where(low, v, 1.0)).astype(BF)
                g = dot(aug, full[c, h])
                g_s[rows, cols] = jnp.where(mask, g, g_s[rows, cols])
                outs.append(dot_nt(pk[rows, cols], full[c, h]))
            v_s[rows, lanes] = jnp.where(narrow, jnp.where(low, outs[0], outs[1]), v_s[rows, lanes])

    over_cells(bounds, blk, cells, BLK, one)
    for p in range(PAIRS):
        lanes = slice(128 * p, 128 * p + 128)
        feats = []
        for odd in (0, 1):
            cols = slice(FEATS * (2 * p + odd), FEATS * (2 * p + odd + 1))
            feats.append(g_s[:, cols] * pk[:, cols].astype(F32))
        dk_o[:, lanes] = phi_back(sk[:, lanes].astype(F32), feats, rhs, low).astype(BF)
    dk = dk_o[...]
    dv = v_s[...].astype(BF)
    dv_o[...] = dv
    gk_s[...] += dot_tn(a1[...], dk)
    gv_s[...] += dot_tn(a1[...], dv)
    sum_s[1:2] += jnp.sum(dk.astype(F32), 0, keepdims=True)
    sum_s[2:3] += jnp.sum(dv.astype(F32), 0, keepdims=True)

    @pl.when(blk == pl.num_programs(0) - 1)
    def _():
        for copy in made:
            copy.wait()
        gain = w_s[:, 3 * d : 3 * d + 1].astype(F32)
        shift = w_s[:, 3 * d + 1 : 3 * d + 2].astype(F32)
        total = jnp.zeros((d, 1), F32)
        plain = jnp.zeros((d, 1), F32)

        def put(lo, value):
            cols = slice(lo, lo + value.shape[1])
            if paired:
                kept, sent = both_cores(value.reshape(outs[0].shape[0], 2, rows, value.shape[1]))
                outs[0][:, :, cols] = kept.astype(BF)
                outs[1][:, :, cols] = sent.astype(BF)
            else:
                outs[0][:, cols] = value.astype(BF)

        for i, grad in enumerate((gq_s, gk_s, gv_s)):
            weight = w_s[:, i * d : (i + 1) * d].astype(F32)
            line = sum_s[i : i + 1]
            total += jnp.sum(weight * grad[...], -1, keepdims=True)
            plain += jnp.sum(weight * line, -1, keepdims=True)
            put(i * d, grad[...])
        lines = [gvec[i : i + 1] for i in range(5)] + by_owner(vup[...], rows, wide)
        vt = pad_rows(lines, 128).T
        lane = lax.broadcasted_iota(jnp.int32, vt.shape, 1)
        vt = jnp.where(lane == 0, (total - shift * plain) / gain, jnp.where(lane == 1, plain, vt))
        put(3 * d, vt)


def run_key_back(bounds, a1, pk, vr, sk, gvec, vup, bank, w, gq, qsum, sums, rows, wide, paired, cells):
    n, d = a1.shape
    total = w.shape[1]
    gout = [(d // (2 * rows), rows, total)] * 2 if paired else [(d, total)]
    square = pltpu.VMEM((d, d), F32)
    return pl.pallas_call(
        functools.partial(key_back_kernel, cells, n, len(sums), paired, rows, wide),
        grid=(n // BLK,),
        in_specs=[SMEM, rows_spec(d), rows_spec(HEADS * FEATS), rows_spec(d), rows_spec(d)]
        + whole_specs((gvec, vup, bank)) + [HBM, HBM] + whole_specs((qsum,))
        + whole_specs(sums),
        out_specs=[rows_spec(d), rows_spec(d)] + [whole_spec(g) for g in gout],
        out_shape=[shape(n, d), shape(n, d)] + [shape(*g) for g in gout],
        scratch_shapes=[
            pltpu.VMEM((cells, HEADS, 128, FEATS), BF),
            pltpu.VMEM((BLK, HEADS * FEATS), F32),
            pltpu.VMEM((BLK, d), F32),
            pltpu.VMEM((2, 128, FEATS), BF),
            square,
            square,
            pltpu.VMEM((8, d), F32),
            pltpu.VMEM(w.shape, BF),
            square,
            pltpu.SemaphoreType.DMA((2,)),
        ],
        compiler_params=params(),
        cost_estimate=cost(6, 14),
        name="key_back",
    )(bounds, a1, pk, vr, sk, gvec, vup, bank, w, gq, qsum, *sums)


def token_back_kernel(x, dq, dk, dv, dx, vec, w, gt_o):
    d = x.shape[1]
    da1 = dot_nt(dq[...], w[:, :d]) + dot_nt(dk[...], w[:, d : 2 * d]) + dot_nt(dv[...], w[:, 2 * d : 3 * d])
    z, r = norm_stats(x[...].astype(F32))
    dz = da1 * vec[0:1]
    m1 = jnp.sum(dz, -1, keepdims=True) * (1.0 / d)
    m2 = jnp.sum(dz * z, -1, keepdims=True) * (1.0 / d)
    gt_o[...] = dx[...] + r * (dz - m1 - z * m2)


def run_token_back(x, dq, dk, dv, dx, vec, w):
    n, d = x.shape
    return pl.pallas_call(
        token_back_kernel,
        grid=(n // BLK,),
        in_specs=[rows_spec(d)] * 5 + whole_specs((vec, w)),
        out_specs=rows_spec(d),
        out_shape=shape(n, d, kind=F32),
        compiler_params=params(),
        cost_estimate=cost(2, 8),
        name="token_back",
    )(x, dq, dk, dv, dx, vec, w)


AXES = ("dp", "fsdp")
Z_ALL = (0, 1, 2, 3)
LEAD_MASKS = (Z_ALL, (4, 5, 6, 7), (8, 9, 10, 11), (12, 13, 14, 15))


def flip(x, axis, size, mask):
    return lax.ppermute(x, axis, [(i, i ^ mask) for i in range(size)])


def to_core(x, fsdp):
    return flip(x, "fsdp", fsdp, 1)


def to_z(x, fsdp, mask):
    return flip(x, "fsdp", fsdp, 2 * mask)


def tie(*values):
    return lax.optimization_barrier(values)


def same_core_groups(dp, fsdp):
    return [[d * fsdp + 2 * z + c for d in range(dp) for z in range(fsdp // 2)] for c in range(2)]


def chip_groups(fsdp):
    return [[2 * z + c for z in range(fsdp // 2)] for c in range(2)]


def pack_kernel(wide, w_qkv, g1, s1, w_out, g2, s2, w_up, b_up, w_down, b_down, lead, body):
    rows = w_qkv.shape[0]
    d = w_out.shape[1]
    total = w_qkv.shape[1]
    place = lax.broadcasted_iota(jnp.int32, (128, rows), 0)
    up = b_up[...].astype(F32).reshape(1, -1)
    lines = [v[...].astype(F32).reshape(1, -1) for v in (g1, s1, g2, s2, b_down)]
    lines += [up[:, j * rows : (j + 1) * rows] for j in range(wide)]
    table = jnp.zeros((128, rows), F32)
    for i, line in enumerate(lines):
        table = jnp.where(place == i, line, table)
    across = lax.broadcasted_iota(jnp.int32, (rows, rows), 0) == lax.broadcasted_iota(jnp.int32, (rows, rows), 1)
    lead[:, :total] = w_qkv[...]
    lead[:, total:] = dot_nt(jnp.where(across, 1.0, 0.0).astype(BF), table.astype(BF)).astype(BF)
    body[:rows] = w_out[...]
    for j in range(wide):
        body[rows * (1 + j) : rows * (2 + j)] = w_up[:, j * d : (j + 1) * d]
    body[rows * (1 + wide) :] = w_down[...]


def final_kernel(rows, wide, count, *refs):
    parts, outs = refs[:count], refs[2 * count :]
    wout, wup, wdown, wqkv, *lines = outs
    d = wout.shape[1]
    add = lambda refs: functools.reduce(lambda a, b: a + b, [v[...].astype(F32) for v in refs])
    total = add(refs[count : 2 * count])
    for j in range(wide):
        wup[:, j * d : (j + 1) * d] = total[rows * j : rows * (j + 1)]
    wout[...] = total[rows * wide : rows * (1 + wide)]
    wdown[...] = total[rows * (1 + wide) :]
    total = add(parts)
    cols = wqkv.shape[1]
    wqkv[...] = total[:, :cols]
    table = total[:, cols:].T
    for i in range(5):
        lines[i][...] = table[i]
    lines[5][...] = jnp.concatenate([table[5 + j : 6 + j] for j in range(wide)], 1)[0]


def run_final(lead_parts, body_parts, rows, wide):
    d = body_parts[0].shape[1]
    return pl.pallas_call(
        functools.partial(final_kernel, rows, wide, len(lead_parts)),
        in_specs=[VM] * (2 * len(lead_parts)),
        out_specs=[VM] * 10,
        out_shape=[
            shape(rows, d, kind=F32), shape(rows, wide * d, kind=F32), shape(rows * wide, d, kind=F32),
            shape(rows, 3 * d, kind=F32),
        ]
        + [shape(rows, kind=F32)] * 5
        + [shape(rows * wide, kind=F32)],
        name="final",
    )(*lead_parts, *body_parts)


def local(dp, fsdp, tokens, bounds, padding, bank, ln1_gain, ln1_bias, w_qkv, w_out, ln2_gain, ln2_bias,
          w_up, b_up, w_down, b_down, cotangent):
    ndev = dp * fsdp
    x = tokens[0]
    dy = cotangent[0]
    n, d = x.shape
    ff = w_up.shape[1]
    cells = bounds.shape[1] - 1
    chips = fsdp // 2
    rows = d // ndev
    wide = ff // d
    frow = ff // ndev
    paired = dp == 4 and fsdp == 8

    shards = (w_qkv, ln1_gain, ln1_bias, w_out, ln2_gain, ln2_bias, w_up, b_up, w_down, b_down)
    if paired:
        lead, body = pl.pallas_call(
            functools.partial(pack_kernel, wide),
            in_specs=[VM] * len(shards),
            out_specs=[VM, VM],
            out_shape=[shape(rows, 3 * d + 128), shape(rows * (1 + wide) + frow, d)],
            name="pack",
        )(*shards)
    else:
        vecs = jnp.concatenate([ln1_gain, ln1_bias, ln2_gain, ln2_bias, b_down, b_up]).reshape(5 + wide, rows)
        lead = jnp.concatenate([w_qkv, jnp.pad(vecs, ((0, 128 - 5 - wide), (0, 0))).T], 1)
        body = jnp.concatenate([w_out] + [w_up[:, j * d : (j + 1) * d] for j in range(wide)] + [w_down], 0)
    cut = rows * (1 + wide)

    if paired:
        first = jnp.stack([lead] + [to_z(lead, fsdp, k) for k in (1, 2, 3)])
        lead_own = [first] + [flip(first, "dp", dp, k) for k in (1, 2, 3)]
        pair = jnp.stack([body, to_z(body, fsdp, 1)])
        pair, *lead_own = tie(pair, *lead_own)
        lead_pieces = lead_own + [to_core(v, fsdp) for v in lead_own]
        four = jnp.concatenate([pair, to_z(pair, fsdp, 2)])
        lead_places = tuple((m, 0, rows) for m in LEAD_MASKS)
    else:
        lead_pieces = [lax.all_gather(lead, AXES, axis=0, tiled=True)]
        parts = lax.all_gather(body, AXES, axis=0)
        take = lambda lo, size: parts[:, lo : lo + size].reshape(ndev * size, d)
        body_pieces = [
            take(0, rows), jnp.concatenate([take((1 + j) * rows, rows) for j in range(wide)], 1), take(cut, frow),
        ]
        lead_places = body_places = None

    def far_sums(out):
        return lax.all_to_all(out, "fsdp", 0, 0, axis_index_groups=chip_groups(fsdp), tiled=True)

    a1, sk, pk, vr, sums, vec, *w = run_keys(bounds, x, padding, bank, lead_pieces, lead_places, cells)
    w = w[0].reshape(d, -1) if paired else lead_pieces[0]
    if paired:
        sums, four = tie(sums, four)
        sums = [sums, to_core(sums, fsdp)]
        out = run_spread(bounds, *sums, chips, n, cells)
        a1_q, out = tie(a1, out)
        far = far_sums(out)
        up, down = four[:, :cut], four[:, cut:]
        up_x, down_y = flip(up, "dp", dp, 1), flip(down, "dp", dp, 2)
        up_y = flip(jnp.concatenate([up, up_x]), "dp", dp, 2)
        down_x = flip(jnp.concatenate([down, down_y]), "dp", dp, 1)
        sq, pq, up_line = run_queries(a1_q, w, bank, vec, rows, wide)
        early = [to_core(v, fsdp) for v in (four, up_x, down_y)]
        up_y, down_x, pq, up_line, *early = tie(up_y, down_x, pq, up_line, *early)
        body_pieces = [four, up_x, down_y, up_y, down_x] + early + [to_core(v, fsdp) for v in (up_y, down_x)]
        body_places = (
            (Z_ALL, 0, cut + frow), ((4, 5, 6, 7), 0, cut), ((8, 9, 10, 11), cut, cut + frow),
            ((8, 9, 10, 11, 12, 13, 14, 15), 0, cut), ((4, 5, 6, 7, 12, 13, 14, 15), cut, cut + frow),
        )
        sums = sums + [far, to_core(far, fsdp)]
    else:
        sums = [lax.psum(sums, "fsdp")]
        sq, pq, up_line = run_queries(a1, w, bank, vec, rows, wide)
    mixed, gr, dpre, a2, ar, do, dx2, grads, gvec, vup, sums, full = run_middle(
        bounds, x, dy, padding, pq, vec, up_line, sums, body_pieces, body_places, ff, cells
    )
    back = lambda gq, qsum, sums: run_key_back(
        bounds, a1, pk, vr, sk, gvec, vup, bank, w, gq, qsum, sums, rows, wide, paired, cells
    )
    if paired:
        top, top_sent, low, low_sent = run_weights(a2, dpre, gr, dy, ar, do, rows)
        got, top_sent, low_sent = tie(to_core(sums, fsdp), top_sent, low_sent)
        sums = [sums, got]
        out = run_spread(bounds, *sums, chips, n, cells)
        far = far_sums(out)
        plus = lambda *parts: functools.reduce(lambda a, b: a + b, [v.astype(F32) for v in parts]).astype(BF)
        pick = lambda value, at, dim: lax.dynamic_index_in_dim(value, at, dim, keepdims=False)
        folded = run_fold(top, to_core(top_sent, fsdp), low, to_core(low_sent, fsdp), dp)
        grads, *folded = tie(grads, *folded)
        spread = [flip(v, "dp", dp, k) for k, v in enumerate(folded) if k]
        dq, gq, qsum = run_query_back(bounds, grads, pq, sq, full, bank, a1, cells)
        far, gq, qsum = tie(far, gq, qsum)
        dk, dv, kept, sent = back(gq, qsum, sums + [far, to_core(far, fsdp)])
        kept, sent, *spread = tie(kept, sent, *spread)
        whole = plus(folded[0], *spread)
        zpos = lax.axis_index("fsdp") // 2
        parts = [pick(whole, zpos, 0)] + [to_z(pick(whole, zpos ^ k, 0), fsdp, k) for k in (1, 2, 3)]
        half = plus(kept, to_core(sent, fsdp)).reshape((dp, chips) + kept.shape[1:])
        dpos = lax.axis_index("dp")
        half = plus(pick(half, dpos, 0), *[flip(pick(half, dpos ^ k, 0), "dp", dp, k) for k in (1, 2, 3)])
        lead_parts = [pick(half, zpos, 0)] + [to_z(pick(half, zpos ^ k, 0), fsdp, k) for k in (1, 2, 3)]
        wout, wup, wdown, wqkv, *vecs = run_final(lead_parts, parts, rows, wide)
    else:
        dq, gq, qsum = run_query_back(bounds, grads, pq, sq, full, bank, a1, cells)
        dk, dv, glead = back(gq, qsum, [lax.psum(sums, "fsdp")])
        gup = dot_tn(a2, dpre)
        blocks = lambda g, size: g.reshape(ndev, size, d)
        gbody = jnp.concatenate(
            [blocks(dot_tn(ar, do), rows)]
            + [blocks(gup[:, j * d : (j + 1) * d], rows) for j in range(wide)]
            + [blocks(dot_tn(gr, dy), frow)], 1
        )
        gbody = lax.psum_scatter(gbody, AXES, scatter_dimension=0, tiled=True)[0]
        glead = lax.psum_scatter(glead.astype(F32), AXES, scatter_dimension=0, tiled=True)
        gvec = glead[:, 3 * d :].T
        vecs = [gvec[i] for i in range(5)] + [gvec[5 : 5 + wide].reshape(-1)]
        wqkv, wout, wdown = glead[:, : 3 * d], gbody[:rows], gbody[cut:]
        wup = jnp.concatenate([gbody[(1 + j) * rows : (2 + j) * rows] for j in range(wide)], 1)
    gt = run_token_back(x, dq, dk, dv, dx2, vec, w)
    return (
        mixed[None], gt[None], vecs[0], vecs[1], wqkv, wout, vecs[2], vecs[3], wup, vecs[5], wdown, vecs[4],
    )


def solution(mesh):
    both = P(("dp", "fsdp"))
    mat = P(("dp", "fsdp"), None)
    act = P("dp", "fsdp", None)
    return jax.shard_map(
        functools.partial(local, mesh.shape["dp"], mesh.shape["fsdp"]),
        mesh=mesh,
        in_specs=(act, P("dp", None), P("dp", "fsdp"), P(), both, both, mat, mat, both, both, mat, both, mat, both, act),
        out_specs=(act, act, both, both, mat, mat, both, both, mat, both, mat, both),
        check_vma=False,
    )
```

```python
import functools
import math

import jax
import jax.numpy as jnp
from jax import lax
from jax.experimental import pallas as pl
from jax.experimental.pallas import tpu as pltpu
from jax.sharding import PartitionSpec as P

HEADS = 8
FEATS = 256
HEAD = 64
PAIRS = HEADS // 2
SCALE = HEAD ** (-0.25)
LOGF = 0.5 * math.log(FEATS)
BLK = 256
WIDE_BLK = 512
SUB = 256
KVROWS = 272
BF = jnp.bfloat16
F32 = jnp.float32
VMEM_LIMIT = 56 * 1024 * 1024


def dot(a, b):
    return jnp.dot(a, b, preferred_element_type=F32)


def dot_nt(a, b):
    return lax.dot_general(a, b, (((1,), (1,)), ((), ())), preferred_element_type=F32)


def dot_tn(a, b):
    return lax.dot_general(a, b, (((0,), (0,)), ((), ())), preferred_element_type=F32)


def norm_stats(x):
    width = x.shape[-1]
    c = x - jnp.sum(x, -1, keepdims=True) * (1.0 / width)
    r = lax.rsqrt(jnp.sum(c * c, -1, keepdims=True) * (1.0 / width) + 1e-05)
    return c * r, r


def lane_low(n):
    return lax.broadcasted_iota(jnp.int32, (n, 128), 1) < HEAD


def phi_pair(u, rhs_main, rhs_rest):
    low = lane_low(u.shape[0])
    s = u * SCALE
    hi = s.astype(BF)
    lo = (s - hi.astype(F32)).astype(BF)
    both = jnp.concatenate([hi, lo], 1)
    s2 = s * s
    feats = []
    for odd in (0, 1):
        lifted = dot(both, rhs_main[odd]) + dot(hi, rhs_rest[odd])
        half = jnp.sum(jnp.where(low, 0.0, s2) if odd else jnp.where(low, s2, 0.0), -1, keepdims=True)
        feats.append(jnp.exp(lifted - (0.5 * half + LOGF)))
    return s, feats


def over_cells(bounds, blk, cells, block, body):
    for sub in range(block // SUB):
        first = lax.axis_index("fsdp") * (pl.num_programs(0) * block) + blk * block + sub * SUB
        rows = slice(sub * SUB, (sub + 1) * SUB)

        def one(c, carry):
            body(c, rows, first)
            return carry

        lax.fori_loop(cell_at(bounds, first, cells), cell_at(bounds, first + SUB - 1, cells) + 1, one, 0)


def cell_at(bounds, slot, cells):
    cell = jnp.int32(0)
    for c in range(1, cells):
        cell += (bounds[0, c] <= slot).astype(jnp.int32)
    return cell


def cell_mask(bounds, c, first, cols):
    place = lax.broadcasted_iota(jnp.int32, (SUB, cols), 0) + first
    return (place >= bounds[0, c]) & (place < bounds[0, c + 1])


def store_sums(acc, out, cells, summed):
    rows = lax.broadcasted_iota(jnp.int32, (16, FEATS), 0)
    for half in (0, 1):
        for c in range(cells):
            tail = jnp.zeros((16, FEATS), F32)
            for i in range(PAIRS):
                part = acc[c, half * PAIRS + i]
                body, rest = (part[HEAD:], part[:HEAD]) if i % 2 else (part[:HEAD], part[HEAD:])
                out[half, c, i * HEAD : (i + 1) * HEAD, :] = body.astype(BF)
                line = jnp.sum(rest, 0, keepdims=True) if summed else rest[0:1]
                tail = jnp.where(rows == i, line, tail)
            out[half, c, PAIRS * HEAD :, :] = tail.astype(BF)


def load_sums(bounds, sums, full, slots, cells, single):
    rows = lax.broadcasted_iota(jnp.int32, (HEAD, FEATS), 0)
    spot = lax.axis_index("fsdp")
    if len(sums) > 1:
        own, got, far_own, far_other = sums
        core = spot % 2
        start = (spot // 2) * (2 * slots)
        first, last = cell_at(bounds, start, cells), cell_at(bounds, start + 2 * slots - 1, cells)
    for slot in (0, 1):
        if len(sums) > 1:
            half = core ^ slot
            far = far_other if slot else far_own
            before = jnp.zeros(far.shape[1:], F32)
            after = jnp.zeros(far.shape[1:], F32)
            for z in range(far.shape[0]):
                part = far[z].astype(F32)
                before += jnp.where(z < spot // 2, part, 0.0)
                after += jnp.where(z > spot // 2, part, 0.0)
        else:
            half = slot
        for c in range(cells):
            if len(sums) > 1:
                total = own[half, c].astype(F32) + got[half, c].astype(F32)
                total += jnp.where(first == c, before, 0.0) + jnp.where(last == c, after, 0.0)
            else:
                total = sums[0][half, c].astype(F32)
            for i in range(PAIRS):
                body = total[i * HEAD : (i + 1) * HEAD].astype(BF)
                line = jnp.broadcast_to(total[PAIRS * HEAD + i : PAIRS * HEAD + i + 1], (HEAD, FEATS))
                if single:
                    line = jnp.where(rows == 0, line, 0.0)
                line = line.astype(BF)
                h = half * PAIRS + i
                full[c, h, :HEAD, :] = line if i % 2 else body
                full[c, h, HEAD:, :] = body if i % 2 else line


def keep_lanes(pad):
    return jnp.broadcast_to(pad[...].astype(F32), (128, pad.shape[1])).T


def feature_parts(bank, main, rest):
    w = bank[...]
    hi = w.astype(BF)
    lo = (w - hi.astype(F32)).astype(BF)
    none = jnp.zeros_like(hi)
    main[0] = jnp.concatenate([hi, none, hi, none], 0)
    main[1] = jnp.concatenate([none, hi, none, hi], 0)
    rest[0] = jnp.concatenate([lo, none], 0)
    rest[1] = jnp.concatenate([none, lo], 0)


def back_parts(bank, rhs):
    hi = bank[...].astype(BF)
    ones = jnp.ones_like(hi)
    rhs[0] = jnp.concatenate([hi, ones], 0)
    rhs[1] = jnp.concatenate([ones, hi], 0)


FEATURE_SCRATCH = [pltpu.VMEM((2, 4 * HEAD, FEATS), BF), pltpu.VMEM((2, 2 * HEAD, FEATS), BF)]


def copies(pieces, places, target, sems):
    spot = lax.axis_index("fsdp")
    core = spot % 2
    chip = lax.axis_index("dp") * (target.shape[0] // lax.axis_size("dp")) + spot // 2
    made = []
    for i, (masks, lo, hi) in enumerate(places):
        for side in (0, 1):
            src = pieces[i + side * len(places)]
            for k, mask in enumerate(masks):
                dst = target.at[chip ^ mask, core ^ side, lo:hi]
                made.append(pltpu.make_async_copy(src.at[k], dst, sems.at[len(made)]))
    return made


def both_cores(value):
    mine = lax.axis_index("fsdp") % 2 == 0
    a, b = value[:, 0], value[:, 1]
    return jnp.where(mine, a, b), jnp.where(mine, b, a)


def columns(ref, lo, hi):
    value = ref[..., lo:hi]
    return value.reshape(-1, value.shape[-1])


def key_kernel(cells, places, bounds, x, pad, bank, *refs):
    count = 2 * len(places) if places else 1
    pieces, (a1_o, sk_o, pk_o, vr_o, sums_o, vec_o), refs = refs[:count], refs[count : count + 6], refs[count + 6 :]
    if places:
        w_o, acc, rm, rr, w, sems, out_sem = refs
        leave = pltpu.make_async_copy(w, w_o, out_sem)
    else:
        w = pieces[0]
        acc, rm, rr = refs
    blk = pl.program_id(0)
    d = x.shape[1]

    @pl.when(blk == 0)
    def _():
        if places:
            made = copies(pieces, places, w, sems)
            for copy in made:
                copy.start()
        acc[...] = jnp.zeros_like(acc)
        feature_parts(bank, rm, rr)
        if places:
            for copy in made:
                copy.wait()
            leave.start()
        vec_o[...] = columns(w, 3 * d, 3 * d + 128).astype(F32).T[:16]

    keep = keep_lanes(pad)
    keep = jnp.concatenate([keep, keep], 1)
    z, _ = norm_stats(x[...].astype(F32))
    a1 = (z * vec_o[0:1] + vec_o[1:2]).astype(BF)
    a1_o[...] = a1
    keys = dot(a1, columns(w, d, 2 * d))
    vr_o[...] = dot(a1, columns(w, 2 * d, 3 * d)).astype(BF)
    for p in range(PAIRS):
        s, feats = phi_pair(keys[:, 128 * p : 128 * p + 128], rm, rr)
        sk_o[:, 128 * p : 128 * p + 128] = s.astype(BF)
        for odd in (0, 1):
            h = 2 * p + odd
            pk_o[:, FEATS * h : FEATS * (h + 1)] = (keep * feats[odd]).astype(BF)
    low = lane_low(SUB)

    def one(c, rows, first):
        mask = cell_mask(bounds, c, first, 128)
        for p in range(PAIRS):
            v = vr_o[rows, 128 * p : 128 * p + 128].astype(F32)
            for odd in (0, 1):
                h = 2 * p + odd
                aug = jnp.where(low, 1.0, v) if odd else jnp.where(low, v, 1.0)
                aug = jnp.where(mask, aug, 0.0).astype(BF)
                acc[c, h] += dot_tn(aug, pk_o[rows, FEATS * h : FEATS * (h + 1)])

    over_cells(bounds, blk, cells, BLK, one)

    @pl.when(blk == pl.num_programs(0) - 1)
    def _():
        store_sums(acc, sums_o, cells, False)
        if places:
            leave.wait()


PAD = pl.BlockSpec((1, BLK), lambda i: (0, i))


def rows_spec(cols):
    return pl.BlockSpec((BLK, cols), lambda i: (i, 0))


def wide_spec(cols):
    return pl.BlockSpec((WIDE_BLK, cols), lambda i: (i, 0))


def whole_spec(shape):
    return pl.BlockSpec(shape, lambda i: (0,) * len(shape))


def whole_specs(arrays):
    return [whole_spec(v.shape) for v in arrays]


SMEM = pl.BlockSpec(memory_space=pltpu.SMEM)
ANY = pl.BlockSpec(memory_space=pl.ANY)
HBM = pl.BlockSpec(memory_space=pltpu.HBM)
VM = pl.BlockSpec(memory_space=pltpu.VMEM)


def params():
    return pltpu.CompilerParams(vmem_limit_bytes=VMEM_LIMIT, dimension_semantics=("arbitrary",))


def cost(gflop, mb):
    return pl.CostEstimate(flops=int(gflop * 1e3), bytes_accessed=int(mb * 1e3), transcendentals=0)


def sums_shape(cells):
    return (2, cells, KVROWS, FEATS)


def shape(*dims, kind=BF):
    return jax.ShapeDtypeStruct(dims, kind)


def run_keys(bounds, x, padding, bank, pieces, places, cells):
    n, d = x.shape
    out_specs = [
        rows_spec(d), rows_spec(d), rows_spec(HEADS * FEATS), rows_spec(d), whole_spec(sums_shape(cells)), whole_spec((16, d)),
    ]
    out_shape = [
        shape(n, d), shape(n, d), shape(n, HEADS * FEATS), shape(n, d), shape(*sums_shape(cells)), shape(16, d, kind=F32),
    ]
    scratch = [pltpu.VMEM((cells, HEADS, 128, FEATS), F32)] + FEATURE_SCRATCH
    if places:
        piece = pieces[0].shape
        w = (d // (2 * piece[1]), 2) + piece[1:]
        out_specs.append(HBM)
        out_shape.append(shape(*w))
        scratch += [pltpu.VMEM(w, BF), pltpu.SemaphoreType.DMA((d // piece[1],)), pltpu.SemaphoreType.DMA]
    return pl.pallas_call(
        functools.partial(key_kernel, cells, places),
        grid=(n // BLK,),
        in_specs=[SMEM, rows_spec(d), PAD, whole_spec(bank.shape)]
        + ([ANY] * len(pieces) if places else whole_specs(pieces)),
        out_specs=out_specs,
        out_shape=out_shape,
        scratch_shapes=scratch,
        compiler_params=params(),
        cost_estimate=cost(8, 10),
        name="keys",
    )(bounds, x, padding, bank, *pieces)


def shuffle(j, rows, wide, d):
    a = lax.broadcasted_iota(jnp.int32, (d, d // wide), 0)
    b = lax.broadcasted_iota(jnp.int32, (d, d // wide), 1)
    hit = (a // (rows * wide) == b // rows) & (a % (rows * wide) == rows * j + b % rows)
    return jnp.where(hit, 1.0, 0.0).astype(BF)


def pad_rows(lines, count):
    return jnp.concatenate(lines + [jnp.zeros((count - len(lines), lines[0].shape[1]), lines[0].dtype)], 0)


def in_order(table, rows, wide):
    d = table.shape[1]
    part = d // wide
    total = jnp.zeros((8, d), F32)
    for j in range(wide):
        lines = pad_rows([table[5 + j : 6 + j, part * k : part * (k + 1)] for k in range(wide)], 8)
        total += dot_nt(lines.astype(BF), shuffle(j, rows, wide, d))
    return total


def by_owner(lines, rows, wide):
    d = lines.shape[1]
    out = []
    for j in range(wide):
        got = dot(lines.astype(BF), shuffle(j, rows, wide, d))
        out.append(jnp.concatenate([got[k : k + 1] for k in range(wide)], 1))
    return out


def query_kernel(rows, wide, a1, wq, bank, vec, sq_o, pq_o, up_o, rm, rr):
    @pl.when(pl.program_id(0) == 0)
    def _():
        feature_parts(bank, rm, rr)
        up_o[...] = in_order(vec[...], rows, wide)

    q = dot(a1[...], wq[...])
    for p in range(PAIRS):
        s, feats = phi_pair(q[:, 128 * p : 128 * p + 128], rm, rr)
        sq_o[:, 128 * p : 128 * p + 128] = s.astype(BF)
        for odd in (0, 1):
            h = 2 * p + odd
            pq_o[:, FEATS * h : FEATS * (h + 1)] = feats[odd].astype(BF)


def run_queries(a1, w, bank, vec, rows, wide):
    n, d = a1.shape
    return pl.pallas_call(
        functools.partial(query_kernel, rows, wide),
        grid=(n // BLK,),
        in_specs=[rows_spec(d), whole_spec((d, d)), whole_spec(bank.shape), whole_spec(vec.shape)],
        out_specs=[rows_spec(d), rows_spec(HEADS * FEATS), whole_spec((8, d))],
        out_shape=[shape(n, d), shape(n, HEADS * FEATS), shape(8, d, kind=F32)],
        scratch_shapes=FEATURE_SCRATCH,
        compiler_params=params(),
        cost_estimate=cost(5, 7),
        name="queries",
    )(a1, w, bank, vec)


def spread_kernel(cells, slots, bounds, own, got, out, mine, theirs, sems):
    spot = lax.axis_index("fsdp")
    core = spot % 2
    made = []
    for z in range(out.shape[0]):
        c = cell_at(bounds, z * (2 * slots) + jnp.where(z > spot // 2, 0, 2 * slots - 1), cells)
        made.append(pltpu.make_async_copy(own.at[core, c], mine.at[z], sems.at[0, z]))
        made.append(pltpu.make_async_copy(got.at[core, c], theirs.at[z], sems.at[1, z]))
    for copy in made:
        copy.start()
    for z in range(out.shape[0]):
        made[2 * z].wait()
        made[2 * z + 1].wait()
        out[z] = (mine[z].astype(F32) + theirs[z].astype(F32)).astype(BF)


def run_spread(bounds, own, got, chips, slots, cells):
    part = pltpu.VMEM((chips, KVROWS, FEATS), BF)
    return pl.pallas_call(
        functools.partial(spread_kernel, cells, slots),
        in_specs=[SMEM, HBM, ANY],
        out_specs=VM,
        out_shape=shape(chips, KVROWS, FEATS),
        scratch_shapes=[part, part, pltpu.SemaphoreType.DMA((2, chips))],
        compiler_params=pltpu.CompilerParams(vmem_limit_bytes=4 * 1024 * 1024),
        cost_estimate=cost(0.001, 2),
        name="spread",
    )(bounds, own, got)


def middle_kernel(cells, slots, nsums, places, bounds, x, dy_r, pad, pq, vec, b_up, *refs):
    sums, refs = refs[:nsums], refs[nsums:]
    count = 2 * len(places) if places else 3
    pieces, refs = refs[:count], refs[count:]
    mixed_o, gr_o, dpre_o, a2_o, ar_o, do_o, dx_o, grads_o, vec_o, vup_o, sums_o, full_o = refs[:12]
    acc, num_s, den_s, full, gr_s, dpre_s, out_sems = refs[12:19]
    blk = pl.program_id(0)
    width = x.shape[1]
    wide = gr_o.shape[1] // width
    if places:
        w, sems = refs[19:]
        rows = width // (2 * w.shape[0])
        base = rows * (1 + wide)
        w_out = lambda: w[:, :, 0:rows, :].reshape(width, width)
        w_up = lambda j: w[:, :, rows * (1 + j) : rows * (2 + j), :].reshape(width, width)
        w_down = lambda j: w[j * (w.shape[0] // wide) : (j + 1) * (w.shape[0] // wide), :, base:, :].reshape(width, width)
    else:
        w_out = lambda: pieces[0][...]
        w_up = lambda j: pieces[1][:, j * width : (j + 1) * width]
        w_down = lambda j: pieces[2][j * width : (j + 1) * width, :]

    full_out = pltpu.make_async_copy(full, full_o, out_sems.at[2, 0])
    size = x.shape[0]

    def leave(i, j, at):
        src, dst = ((gr_s, gr_o), (dpre_s, dpre_o))[i]
        cols = slice(j * width, (j + 1) * width)
        rows = pl.ds(pl.multiple_of(at * size, size), size)
        return pltpu.make_async_copy(src.at[:, cols], dst.at[rows, cols], out_sems.at[i, j])

    @pl.when(blk == 0)
    def _():
        if places:
            for copy in copies(pieces, places, w, sems):
                copy.start()
        acc[...] = jnp.zeros_like(acc)
        vec_o[...] = jnp.zeros_like(vec_o)
        vup_o[...] = jnp.zeros_like(vup_o)
        load_sums(bounds, sums, full, slots, cells, False)
        full_out.start()

    @pl.when(blk > 0)
    def _():
        for j in range(wide):
            leave(0, j, blk - 1).wait()
            leave(1, j, blk - 1).wait()

    low = lane_low(SUB)

    def attend(c, rows, first):
        mask = cell_mask(bounds, c, first, 128)
        for p in range(PAIRS):
            h = 2 * p
            lanes = slice(128 * p, 128 * p + 128)
            r0 = dot_nt(pq[rows, FEATS * h : FEATS * (h + 1)], full[c, h])
            r1 = dot_nt(pq[rows, FEATS * (h + 1) : FEATS * (h + 2)], full[c, h + 1])
            num = jnp.where(low, r0, r1)
            den = pltpu.roll(jnp.where(low, r1, r0), HEAD, 1)
            num_s[rows, lanes] = jnp.where(mask, num, num_s[rows, lanes])
            den_s[rows, lanes] = jnp.where(mask, den, den_s[rows, lanes])

    over_cells(bounds, blk, cells, x.shape[0], attend)
    if places:
        @pl.when(blk == 0)
        def _():
            for copy in copies(pieces, places, w, sems):
                copy.wait()

    keep = keep_lanes(pad)
    keep = jnp.concatenate([keep] * (width // 128), 1)
    inv = 1.0 / den_s[...]
    ar = (keep * num_s[...] * inv).astype(BF)
    ar_o[...] = ar
    x2 = x[...].astype(F32) + dot(ar, w_out())
    z2, r2 = norm_stats(x2)
    g2 = vec[2:3]
    a2 = (z2 * g2 + vec[3:4]).astype(BF)
    a2_o[...] = a2
    dy = dy_r[...]
    mixed = x2 + vec[4:5]
    da2 = jnp.zeros_like(x2)
    k0 = math.sqrt(2.0 / math.pi)
    k1 = 0.044715 * k0
    for j in range(wide):
        cols = slice(j * width, (j + 1) * width)
        pre = dot(a2, w_up(j)) + b_up[j : j + 1]
        sq = pre * pre
        t = jnp.tanh(pre * (k0 + k1 * sq))
        half = 0.5 + 0.5 * t
        act = pre * half
        slope = half + act * (1.0 - t) * (k0 + (3.0 * k1) * sq)
        gr = act.astype(BF)
        gr_s[:, cols] = gr
        leave(0, j, blk).start()
        mixed += dot(gr, w_down(j))
        dpre = (dot_nt(dy, w_down(j)) * slope).astype(BF)
        dpre_s[:, cols] = dpre
        leave(1, j, blk).start()
        da2 += dot_nt(dpre, w_up(j))
        vup_o[j : j + 1] += jnp.sum(dpre.astype(F32), 0, keepdims=True)
    mixed_o[...] = mixed.astype(BF)
    dyf = dy.astype(F32)
    dz = da2 * g2
    m1 = jnp.sum(dz, -1, keepdims=True) * (1.0 / width)
    m2 = jnp.sum(dz * z2, -1, keepdims=True) * (1.0 / width)
    dx2 = dyf + r2 * (dz - m1 - z2 * m2)
    dx_o[...] = dx2
    vec_o[2:3, :] += jnp.sum(da2 * z2, 0, keepdims=True)
    vec_o[3:4, :] += jnp.sum(da2, 0, keepdims=True)
    vec_o[4:5, :] += jnp.sum(dyf, 0, keepdims=True)
    do = dx2.astype(BF)
    do_o[...] = do
    dattn = keep * dot_nt(do, w_out()).astype(BF).astype(F32)
    dnum = dattn * inv
    dden = -dnum * num_s[...] * inv
    low = lane_low(x.shape[0])
    for p in range(PAIRS):
        lanes = slice(128 * p, 128 * p + 128)
        mine = dnum[:, lanes]
        swap = pltpu.roll(dden[:, lanes], HEAD, 1)
        h = 2 * p
        grads_o[:, 128 * h : 128 * h + 128] = jnp.where(low, mine, swap).astype(BF)
        grads_o[:, 128 * h + 128 : 128 * h + 256] = jnp.where(low, swap, mine).astype(BF)

    def gather(c, rows, first):
        mask = cell_mask(bounds, c, first, 128)
        for h in range(HEADS):
            part = grads_o[rows, 128 * h : 128 * h + 128]
            part = jnp.where(mask, part.astype(F32), 0.0).astype(BF)
            acc[c, h] += dot_tn(part, pq[rows, FEATS * h : FEATS * (h + 1)])

    over_cells(bounds, blk, cells, x.shape[0], gather)

    @pl.when(blk == pl.num_programs(0) - 1)
    def _():
        store_sums(acc, sums_o, cells, True)
        full_out.wait()
        for j in range(wide):
            leave(0, j, blk).wait()
            leave(1, j, blk).wait()


def run_middle(bounds, x, dy, padding, pq, vec, b_up, sums, pieces, places, ff, cells):
    n, d = x.shape
    wide = HEADS * 128
    full = (cells, HEADS, 128, FEATS)
    scratch = [
        pltpu.VMEM(full, F32), pltpu.VMEM((WIDE_BLK, d), F32), pltpu.VMEM((WIDE_BLK, d), F32), pltpu.VMEM(full, BF),
        pltpu.VMEM((WIDE_BLK, ff), BF), pltpu.VMEM((WIDE_BLK, ff), BF), pltpu.SemaphoreType.DMA((3, ff // d)),
    ]
    if places:
        rows = max(hi for _, _, hi in places)
        chips = 1 + max(m for masks, _, _ in places for m in masks)
        number = 2 * sum(len(masks) for masks, _, _ in places)
        scratch += [pltpu.VMEM((chips, 2, rows, d), BF), pltpu.SemaphoreType.DMA((number,))]
    return pl.pallas_call(
        functools.partial(middle_kernel, cells, n, len(sums), places),
        grid=(n // WIDE_BLK,),
        in_specs=[
            SMEM, wide_spec(d), wide_spec(d), pl.BlockSpec((1, WIDE_BLK), lambda i: (0, i)), wide_spec(HEADS * FEATS), whole_spec(vec.shape), whole_spec(b_up.shape),
        ]
        + whole_specs(sums)
        + ([ANY] * len(pieces) if places else whole_specs(pieces)),
        out_specs=[
            wide_spec(d), HBM, HBM, wide_spec(d), wide_spec(d), wide_spec(d),
            wide_spec(d), wide_spec(wide), whole_spec((16, d)), whole_spec((8, d)),
            whole_spec(sums_shape(cells)), HBM,
        ],
        out_shape=[
            shape(n, d), shape(n, ff), shape(n, ff), shape(n, d), shape(n, d), shape(n, d),
            shape(n, d, kind=F32), shape(n, wide), shape(16, d, kind=F32), shape(8, d, kind=F32),
            shape(*sums_shape(cells)), shape(*full),
        ],
        scratch_shapes=scratch,
        compiler_params=params(),
        cost_estimate=cost(14, 30),
        name="middle",
    )(bounds, x, dy, padding, pq, vec, b_up, *sums, *pieces)


def phi_back(s, feats, rhs, low):
    r0 = dot_nt(feats[0].astype(BF), rhs[0])
    r1 = dot_nt(feats[1].astype(BF), rhs[1])
    total = pltpu.roll(jnp.where(low, r1, r0), HEAD, 1)
    return (jnp.where(low, r0, r1) - s * total) * SCALE


def query_back_kernel(cells, bounds, grads, pq, sq, full, bank, a1, dq_o, gq_o, sum_o, g_s, rhs):
    blk = pl.program_id(0)

    @pl.when(blk == 0)
    def _():
        back_parts(bank, rhs)
        gq_o[...] = jnp.zeros_like(gq_o)
        sum_o[...] = jnp.zeros_like(sum_o)

    low = lane_low(BLK)

    def one(c, rows, first):
        mask = cell_mask(bounds, c, first, FEATS)
        for h in range(HEADS):
            cols = slice(FEATS * h, FEATS * (h + 1))
            g = dot(grads[rows, 128 * h : 128 * h + 128], full[c, h])
            g_s[rows, cols] = jnp.where(mask, g, g_s[rows, cols])

    over_cells(bounds, blk, cells, BLK, one)
    for p in range(PAIRS):
        lanes = slice(128 * p, 128 * p + 128)
        feats = []
        for odd in (0, 1):
            cols = slice(FEATS * (2 * p + odd), FEATS * (2 * p + odd + 1))
            feats.append(g_s[:, cols] * pq[:, cols].astype(F32))
        dq_o[:, lanes] = phi_back(sq[:, lanes].astype(F32), feats, rhs, low).astype(BF)
    dq = dq_o[...]
    gq_o[...] += dot_tn(a1[...], dq)
    sum_o[0:1] += jnp.sum(dq.astype(F32), 0, keepdims=True)


def run_query_back(bounds, grads, pq, sq, full, bank, a1, cells):
    n, d = sq.shape
    return pl.pallas_call(
        functools.partial(query_back_kernel, cells),
        grid=(n // BLK,),
        in_specs=[
            SMEM, rows_spec(HEADS * 128), rows_spec(HEADS * FEATS), rows_spec(d),
            whole_spec(full.shape), whole_spec(bank.shape), rows_spec(d),
        ],
        out_specs=[rows_spec(d), whole_spec((d, d)), whole_spec((8, d))],
        out_shape=[shape(n, d), shape(d, d, kind=F32), shape(8, d, kind=F32)],
        scratch_shapes=[pltpu.VMEM((BLK, HEADS * FEATS), F32), pltpu.VMEM((2, 128, FEATS), BF)],
        compiler_params=params(),
        cost_estimate=cost(3, 8),
        name="query_back",
    )(bounds, grads, pq, sq, full, bank, a1)


def weight_kernel(rows, a2, dpre, gr, dy, ar, do, top_k, top_s, low_k, low_s, ar_s, do_s, sems):
    j = pl.program_id(0)
    last = pl.num_programs(0) - 1
    d = a2.shape[1]
    made = [pltpu.make_async_copy(src, dst, sems.at[i]) for i, (src, dst) in enumerate(((ar, ar_s), (do, do_s)))]

    def put(value, kept, sent):
        count, size = kept.shape[:2]
        mine, theirs = both_cores(value.reshape(count, 2, size, d))
        kept[...] = mine.astype(BF)
        sent[...] = theirs.astype(BF)

    @pl.when(j == 0)
    def _():
        for copy in made:
            copy.start()

    @pl.when(j < last)
    def _():
        put(dot_tn(a2[...], dpre[...]), top_k, top_s)
        put(dot_tn(gr[...], dy[...]), low_k, low_s)

    @pl.when(j == last)
    def _():
        for copy in made:
            copy.wait()
        put(dot_tn(ar_s[...], do_s[...]), top_k, top_s)


def run_weights(a2, dpre, gr, dy, ar, do, rows):
    n, d = a2.shape
    wide = dpre.shape[1] // d
    chips = d // (2 * rows)
    cols = pl.BlockSpec((n, d), lambda j: (0, jnp.minimum(j, wide - 1)))
    whole = whole_spec((n, d))
    top = pl.BlockSpec((chips, rows, d), lambda j: (0, j, 0))
    low = pl.BlockSpec((chips // wide, rows * wide, d), lambda j: (jnp.minimum(j, wide - 1), 0, 0))
    tops, lows = shape(chips, rows * (wide + 1), d), shape(chips, rows * wide, d)
    return pl.pallas_call(
        functools.partial(weight_kernel, rows),
        grid=(wide + 1,),
        in_specs=[whole, cols, cols, whole, HBM, HBM],
        out_specs=[top, top, low, low],
        out_shape=[tops, tops, lows, lows],
        scratch_shapes=[pltpu.VMEM((n, d), BF), pltpu.VMEM((n, d), BF), pltpu.SemaphoreType.DMA((2,))],
        compiler_params=params(),
        cost_estimate=cost(5, 20),
        name="weights",
    )(a2, dpre, gr, dy, ar, do)


def fold_kernel(parts, *refs):
    ins, outs, bufs, sems = refs[:4], refs[4 : 4 + parts], refs[4 + parts : 8 + parts], refs[8 + parts]
    me = lax.axis_index("dp")
    size = ins[0].shape[0] // parts
    made = []
    for k in range(parts):
        rows = pl.ds((me ^ k) * size, size)
        for i in range(4):
            made.append(pltpu.make_async_copy(ins[i].at[rows], bufs[i].at[k], sems.at[k, i]))
    for copy in made:
        copy.start()
    cut = ins[0].shape[1]
    for k in range(parts):
        for copy in made[4 * k : 4 * k + 4]:
            copy.wait()
        outs[k][:, :cut] = (bufs[0][k].astype(F32) + bufs[1][k].astype(F32)).astype(BF)
        outs[k][:, cut:] = (bufs[2][k].astype(F32) + bufs[3][k].astype(F32)).astype(BF)


def run_fold(top, top_got, low, low_got, parts):
    size, d = top.shape[0] // parts, top.shape[2]
    out = shape(size, top.shape[1] + low.shape[1], d)
    bufs = [pltpu.VMEM((parts, size) + v.shape[1:], BF) for v in (top, top_got, low, low_got)]
    return pl.pallas_call(
        functools.partial(fold_kernel, parts),
        in_specs=[HBM, ANY, HBM, ANY],
        out_specs=[VM] * parts,
        out_shape=[out] * parts,
        scratch_shapes=bufs + [pltpu.SemaphoreType.DMA((parts, 4))],
        compiler_params=pltpu.CompilerParams(vmem_limit_bytes=16 * 1024 * 1024),
        cost_estimate=cost(0.001, 7),
        name="fold",
    )(top, top_got, low, low_got)


def key_back_kernel(cells, slots, nsums, paired, rows, wide, bounds, a1, pk, vr, sk, gvec, vup, bank, w, gq, qsum, *refs):
    sums, refs = refs[:nsums], refs[nsums:]
    dk_o, dv_o, outs = refs[0], refs[1], refs[2 : 4 if paired else 3]
    full, g_s, v_s, rhs, gk_s, gv_s, sum_s, w_s, gq_s, sems = refs[4 if paired else 3 :]
    made = [pltpu.make_async_copy(a, b, sems.at[i]) for i, (a, b) in enumerate(((w, w_s), (gq, gq_s)))]
    blk = pl.program_id(0)
    d = a1.shape[1]

    @pl.when(blk == 0)
    def _():
        for copy in made:
            copy.start()
        gk_s[...] = jnp.zeros_like(gk_s)
        gv_s[...] = jnp.zeros_like(gv_s)
        sum_s[...] = qsum[...]
        back_parts(bank, rhs)
        load_sums(bounds, sums, full, slots, cells, True)

    low = lane_low(BLK)

    def one(c, rows, first):
        mask = cell_mask(bounds, c, first, FEATS)
        narrow = cell_mask(bounds, c, first, 128)
        low = lane_low(SUB)
        for p in range(PAIRS):
            lanes = slice(128 * p, 128 * p + 128)
            v = vr[rows, lanes].astype(F32)
            outs = []
            for odd in (0, 1):
                h = 2 * p + odd
                cols = slice(FEATS * h, FEATS * (h + 1))
                aug = (jnp.where(low, 1.0, v) if odd else jnp.where(low, v, 1.0)).astype(BF)
                g = dot(aug, full[c, h])
                g_s[rows, cols] = jnp.where(mask, g, g_s[rows, cols])
                outs.append(dot_nt(pk[rows, cols], full[c, h]))
            v_s[rows, lanes] = jnp.where(narrow, jnp.where(low, outs[0], outs[1]), v_s[rows, lanes])

    over_cells(bounds, blk, cells, BLK, one)
    for p in range(PAIRS):
        lanes = slice(128 * p, 128 * p + 128)
        feats = []
        for odd in (0, 1):
            cols = slice(FEATS * (2 * p + odd), FEATS * (2 * p + odd + 1))
            feats.append(g_s[:, cols] * pk[:, cols].astype(F32))
        dk_o[:, lanes] = phi_back(sk[:, lanes].astype(F32), feats, rhs, low).astype(BF)
    dk = dk_o[...]
    dv = v_s[...].astype(BF)
    dv_o[...] = dv
    gk_s[...] += dot_tn(a1[...], dk)
    gv_s[...] += dot_tn(a1[...], dv)
    sum_s[1:2] += jnp.sum(dk.astype(F32), 0, keepdims=True)
    sum_s[2:3] += jnp.sum(dv.astype(F32), 0, keepdims=True)

    @pl.when(blk == pl.num_programs(0) - 1)
    def _():
        for copy in made:
            copy.wait()
        gain = w_s[:, 3 * d : 3 * d + 1].astype(F32)
        shift = w_s[:, 3 * d + 1 : 3 * d + 2].astype(F32)
        total = jnp.zeros((d, 1), F32)
        plain = jnp.zeros((d, 1), F32)

        def put(lo, value):
            cols = slice(lo, lo + value.shape[1])
            if paired:
                kept, sent = both_cores(value.reshape(outs[0].shape[0], 2, rows, value.shape[1]))
                outs[0][:, :, cols] = kept.astype(BF)
                outs[1][:, :, cols] = sent.astype(BF)
            else:
                outs[0][:, cols] = value.astype(BF)

        for i, grad in enumerate((gq_s, gk_s, gv_s)):
            weight = w_s[:, i * d : (i + 1) * d].astype(F32)
            line = sum_s[i : i + 1]
            total += jnp.sum(weight * grad[...], -1, keepdims=True)
            plain += jnp.sum(weight * line, -1, keepdims=True)
            put(i * d, grad[...])
        lines = [gvec[i : i + 1] for i in range(5)] + by_owner(vup[...], rows, wide)
        vt = pad_rows(lines, 128).T
        lane = lax.broadcasted_iota(jnp.int32, vt.shape, 1)
        vt = jnp.where(lane == 0, (total - shift * plain) / gain, jnp.where(lane == 1, plain, vt))
        put(3 * d, vt)


def run_key_back(bounds, a1, pk, vr, sk, gvec, vup, bank, w, gq, qsum, sums, rows, wide, paired, cells):
    n, d = a1.shape
    total = w.shape[1]
    gout = [(d // (2 * rows), rows, total)] * 2 if paired else [(d, total)]
    square = pltpu.VMEM((d, d), F32)
    return pl.pallas_call(
        functools.partial(key_back_kernel, cells, n, len(sums), paired, rows, wide),
        grid=(n // BLK,),
        in_specs=[SMEM, rows_spec(d), rows_spec(HEADS * FEATS), rows_spec(d), rows_spec(d)]
        + whole_specs((gvec, vup, bank)) + [HBM, HBM] + whole_specs((qsum,))
        + whole_specs(sums),
        out_specs=[rows_spec(d), rows_spec(d)] + [whole_spec(g) for g in gout],
        out_shape=[shape(n, d), shape(n, d)] + [shape(*g) for g in gout],
        scratch_shapes=[
            pltpu.VMEM((cells, HEADS, 128, FEATS), BF),
            pltpu.VMEM((BLK, HEADS * FEATS), F32),
            pltpu.VMEM((BLK, d), F32),
            pltpu.VMEM((2, 128, FEATS), BF),
            square,
            square,
            pltpu.VMEM((8, d), F32),
            pltpu.VMEM(w.shape, BF),
            square,
            pltpu.SemaphoreType.DMA((2,)),
        ],
        compiler_params=params(),
        cost_estimate=cost(6, 14),
        name="key_back",
    )(bounds, a1, pk, vr, sk, gvec, vup, bank, w, gq, qsum, *sums)


def token_back_kernel(x, dq, dk, dv, dx, vec, w, gt_o):
    d = x.shape[1]
    da1 = dot_nt(dq[...], w[:, :d]) + dot_nt(dk[...], w[:, d : 2 * d]) + dot_nt(dv[...], w[:, 2 * d : 3 * d])
    z, r = norm_stats(x[...].astype(F32))
    dz = da1 * vec[0:1]
    m1 = jnp.sum(dz, -1, keepdims=True) * (1.0 / d)
    m2 = jnp.sum(dz * z, -1, keepdims=True) * (1.0 / d)
    gt_o[...] = dx[...] + r * (dz - m1 - z * m2)


def run_token_back(x, dq, dk, dv, dx, vec, w):
    n, d = x.shape
    return pl.pallas_call(
        token_back_kernel,
        grid=(n // WIDE_BLK,),
        in_specs=[wide_spec(d)] * 5 + whole_specs((vec, w)),
        out_specs=wide_spec(d),
        out_shape=shape(n, d, kind=F32),
        compiler_params=params(),
        cost_estimate=cost(2, 8),
        name="token_back",
    )(x, dq, dk, dv, dx, vec, w)


AXES = ("dp", "fsdp")
Z_ALL = (0, 1, 2, 3)
LEAD_MASKS = (Z_ALL, (4, 5, 6, 7), (8, 9, 10, 11), (12, 13, 14, 15))


def flip(x, axis, size, mask):
    return lax.ppermute(x, axis, [(i, i ^ mask) for i in range(size)])


def to_core(x, fsdp):
    return flip(x, "fsdp", fsdp, 1)


def to_z(x, fsdp, mask):
    return flip(x, "fsdp", fsdp, 2 * mask)


def tie(*values):
    return lax.optimization_barrier(values)


def same_core_groups(dp, fsdp):
    return [[d * fsdp + 2 * z + c for d in range(dp) for z in range(fsdp // 2)] for c in range(2)]


def chip_groups(fsdp):
    return [[2 * z + c for z in range(fsdp // 2)] for c in range(2)]


def pack_kernel(wide, w_qkv, g1, s1, w_out, g2, s2, w_up, b_up, w_down, b_down, lead, body):
    rows = w_qkv.shape[0]
    d = w_out.shape[1]
    total = w_qkv.shape[1]
    place = lax.broadcasted_iota(jnp.int32, (128, rows), 0)
    up = b_up[...].astype(F32).reshape(1, -1)
    lines = [v[...].astype(F32).reshape(1, -1) for v in (g1, s1, g2, s2, b_down)]
    lines += [up[:, j * rows : (j + 1) * rows] for j in range(wide)]
    table = jnp.zeros((128, rows), F32)
    for i, line in enumerate(lines):
        table = jnp.where(place == i, line, table)
    across = lax.broadcasted_iota(jnp.int32, (rows, rows), 0) == lax.broadcasted_iota(jnp.int32, (rows, rows), 1)
    lead[:, :total] = w_qkv[...]
    lead[:, total:] = dot_nt(jnp.where(across, 1.0, 0.0).astype(BF), table.astype(BF)).astype(BF)
    body[:rows] = w_out[...]
    for j in range(wide):
        body[rows * (1 + j) : rows * (2 + j)] = w_up[:, j * d : (j + 1) * d]
    body[rows * (1 + wide) :] = w_down[...]


def final_kernel(rows, wide, count, *refs):
    parts, outs = refs[:count], refs[2 * count :]
    wout, wup, wdown, wqkv, *lines = outs
    d = wout.shape[1]
    add = lambda refs: functools.reduce(lambda a, b: a + b, [v[...].astype(F32) for v in refs])
    total = add(refs[count : 2 * count])
    for j in range(wide):
        wup[:, j * d : (j + 1) * d] = total[rows * j : rows * (j + 1)]
    wout[...] = total[rows * wide : rows * (1 + wide)]
    wdown[...] = total[rows * (1 + wide) :]
    total = add(parts)
    cols = wqkv.shape[1]
    wqkv[...] = total[:, :cols]
    table = total[:, cols:].T
    for i in range(5):
        lines[i][...] = table[i]
    lines[5][...] = jnp.concatenate([table[5 + j : 6 + j] for j in range(wide)], 1)[0]


def run_final(lead_parts, body_parts, rows, wide):
    d = body_parts[0].shape[1]
    return pl.pallas_call(
        functools.partial(final_kernel, rows, wide, len(lead_parts)),
        in_specs=[VM] * (2 * len(lead_parts)),
        out_specs=[VM] * 10,
        out_shape=[
            shape(rows, d, kind=F32), shape(rows, wide * d, kind=F32), shape(rows * wide, d, kind=F32),
            shape(rows, 3 * d, kind=F32),
        ]
        + [shape(rows, kind=F32)] * 5
        + [shape(rows * wide, kind=F32)],
        name="final",
    )(*lead_parts, *body_parts)


def local(dp, fsdp, tokens, bounds, padding, bank, ln1_gain, ln1_bias, w_qkv, w_out, ln2_gain, ln2_bias,
          w_up, b_up, w_down, b_down, cotangent):
    ndev = dp * fsdp
    x = tokens[0]
    dy = cotangent[0]
    n, d = x.shape
    ff = w_up.shape[1]
    cells = bounds.shape[1] - 1
    chips = fsdp // 2
    rows = d // ndev
    wide = ff // d
    frow = ff // ndev
    paired = dp == 4 and fsdp == 8

    shards = (w_qkv, ln1_gain, ln1_bias, w_out, ln2_gain, ln2_bias, w_up, b_up, w_down, b_down)
    if paired:
        lead, body = pl.pallas_call(
            functools.partial(pack_kernel, wide),
            in_specs=[VM] * len(shards),
            out_specs=[VM, VM],
            out_shape=[shape(rows, 3 * d + 128), shape(rows * (1 + wide) + frow, d)],
            name="pack",
        )(*shards)
    else:
        vecs = jnp.concatenate([ln1_gain, ln1_bias, ln2_gain, ln2_bias, b_down, b_up]).reshape(5 + wide, rows)
        lead = jnp.concatenate([w_qkv, jnp.pad(vecs, ((0, 128 - 5 - wide), (0, 0))).T], 1)
        body = jnp.concatenate([w_out] + [w_up[:, j * d : (j + 1) * d] for j in range(wide)] + [w_down], 0)
    cut = rows * (1 + wide)

    if paired:
        first = jnp.stack([lead] + [to_z(lead, fsdp, k) for k in (1, 2, 3)])
        lead_own = [first] + [flip(first, "dp", dp, k) for k in (1, 2, 3)]
        pair = jnp.stack([body, to_z(body, fsdp, 1)])
        pair, *lead_own = tie(pair, *lead_own)
        lead_pieces = lead_own + [to_core(v, fsdp) for v in lead_own]
        four = jnp.concatenate([pair, to_z(pair, fsdp, 2)])
        lead_places = tuple((m, 0, rows) for m in LEAD_MASKS)
    else:
        lead_pieces = [lax.all_gather(lead, AXES, axis=0, tiled=True)]
        parts = lax.all_gather(body, AXES, axis=0)
        take = lambda lo, size: parts[:, lo : lo + size].reshape(ndev * size, d)
        body_pieces = [
            take(0, rows), jnp.concatenate([take((1 + j) * rows, rows) for j in range(wide)], 1), take(cut, frow),
        ]
        lead_places = body_places = None

    def far_sums(out):
        return lax.all_to_all(out, "fsdp", 0, 0, axis_index_groups=chip_groups(fsdp), tiled=True)

    a1, sk, pk, vr, sums, vec, *w = run_keys(bounds, x, padding, bank, lead_pieces, lead_places, cells)
    w = w[0].reshape(d, -1) if paired else lead_pieces[0]
    if paired:
        sums, four = tie(sums, four)
        sums = [sums, to_core(sums, fsdp)]
        out = run_spread(bounds, *sums, chips, n, cells)
        a1_q, out = tie(a1, out)
        far = far_sums(out)
        up, down = four[:, :cut], four[:, cut:]
        up_x, down_y = flip(up, "dp", dp, 1), flip(down, "dp", dp, 2)
        up_y = flip(jnp.concatenate([up, up_x]), "dp", dp, 2)
        down_x = flip(jnp.concatenate([down, down_y]), "dp", dp, 1)
        sq, pq, up_line = run_queries(a1_q, w, bank, vec, rows, wide)
        early = [to_core(v, fsdp) for v in (four, up_x, down_y)]
        up_y, down_x, pq, up_line, *early = tie(up_y, down_x, pq, up_line, *early)
        body_pieces = [four, up_x, down_y, up_y, down_x] + early + [to_core(v, fsdp) for v in (up_y, down_x)]
        body_places = (
            (Z_ALL, 0, cut + frow), ((4, 5, 6, 7), 0, cut), ((8, 9, 10, 11), cut, cut + frow),
            ((8, 9, 10, 11, 12, 13, 14, 15), 0, cut), ((4, 5, 6, 7, 12, 13, 14, 15), cut, cut + frow),
        )
        sums = sums + [far, to_core(far, fsdp)]
    else:
        sums = [lax.psum(sums, "fsdp")]
        sq, pq, up_line = run_queries(a1, w, bank, vec, rows, wide)
    mixed, gr, dpre, a2, ar, do, dx2, grads, gvec, vup, sums, full = run_middle(
        bounds, x, dy, padding, pq, vec, up_line, sums, body_pieces, body_places, ff, cells
    )
    back = lambda gq, qsum, sums: run_key_back(
        bounds, a1, pk, vr, sk, gvec, vup, bank, w, gq, qsum, sums, rows, wide, paired, cells
    )
    if paired:
        top, top_sent, low, low_sent = run_weights(a2, dpre, gr, dy, ar, do, rows)
        got, top_sent, low_sent = tie(to_core(sums, fsdp), top_sent, low_sent)
        sums = [sums, got]
        out = run_spread(bounds, *sums, chips, n, cells)
        far = far_sums(out)
        plus = lambda *parts: functools.reduce(lambda a, b: a + b, [v.astype(F32) for v in parts]).astype(BF)
        pick = lambda value, at, dim: lax.dynamic_index_in_dim(value, at, dim, keepdims=False)
        folded = run_fold(top, to_core(top_sent, fsdp), low, to_core(low_sent, fsdp), dp)
        grads, *folded = tie(grads, *folded)
        spread = [flip(v, "dp", dp, k) for k, v in enumerate(folded) if k]
        dq, gq, qsum = run_query_back(bounds, grads, pq, sq, full, bank, a1, cells)
        far, gq, qsum = tie(far, gq, qsum)
        dk, dv, kept, sent = back(gq, qsum, sums + [far, to_core(far, fsdp)])
        kept, sent, *spread = tie(kept, sent, *spread)
        whole = plus(folded[0], *spread)
        zpos = lax.axis_index("fsdp") // 2
        parts = [pick(whole, zpos, 0)] + [to_z(pick(whole, zpos ^ k, 0), fsdp, k) for k in (1, 2, 3)]
        half = plus(kept, to_core(sent, fsdp)).reshape((dp, chips) + kept.shape[1:])
        dpos = lax.axis_index("dp")
        half = plus(pick(half, dpos, 0), *[flip(pick(half, dpos ^ k, 0), "dp", dp, k) for k in (1, 2, 3)])
        lead_parts = [pick(half, zpos, 0)] + [to_z(pick(half, zpos ^ k, 0), fsdp, k) for k in (1, 2, 3)]
        wout, wup, wdown, wqkv, *vecs = run_final(lead_parts, parts, rows, wide)
    else:
        dq, gq, qsum = run_query_back(bounds, grads, pq, sq, full, bank, a1, cells)
        dk, dv, glead = back(gq, qsum, [lax.psum(sums, "fsdp")])
        gup = dot_tn(a2, dpre)
        blocks = lambda g, size: g.reshape(ndev, size, d)
        gbody = jnp.concatenate(
            [blocks(dot_tn(ar, do), rows)]
            + [blocks(gup[:, j * d : (j + 1) * d], rows) for j in range(wide)]
            + [blocks(dot_tn(gr, dy), frow)], 1
        )
        gbody = lax.psum_scatter(gbody, AXES, scatter_dimension=0, tiled=True)[0]
        glead = lax.psum_scatter(glead.astype(F32), AXES, scatter_dimension=0, tiled=True)
        gvec = glead[:, 3 * d :].T
        vecs = [gvec[i] for i in range(5)] + [gvec[5 : 5 + wide].reshape(-1)]
        wqkv, wout, wdown = glead[:, : 3 * d], gbody[:rows], gbody[cut:]
        wup = jnp.concatenate([gbody[(1 + j) * rows : (2 + j) * rows] for j in range(wide)], 1)
    gt = run_token_back(x, dq, dk, dv, dx2, vec, w)
    return (
        mixed[None], gt[None], vecs[0], vecs[1], wqkv, wout, vecs[2], vecs[3], wup, vecs[5], wdown, vecs[4],
    )


def solution(mesh):
    both = P(("dp", "fsdp"))
    mat = P(("dp", "fsdp"), None)
    act = P("dp", "fsdp", None)
    return jax.shard_map(
        functools.partial(local, mesh.shape["dp"], mesh.shape["fsdp"]),
        mesh=mesh,
        in_specs=(act, P("dp", None), P("dp", "fsdp"), P(), both, both, mat, mat, both, both, mat, both, mat, both, act),
        out_specs=(act, act, both, both, mat, mat, both, both, mat, both, mat, both),
        check_vma=False,
    )
```

```python
import functools
import math

import jax
import jax.numpy as jnp
from jax import lax
from jax.experimental import pallas as pl
from jax.experimental.pallas import tpu as pltpu
from jax.sharding import PartitionSpec as P

HEADS = 8
FEATS = 256
HEAD = 64
PAIRS = HEADS // 2
SCALE = HEAD ** (-0.25)
LOGF = 0.5 * math.log(FEATS)
BLK = 256
WIDE_BLK = 512
SUB = 256
KVROWS = 272
BF = jnp.bfloat16
F32 = jnp.float32
VMEM_LIMIT = 56 * 1024 * 1024


def dot(a, b):
    return jnp.dot(a, b, preferred_element_type=F32)


def dot_nt(a, b):
    return lax.dot_general(a, b, (((1,), (1,)), ((), ())), preferred_element_type=F32)


def dot_tn(a, b):
    return lax.dot_general(a, b, (((0,), (0,)), ((), ())), preferred_element_type=F32)


def norm_stats(x):
    width = x.shape[-1]
    c = x - jnp.sum(x, -1, keepdims=True) * (1.0 / width)
    r = lax.rsqrt(jnp.sum(c * c, -1, keepdims=True) * (1.0 / width) + 1e-05)
    return c * r, r


def lane_low(n):
    return lax.broadcasted_iota(jnp.int32, (n, 128), 1) < HEAD


def phi_pair(u, rhs_main, rhs_rest):
    low = lane_low(u.shape[0])
    s = u * SCALE
    hi = s.astype(BF)
    lo = (s - hi.astype(F32)).astype(BF)
    both = jnp.concatenate([hi, lo], 1)
    s2 = s * s
    feats = []
    for odd in (0, 1):
        lifted = dot(both, rhs_main[odd]) + dot(hi, rhs_rest[odd])
        half = jnp.sum(jnp.where(low, 0.0, s2) if odd else jnp.where(low, s2, 0.0), -1, keepdims=True)
        feats.append(jnp.exp(lifted - (0.5 * half + LOGF)))
    return s, feats


def over_cells(bounds, blk, cells, block, body):
    for sub in range(block // SUB):
        first = lax.axis_index("fsdp") * (pl.num_programs(0) * block) + blk * block + sub * SUB
        rows = slice(sub * SUB, (sub + 1) * SUB)

        def one(c, carry):
            body(c, rows, first)
            return carry

        lax.fori_loop(cell_at(bounds, first, cells), cell_at(bounds, first + SUB - 1, cells) + 1, one, 0)


def cell_at(bounds, slot, cells):
    cell = jnp.int32(0)
    for c in range(1, cells):
        cell += (bounds[0, c] <= slot).astype(jnp.int32)
    return cell


def cell_mask(bounds, c, first, cols):
    place = lax.broadcasted_iota(jnp.int32, (SUB, cols), 0) + first
    return (place >= bounds[0, c]) & (place < bounds[0, c + 1])


def store_sums(acc, out, cells, summed):
    rows = lax.broadcasted_iota(jnp.int32, (16, FEATS), 0)
    for half in (0, 1):
        for c in range(cells):
            tail = jnp.zeros((16, FEATS), F32)
            for i in range(PAIRS):
                part = acc[c, half * PAIRS + i]
                body, rest = (part[HEAD:], part[:HEAD]) if i % 2 else (part[:HEAD], part[HEAD:])
                out[half, c, i * HEAD : (i + 1) * HEAD, :] = body.astype(BF)
                line = jnp.sum(rest, 0, keepdims=True) if summed else rest[0:1]
                tail = jnp.where(rows == i, line, tail)
            out[half, c, PAIRS * HEAD :, :] = tail.astype(BF)


def load_sums(bounds, sums, full, slots, cells, single):
    rows = lax.broadcasted_iota(jnp.int32, (HEAD, FEATS), 0)
    spot = lax.axis_index("fsdp")
    if len(sums) > 1:
        own, got, far_own, far_other = sums
        core = spot % 2
        start = (spot // 2) * (2 * slots)
        first, last = cell_at(bounds, start, cells), cell_at(bounds, start + 2 * slots - 1, cells)
    for slot in (0, 1):
        if len(sums) > 1:
            half = core ^ slot
            far = far_other if slot else far_own
            before = jnp.zeros(far.shape[1:], F32)
            after = jnp.zeros(far.shape[1:], F32)
            for z in range(far.shape[0]):
                part = far[z].astype(F32)
                before += jnp.where(z < spot // 2, part, 0.0)
                after += jnp.where(z > spot // 2, part, 0.0)
        else:
            half = slot
        for c in range(cells):
            if len(sums) > 1:
                total = own[half, c].astype(F32) + got[half, c].astype(F32)
                total += jnp.where(first == c, before, 0.0) + jnp.where(last == c, after, 0.0)
            else:
                total = sums[0][half, c].astype(F32)
            for i in range(PAIRS):
                body = total[i * HEAD : (i + 1) * HEAD].astype(BF)
                line = jnp.broadcast_to(total[PAIRS * HEAD + i : PAIRS * HEAD + i + 1], (HEAD, FEATS))
                if single:
                    line = jnp.where(rows == 0, line, 0.0)
                line = line.astype(BF)
                h = half * PAIRS + i
                full[c, h, :HEAD, :] = line if i % 2 else body
                full[c, h, HEAD:, :] = body if i % 2 else line


def keep_lanes(pad):
    return jnp.broadcast_to(pad[...].astype(F32), (128, pad.shape[1])).T


def feature_parts(bank, main, rest):
    w = bank[...]
    hi = w.astype(BF)
    lo = (w - hi.astype(F32)).astype(BF)
    none = jnp.zeros_like(hi)
    main[0] = jnp.concatenate([hi, none, hi, none], 0)
    main[1] = jnp.concatenate([none, hi, none, hi], 0)
    rest[0] = jnp.concatenate([lo, none], 0)
    rest[1] = jnp.concatenate([none, lo], 0)


def back_parts(bank, rhs):
    hi = bank[...].astype(BF)
    ones = jnp.ones_like(hi)
    rhs[0] = jnp.concatenate([hi, ones], 0)
    rhs[1] = jnp.concatenate([ones, hi], 0)


FEATURE_SCRATCH = [pltpu.VMEM((2, 4 * HEAD, FEATS), BF), pltpu.VMEM((2, 2 * HEAD, FEATS), BF)]


def copies(pieces, places, target, sems):
    spot = lax.axis_index("fsdp")
    core = spot % 2
    chip = lax.axis_index("dp") * (target.shape[0] // lax.axis_size("dp")) + spot // 2
    made = []
    for i, (masks, lo, hi) in enumerate(places):
        for side in (0, 1):
            src = pieces[i + side * len(places)]
            for k, mask in enumerate(masks):
                dst = target.at[chip ^ mask, core ^ side, lo:hi]
                made.append(pltpu.make_async_copy(src.at[k], dst, sems.at[len(made)]))
    return made


def both_cores(value):
    mine = lax.axis_index("fsdp") % 2 == 0
    a, b = value[:, 0], value[:, 1]
    return jnp.where(mine, a, b), jnp.where(mine, b, a)


def columns(ref, lo, hi):
    value = ref[..., lo:hi]
    return value.reshape(-1, value.shape[-1])


def key_kernel(cells, places, bounds, x, pad, bank, *refs):
    count = 2 * len(places) if places else 1
    pieces, (a1_o, sk_o, pk_o, vr_o, sums_o, vec_o), refs = refs[:count], refs[count : count + 6], refs[count + 6 :]
    if places:
        w_o, acc, rm, rr, w, sems, out_sem = refs
        leave = pltpu.make_async_copy(w, w_o, out_sem)
    else:
        w = pieces[0]
        acc, rm, rr = refs
    blk = pl.program_id(0)
    d = x.shape[1]

    @pl.when(blk == 0)
    def _():
        if places:
            made = copies(pieces, places, w, sems)
            for copy in made:
                copy.start()
        acc[...] = jnp.zeros_like(acc)
        feature_parts(bank, rm, rr)
        if places:
            for copy in made:
                copy.wait()
            leave.start()
        vec_o[...] = columns(w, 3 * d, 3 * d + 128).astype(F32).T[:16]

    keep = keep_lanes(pad)
    keep = jnp.concatenate([keep, keep], 1)
    z, _ = norm_stats(x[...].astype(F32))
    a1 = (z * vec_o[0:1] + vec_o[1:2]).astype(BF)
    a1_o[...] = a1
    keys = dot(a1, columns(w, d, 2 * d))
    vr_o[...] = dot(a1, columns(w, 2 * d, 3 * d)).astype(BF)
    for p in range(PAIRS):
        s, feats = phi_pair(keys[:, 128 * p : 128 * p + 128], rm, rr)
        sk_o[:, 128 * p : 128 * p + 128] = s.astype(BF)
        for odd in (0, 1):
            h = 2 * p + odd
            pk_o[:, FEATS * h : FEATS * (h + 1)] = (keep * feats[odd]).astype(BF)
    low = lane_low(SUB)

    def one(c, rows, first):
        mask = cell_mask(bounds, c, first, 128)
        for p in range(PAIRS):
            v = vr_o[rows, 128 * p : 128 * p + 128].astype(F32)
            for odd in (0, 1):
                h = 2 * p + odd
                aug = jnp.where(low, 1.0, v) if odd else jnp.where(low, v, 1.0)
                aug = jnp.where(mask, aug, 0.0).astype(BF)
                acc[c, h] += dot_tn(aug, pk_o[rows, FEATS * h : FEATS * (h + 1)])

    over_cells(bounds, blk, cells, BLK, one)

    @pl.when(blk == pl.num_programs(0) - 1)
    def _():
        store_sums(acc, sums_o, cells, False)
        if places:
            leave.wait()


PAD = pl.BlockSpec((1, BLK), lambda i: (0, i))


def rows_spec(cols):
    return pl.BlockSpec((BLK, cols), lambda i: (i, 0))


def wide_spec(cols):
    return pl.BlockSpec((WIDE_BLK, cols), lambda i: (i, 0))


def whole_spec(shape):
    return pl.BlockSpec(shape, lambda i: (0,) * len(shape))


def whole_specs(arrays):
    return [whole_spec(v.shape) for v in arrays]


SMEM = pl.BlockSpec(memory_space=pltpu.SMEM)
ANY = pl.BlockSpec(memory_space=pl.ANY)
HBM = pl.BlockSpec(memory_space=pltpu.HBM)
VM = pl.BlockSpec(memory_space=pltpu.VMEM)


def params(limit=VMEM_LIMIT):
    return pltpu.CompilerParams(vmem_limit_bytes=limit, dimension_semantics=("arbitrary",))


def cost(gflop, mb):
    return pl.CostEstimate(flops=int(gflop * 1e3), bytes_accessed=int(mb * 1e3), transcendentals=0)


def sums_shape(cells):
    return (2, cells, KVROWS, FEATS)


def shape(*dims, kind=BF):
    return jax.ShapeDtypeStruct(dims, kind)


def run_keys(bounds, x, padding, bank, pieces, places, cells):
    n, d = x.shape
    out_specs = [
        rows_spec(d), rows_spec(d), rows_spec(HEADS * FEATS), rows_spec(d), whole_spec(sums_shape(cells)), whole_spec((16, d)),
    ]
    out_shape = [
        shape(n, d), shape(n, d), shape(n, HEADS * FEATS), shape(n, d), shape(*sums_shape(cells)), shape(16, d, kind=F32),
    ]
    scratch = [pltpu.VMEM((cells, HEADS, 128, FEATS), F32)] + FEATURE_SCRATCH
    if places:
        piece = pieces[0].shape
        w = (d // (2 * piece[1]), 2) + piece[1:]
        out_specs.append(HBM)
        out_shape.append(shape(*w))
        scratch += [pltpu.VMEM(w, BF), pltpu.SemaphoreType.DMA((d // piece[1],)), pltpu.SemaphoreType.DMA]
    return pl.pallas_call(
        functools.partial(key_kernel, cells, places),
        grid=(n // BLK,),
        in_specs=[SMEM, rows_spec(d), PAD, whole_spec(bank.shape)]
        + ([ANY] * len(pieces) if places else whole_specs(pieces)),
        out_specs=out_specs,
        out_shape=out_shape,
        scratch_shapes=scratch,
        compiler_params=params(),
        cost_estimate=cost(8, 10),
        name="keys",
    )(bounds, x, padding, bank, *pieces)


def shuffle(j, rows, wide, d):
    a = lax.broadcasted_iota(jnp.int32, (d, d // wide), 0)
    b = lax.broadcasted_iota(jnp.int32, (d, d // wide), 1)
    hit = (a // (rows * wide) == b // rows) & (a % (rows * wide) == rows * j + b % rows)
    return jnp.where(hit, 1.0, 0.0).astype(BF)


def pad_rows(lines, count):
    return jnp.concatenate(lines + [jnp.zeros((count - len(lines), lines[0].shape[1]), lines[0].dtype)], 0)


def in_order(table, rows, wide):
    d = table.shape[1]
    part = d // wide
    total = jnp.zeros((8, d), F32)
    for j in range(wide):
        lines = pad_rows([table[5 + j : 6 + j, part * k : part * (k + 1)] for k in range(wide)], 8)
        total += dot_nt(lines.astype(BF), shuffle(j, rows, wide, d))
    return total


def by_owner(lines, rows, wide):
    d = lines.shape[1]
    out = []
    for j in range(wide):
        got = dot(lines.astype(BF), shuffle(j, rows, wide, d))
        out.append(jnp.concatenate([got[k : k + 1] for k in range(wide)], 1))
    return out


def query_kernel(rows, wide, a1, wq, bank, vec, sq_o, pq_o, up_o, rm, rr):
    @pl.when(pl.program_id(0) == 0)
    def _():
        feature_parts(bank, rm, rr)
        up_o[...] = in_order(vec[...], rows, wide)

    q = dot(a1[...], wq[...])
    for p in range(PAIRS):
        s, feats = phi_pair(q[:, 128 * p : 128 * p + 128], rm, rr)
        sq_o[:, 128 * p : 128 * p + 128] = s.astype(BF)
        for odd in (0, 1):
            h = 2 * p + odd
            pq_o[:, FEATS * h : FEATS * (h + 1)] = feats[odd].astype(BF)


def run_queries(a1, w, bank, vec, rows, wide):
    n, d = a1.shape
    return pl.pallas_call(
        functools.partial(query_kernel, rows, wide),
        grid=(n // BLK,),
        in_specs=[rows_spec(d), whole_spec((d, d)), whole_spec(bank.shape), whole_spec(vec.shape)],
        out_specs=[rows_spec(d), rows_spec(HEADS * FEATS), whole_spec((8, d))],
        out_shape=[shape(n, d), shape(n, HEADS * FEATS), shape(8, d, kind=F32)],
        scratch_shapes=FEATURE_SCRATCH,
        compiler_params=params(),
        cost_estimate=cost(5, 7),
        name="queries",
    )(a1, w, bank, vec)


def spread_kernel(cells, slots, bounds, own, got, out, mine, theirs, sems):
    spot = lax.axis_index("fsdp")
    core = spot % 2
    made = []
    for z in range(out.shape[0]):
        c = cell_at(bounds, z * (2 * slots) + jnp.where(z > spot // 2, 0, 2 * slots - 1), cells)
        made.append(pltpu.make_async_copy(own.at[core, c], mine.at[z], sems.at[0, z]))
        made.append(pltpu.make_async_copy(got.at[core, c], theirs.at[z], sems.at[1, z]))
    for copy in made:
        copy.start()
    for z in range(out.shape[0]):
        made[2 * z].wait()
        made[2 * z + 1].wait()
        out[z] = (mine[z].astype(F32) + theirs[z].astype(F32)).astype(BF)


def run_spread(bounds, own, got, chips, slots, cells):
    part = pltpu.VMEM((chips, KVROWS, FEATS), BF)
    return pl.pallas_call(
        functools.partial(spread_kernel, cells, slots),
        in_specs=[SMEM, HBM, ANY],
        out_specs=VM,
        out_shape=shape(chips, KVROWS, FEATS),
        scratch_shapes=[part, part, pltpu.SemaphoreType.DMA((2, chips))],
        compiler_params=pltpu.CompilerParams(vmem_limit_bytes=4 * 1024 * 1024),
        cost_estimate=cost(0.001, 2),
        name="spread",
    )(bounds, own, got)


def middle_kernel(cells, slots, nsums, places, bounds, x, dy_r, pad, pq, vec, b_up, *refs):
    sums, refs = refs[:nsums], refs[nsums:]
    count = 2 * len(places) if places else 3
    pieces, refs = refs[:count], refs[count:]
    mixed_o, gr_o, dpre_o, a2_o, ar_o, do_o, dx_o, grads_o, vec_o, vup_o, sums_o, full_o = refs[:12]
    acc, num_s, den_s, full, gr_s, dpre_s, out_sems = refs[12:19]
    blk = pl.program_id(0)
    width = x.shape[1]
    wide = gr_o.shape[1] // width
    if places:
        w, sems = refs[19:]
        rows = width // (2 * w.shape[0])
        base = rows * (1 + wide)
        w_out = lambda: w[:, :, 0:rows, :].reshape(width, width)
        w_up = lambda j: w[:, :, rows * (1 + j) : rows * (2 + j), :].reshape(width, width)
        w_down = lambda j: w[j * (w.shape[0] // wide) : (j + 1) * (w.shape[0] // wide), :, base:, :].reshape(width, width)
    else:
        w_out = lambda: pieces[0][...]
        w_up = lambda j: pieces[1][:, j * width : (j + 1) * width]
        w_down = lambda j: pieces[2][j * width : (j + 1) * width, :]

    full_out = pltpu.make_async_copy(full, full_o, out_sems.at[2, 0])
    size = x.shape[0]

    def leave(i, j, at):
        src, dst = ((gr_s, gr_o), (dpre_s, dpre_o))[i]
        cols = slice(j * width, (j + 1) * width)
        rows = pl.ds(pl.multiple_of(at * size, size), size)
        return pltpu.make_async_copy(src.at[:, cols], dst.at[rows, cols], out_sems.at[i, j])

    @pl.when(blk == 0)
    def _():
        if places:
            for copy in copies(pieces, places, w, sems):
                copy.start()
        acc[...] = jnp.zeros_like(acc)
        vec_o[...] = jnp.zeros_like(vec_o)
        vup_o[...] = jnp.zeros_like(vup_o)
        load_sums(bounds, sums, full, slots, cells, False)
        full_out.start()

    @pl.when(blk > 0)
    def _():
        for j in range(wide):
            leave(0, j, blk - 1).wait()
            leave(1, j, blk - 1).wait()

    low = lane_low(SUB)

    def attend(c, rows, first):
        mask = cell_mask(bounds, c, first, 128)
        for p in range(PAIRS):
            h = 2 * p
            lanes = slice(128 * p, 128 * p + 128)
            r0 = dot_nt(pq[rows, FEATS * h : FEATS * (h + 1)], full[c, h])
            r1 = dot_nt(pq[rows, FEATS * (h + 1) : FEATS * (h + 2)], full[c, h + 1])
            num = jnp.where(low, r0, r1)
            den = pltpu.roll(jnp.where(low, r1, r0), HEAD, 1)
            num_s[rows, lanes] = jnp.where(mask, num, num_s[rows, lanes])
            den_s[rows, lanes] = jnp.where(mask, den, den_s[rows, lanes])

    over_cells(bounds, blk, cells, x.shape[0], attend)
    if places:
        @pl.when(blk == 0)
        def _():
            for copy in copies(pieces, places, w, sems):
                copy.wait()

    keep = keep_lanes(pad)
    keep = jnp.concatenate([keep] * (width // 128), 1)
    inv = 1.0 / den_s[...]
    ar = (keep * num_s[...] * inv).astype(BF)
    ar_o[...] = ar
    x2 = x[...].astype(F32) + dot(ar, w_out())
    z2, r2 = norm_stats(x2)
    g2 = vec[2:3]
    a2 = (z2 * g2 + vec[3:4]).astype(BF)
    a2_o[...] = a2
    dy = dy_r[...]
    mixed = x2 + vec[4:5]
    da2 = jnp.zeros_like(x2)
    k0 = math.sqrt(2.0 / math.pi)
    k1 = 0.044715 * k0
    for j in range(wide):
        cols = slice(j * width, (j + 1) * width)
        pre = dot(a2, w_up(j)) + b_up[j : j + 1]
        sq = pre * pre
        t = jnp.tanh(pre * (k0 + k1 * sq))
        half = 0.5 + 0.5 * t
        act = pre * half
        slope = half + act * (1.0 - t) * (k0 + (3.0 * k1) * sq)
        gr = act.astype(BF)
        gr_s[:, cols] = gr
        leave(0, j, blk).start()
        mixed += dot(gr, w_down(j))
        dpre = (dot_nt(dy, w_down(j)) * slope).astype(BF)
        dpre_s[:, cols] = dpre
        leave(1, j, blk).start()
        da2 += dot_nt(dpre, w_up(j))
        vup_o[j : j + 1] += jnp.sum(dpre.astype(F32), 0, keepdims=True)
    mixed_o[...] = mixed.astype(BF)
    dyf = dy.astype(F32)
    dz = da2 * g2
    m1 = jnp.sum(dz, -1, keepdims=True) * (1.0 / width)
    m2 = jnp.sum(dz * z2, -1, keepdims=True) * (1.0 / width)
    dx2 = dyf + r2 * (dz - m1 - z2 * m2)
    dx_o[...] = dx2
    vec_o[2:3, :] += jnp.sum(da2 * z2, 0, keepdims=True)
    vec_o[3:4, :] += jnp.sum(da2, 0, keepdims=True)
    vec_o[4:5, :] += jnp.sum(dyf, 0, keepdims=True)
    do = dx2.astype(BF)
    do_o[...] = do
    dattn = keep * dot_nt(do, w_out()).astype(BF).astype(F32)
    dnum = dattn * inv
    dden = -dnum * num_s[...] * inv
    low = lane_low(x.shape[0])
    for p in range(PAIRS):
        lanes = slice(128 * p, 128 * p + 128)
        mine = dnum[:, lanes]
        swap = pltpu.roll(dden[:, lanes], HEAD, 1)
        h = 2 * p
        grads_o[:, 128 * h : 128 * h + 128] = jnp.where(low, mine, swap).astype(BF)
        grads_o[:, 128 * h + 128 : 128 * h + 256] = jnp.where(low, swap, mine).astype(BF)

    def gather(c, rows, first):
        mask = cell_mask(bounds, c, first, 128)
        for h in range(HEADS):
            part = grads_o[rows, 128 * h : 128 * h + 128]
            part = jnp.where(mask, part.astype(F32), 0.0).astype(BF)
            acc[c, h] += dot_tn(part, pq[rows, FEATS * h : FEATS * (h + 1)])

    over_cells(bounds, blk, cells, x.shape[0], gather)

    @pl.when(blk == pl.num_programs(0) - 1)
    def _():
        store_sums(acc, sums_o, cells, True)
        full_out.wait()
        for j in range(wide):
            leave(0, j, blk).wait()
            leave(1, j, blk).wait()


def run_middle(bounds, x, dy, padding, pq, vec, b_up, sums, pieces, places, ff, cells):
    n, d = x.shape
    wide = HEADS * 128
    full = (cells, HEADS, 128, FEATS)
    scratch = [
        pltpu.VMEM(full, F32), pltpu.VMEM((WIDE_BLK, d), F32), pltpu.VMEM((WIDE_BLK, d), F32), pltpu.VMEM(full, BF),
        pltpu.VMEM((WIDE_BLK, ff), BF), pltpu.VMEM((WIDE_BLK, ff), BF), pltpu.SemaphoreType.DMA((3, ff // d)),
    ]
    if places:
        rows = max(hi for _, _, hi in places)
        chips = 1 + max(m for masks, _, _ in places for m in masks)
        number = 2 * sum(len(masks) for masks, _, _ in places)
        scratch += [pltpu.VMEM((chips, 2, rows, d), BF), pltpu.SemaphoreType.DMA((number,))]
    return pl.pallas_call(
        functools.partial(middle_kernel, cells, n, len(sums), places),
        grid=(n // WIDE_BLK,),
        in_specs=[
            SMEM, wide_spec(d), wide_spec(d), pl.BlockSpec((1, WIDE_BLK), lambda i: (0, i)), wide_spec(HEADS * FEATS), whole_spec(vec.shape), whole_spec(b_up.shape),
        ]
        + whole_specs(sums)
        + ([ANY] * len(pieces) if places else whole_specs(pieces)),
        out_specs=[
            wide_spec(d), HBM, HBM, wide_spec(d), wide_spec(d), wide_spec(d),
            wide_spec(d), wide_spec(wide), whole_spec((16, d)), whole_spec((8, d)),
            whole_spec(sums_shape(cells)), HBM,
        ],
        out_shape=[
            shape(n, d), shape(n, ff), shape(n, ff), shape(n, d), shape(n, d), shape(n, d),
            shape(n, d, kind=F32), shape(n, wide), shape(16, d, kind=F32), shape(8, d, kind=F32),
            shape(*sums_shape(cells)), shape(*full),
        ],
        scratch_shapes=scratch,
        compiler_params=params(),
        cost_estimate=cost(14, 30),
        name="middle",
    )(bounds, x, dy, padding, pq, vec, b_up, *sums, *pieces)


def phi_back(s, feats, rhs, low):
    r0 = dot_nt(feats[0].astype(BF), rhs[0])
    r1 = dot_nt(feats[1].astype(BF), rhs[1])
    total = pltpu.roll(jnp.where(low, r1, r0), HEAD, 1)
    return (jnp.where(low, r0, r1) - s * total) * SCALE


def query_back_kernel(cells, bounds, grads, pq, sq, full, bank, a1, dq_o, gq_o, sum_o, g_s, rhs):
    blk = pl.program_id(0)

    @pl.when(blk == 0)
    def _():
        back_parts(bank, rhs)
        gq_o[...] = jnp.zeros_like(gq_o)
        sum_o[...] = jnp.zeros_like(sum_o)

    low = lane_low(BLK)

    def one(c, rows, first):
        mask = cell_mask(bounds, c, first, FEATS)
        for h in range(HEADS):
            cols = slice(FEATS * h, FEATS * (h + 1))
            g = dot(grads[rows, 128 * h : 128 * h + 128], full[c, h])
            g_s[rows, cols] = jnp.where(mask, g, g_s[rows, cols])

    over_cells(bounds, blk, cells, BLK, one)
    for p in range(PAIRS):
        lanes = slice(128 * p, 128 * p + 128)
        feats = []
        for odd in (0, 1):
            cols = slice(FEATS * (2 * p + odd), FEATS * (2 * p + odd + 1))
            feats.append(g_s[:, cols] * pq[:, cols].astype(F32))
        dq_o[:, lanes] = phi_back(sq[:, lanes].astype(F32), feats, rhs, low).astype(BF)
    dq = dq_o[...]
    gq_o[...] += dot_tn(a1[...], dq)
    sum_o[0:1] += jnp.sum(dq.astype(F32), 0, keepdims=True)


def run_query_back(bounds, grads, pq, sq, full, bank, a1, cells):
    n, d = sq.shape
    return pl.pallas_call(
        functools.partial(query_back_kernel, cells),
        grid=(n // BLK,),
        in_specs=[
            SMEM, rows_spec(HEADS * 128), rows_spec(HEADS * FEATS), rows_spec(d),
            whole_spec(full.shape), whole_spec(bank.shape), rows_spec(d),
        ],
        out_specs=[rows_spec(d), whole_spec((d, d)), whole_spec((8, d))],
        out_shape=[shape(n, d), shape(d, d, kind=F32), shape(8, d, kind=F32)],
        scratch_shapes=[pltpu.VMEM((BLK, HEADS * FEATS), F32), pltpu.VMEM((2, 128, FEATS), BF)],
        compiler_params=params(),
        cost_estimate=cost(3, 8),
        name="query_back",
    )(bounds, grads, pq, sq, full, bank, a1)


def weight_kernel(rows, a2, dpre, gr, dy, ar, do, top_k, top_s, low_k, low_s, ar_s, do_s, sems):
    j = pl.program_id(0)
    last = pl.num_programs(0) - 1
    d = a2.shape[1]
    made = [pltpu.make_async_copy(src, dst, sems.at[i]) for i, (src, dst) in enumerate(((ar, ar_s), (do, do_s)))]

    def put(value, kept, sent):
        count, size = kept.shape[:2]
        mine, theirs = both_cores(value.reshape(count, 2, size, d))
        kept[...] = mine.astype(BF)
        sent[...] = theirs.astype(BF)

    @pl.when(j == 0)
    def _():
        for copy in made:
            copy.start()

    @pl.when(j < last)
    def _():
        put(dot_tn(a2[...], dpre[...]), top_k, top_s)
        put(dot_tn(gr[...], dy[...]), low_k, low_s)

    @pl.when(j == last)
    def _():
        for copy in made:
            copy.wait()
        put(dot_tn(ar_s[...], do_s[...]), top_k, top_s)


def run_weights(a2, dpre, gr, dy, ar, do, rows):
    n, d = a2.shape
    wide = dpre.shape[1] // d
    chips = d // (2 * rows)
    cols = pl.BlockSpec((n, d), lambda j: (0, jnp.minimum(j, wide - 1)))
    whole = whole_spec((n, d))
    top = pl.BlockSpec((chips, rows, d), lambda j: (0, j, 0))
    low = pl.BlockSpec((chips // wide, rows * wide, d), lambda j: (jnp.minimum(j, wide - 1), 0, 0))
    tops, lows = shape(chips, rows * (wide + 1), d), shape(chips, rows * wide, d)
    return pl.pallas_call(
        functools.partial(weight_kernel, rows),
        grid=(wide + 1,),
        in_specs=[whole, cols, cols, whole, HBM, HBM],
        out_specs=[top, top, low, low],
        out_shape=[tops, tops, lows, lows],
        scratch_shapes=[pltpu.VMEM((n, d), BF), pltpu.VMEM((n, d), BF), pltpu.SemaphoreType.DMA((2,))],
        compiler_params=params(),
        cost_estimate=cost(5, 20),
        name="weights",
    )(a2, dpre, gr, dy, ar, do)


def fold_kernel(parts, *refs):
    ins, outs, bufs, sems = refs[:4], refs[4 : 4 + parts], refs[4 + parts : 8 + parts], refs[8 + parts]
    me = lax.axis_index("dp")
    size = ins[0].shape[0] // parts
    made = []
    for k in range(parts):
        rows = pl.ds((me ^ k) * size, size)
        for i in range(4):
            made.append(pltpu.make_async_copy(ins[i].at[rows], bufs[i].at[k], sems.at[k, i]))
    for copy in made:
        copy.start()
    cut = ins[0].shape[1]
    for k in range(parts):
        for copy in made[4 * k : 4 * k + 4]:
            copy.wait()
        outs[k][:, :cut] = (bufs[0][k].astype(F32) + bufs[1][k].astype(F32)).astype(BF)
        outs[k][:, cut:] = (bufs[2][k].astype(F32) + bufs[3][k].astype(F32)).astype(BF)


def run_fold(top, top_got, low, low_got, parts):
    size, d = top.shape[0] // parts, top.shape[2]
    out = shape(size, top.shape[1] + low.shape[1], d)
    bufs = [pltpu.VMEM((parts, size) + v.shape[1:], BF) for v in (top, top_got, low, low_got)]
    return pl.pallas_call(
        functools.partial(fold_kernel, parts),
        in_specs=[HBM, ANY, HBM, ANY],
        out_specs=[VM] * parts,
        out_shape=[out] * parts,
        scratch_shapes=bufs + [pltpu.SemaphoreType.DMA((parts, 4))],
        compiler_params=pltpu.CompilerParams(vmem_limit_bytes=16 * 1024 * 1024),
        cost_estimate=cost(0.001, 7),
        name="fold",
    )(top, top_got, low, low_got)


def key_back_kernel(cells, slots, nsums, paired, rows, wide, bounds, a1, pk, vr, sk, gvec, vup, bank, w, gq, qsum, *refs):
    sums, refs = refs[:nsums], refs[nsums:]
    dk_o, dv_o, outs = refs[0], refs[1], refs[2 : 4 if paired else 3]
    full, g_s, v_s, rhs, gk_s, gv_s, sum_s, w_s, gq_s, sems = refs[4 if paired else 3 :]
    made = [pltpu.make_async_copy(a, b, sems.at[i]) for i, (a, b) in enumerate(((w, w_s), (gq, gq_s)))]
    blk = pl.program_id(0)
    d = a1.shape[1]

    @pl.when(blk == 0)
    def _():
        for copy in made:
            copy.start()
        gk_s[...] = jnp.zeros_like(gk_s)
        gv_s[...] = jnp.zeros_like(gv_s)
        sum_s[...] = qsum[...]
        back_parts(bank, rhs)
        load_sums(bounds, sums, full, slots, cells, True)

    low = lane_low(BLK)

    def one(c, rows, first):
        mask = cell_mask(bounds, c, first, FEATS)
        narrow = cell_mask(bounds, c, first, 128)
        low = lane_low(SUB)
        for p in range(PAIRS):
            lanes = slice(128 * p, 128 * p + 128)
            v = vr[rows, lanes].astype(F32)
            outs = []
            for odd in (0, 1):
                h = 2 * p + odd
                cols = slice(FEATS * h, FEATS * (h + 1))
                aug = (jnp.where(low, 1.0, v) if odd else jnp.where(low, v, 1.0)).astype(BF)
                g = dot(aug, full[c, h])
                g_s[rows, cols] = jnp.where(mask, g, g_s[rows, cols])
                outs.append(dot_nt(pk[rows, cols], full[c, h]))
            v_s[rows, lanes] = jnp.where(narrow, jnp.where(low, outs[0], outs[1]), v_s[rows, lanes])

    over_cells(bounds, blk, cells, BLK, one)
    for p in range(PAIRS):
        lanes = slice(128 * p, 128 * p + 128)
        feats = []
        for odd in (0, 1):
            cols = slice(FEATS * (2 * p + odd), FEATS * (2 * p + odd + 1))
            feats.append(g_s[:, cols] * pk[:, cols].astype(F32))
        dk_o[:, lanes] = phi_back(sk[:, lanes].astype(F32), feats, rhs, low).astype(BF)
    dk = dk_o[...]
    dv = v_s[...].astype(BF)
    dv_o[...] = dv
    gk_s[...] += dot_tn(a1[...], dk)
    gv_s[...] += dot_tn(a1[...], dv)
    sum_s[1:2] += jnp.sum(dk.astype(F32), 0, keepdims=True)
    sum_s[2:3] += jnp.sum(dv.astype(F32), 0, keepdims=True)

    @pl.when(blk == pl.num_programs(0) - 1)
    def _():
        for copy in made:
            copy.wait()
        gain = w_s[:, 3 * d : 3 * d + 1].astype(F32)
        shift = w_s[:, 3 * d + 1 : 3 * d + 2].astype(F32)
        total = jnp.zeros((d, 1), F32)
        plain = jnp.zeros((d, 1), F32)

        def put(lo, value):
            cols = slice(lo, lo + value.shape[1])
            if paired:
                kept, sent = both_cores(value.reshape(outs[0].shape[0], 2, rows, value.shape[1]))
                outs[0][:, :, cols] = kept.astype(BF)
                outs[1][:, :, cols] = sent.astype(BF)
            else:
                outs[0][:, cols] = value.astype(BF)

        for i, grad in enumerate((gq_s, gk_s, gv_s)):
            weight = w_s[:, i * d : (i + 1) * d].astype(F32)
            line = sum_s[i : i + 1]
            total += jnp.sum(weight * grad[...], -1, keepdims=True)
            plain += jnp.sum(weight * line, -1, keepdims=True)
            put(i * d, grad[...])
        lines = [gvec[i : i + 1] for i in range(5)] + by_owner(vup[...], rows, wide)
        vt = pad_rows(lines, 128).T
        lane = lax.broadcasted_iota(jnp.int32, vt.shape, 1)
        vt = jnp.where(lane == 0, (total - shift * plain) / gain, jnp.where(lane == 1, plain, vt))
        put(3 * d, vt)


def run_key_back(bounds, a1, pk, vr, sk, gvec, vup, bank, w, gq, qsum, sums, rows, wide, paired, cells):
    n, d = a1.shape
    total = w.shape[1]
    gout = [(d // (2 * rows), rows, total)] * 2 if paired else [(d, total)]
    square = pltpu.VMEM((d, d), F32)
    return pl.pallas_call(
        functools.partial(key_back_kernel, cells, n, len(sums), paired, rows, wide),
        grid=(n // BLK,),
        in_specs=[SMEM, rows_spec(d), rows_spec(HEADS * FEATS), rows_spec(d), rows_spec(d)]
        + whole_specs((gvec, vup, bank)) + [HBM, HBM] + whole_specs((qsum,))
        + whole_specs(sums),
        out_specs=[rows_spec(d), rows_spec(d)] + [whole_spec(g) for g in gout],
        out_shape=[shape(n, d), shape(n, d)] + [shape(*g) for g in gout],
        scratch_shapes=[
            pltpu.VMEM((cells, HEADS, 128, FEATS), BF),
            pltpu.VMEM((BLK, HEADS * FEATS), F32),
            pltpu.VMEM((BLK, d), F32),
            pltpu.VMEM((2, 128, FEATS), BF),
            square,
            square,
            pltpu.VMEM((8, d), F32),
            pltpu.VMEM(w.shape, BF),
            square,
            pltpu.SemaphoreType.DMA((2,)),
        ],
        compiler_params=params(),
        cost_estimate=cost(6, 14),
        name="key_back",
    )(bounds, a1, pk, vr, sk, gvec, vup, bank, w, gq, qsum, *sums)


def token_back_kernel(x, dq, dk, dv, dx, vec, w, gt_o):
    d = x.shape[1]
    da1 = dot_nt(dq[...], w[:, :d]) + dot_nt(dk[...], w[:, d : 2 * d]) + dot_nt(dv[...], w[:, 2 * d : 3 * d])
    z, r = norm_stats(x[...].astype(F32))
    dz = da1 * vec[0:1]
    m1 = jnp.sum(dz, -1, keepdims=True) * (1.0 / d)
    m2 = jnp.sum(dz * z, -1, keepdims=True) * (1.0 / d)
    gt_o[...] = dx[...] + r * (dz - m1 - z * m2)


def run_token_back(x, dq, dk, dv, dx, vec, w):
    n, d = x.shape
    return pl.pallas_call(
        token_back_kernel,
        grid=(n // WIDE_BLK,),
        in_specs=[wide_spec(d)] * 5 + whole_specs((vec, w)),
        out_specs=wide_spec(d),
        out_shape=shape(n, d, kind=F32),
        compiler_params=params(40 * 1024 * 1024),
        cost_estimate=cost(2, 8),
        name="token_back",
    )(x, dq, dk, dv, dx, vec, w)


AXES = ("dp", "fsdp")
Z_ALL = (0, 1, 2, 3)
LEAD_MASKS = (Z_ALL, (4, 5, 6, 7), (8, 9, 10, 11), (12, 13, 14, 15))


def flip(x, axis, size, mask):
    return lax.ppermute(x, axis, [(i, i ^ mask) for i in range(size)])


def to_core(x, fsdp):
    return flip(x, "fsdp", fsdp, 1)


def to_z(x, fsdp, mask):
    return flip(x, "fsdp", fsdp, 2 * mask)


def tie(*values):
    return lax.optimization_barrier(values)


def same_core_groups(dp, fsdp):
    return [[d * fsdp + 2 * z + c for d in range(dp) for z in range(fsdp // 2)] for c in range(2)]


def chip_groups(fsdp):
    return [[2 * z + c for z in range(fsdp // 2)] for c in range(2)]


def pack_kernel(wide, w_qkv, g1, s1, w_out, g2, s2, w_up, b_up, w_down, b_down, lead, body):
    rows = w_qkv.shape[0]
    d = w_out.shape[1]
    total = w_qkv.shape[1]
    place = lax.broadcasted_iota(jnp.int32, (128, rows), 0)
    up = b_up[...].astype(F32).reshape(1, -1)
    lines = [v[...].astype(F32).reshape(1, -1) for v in (g1, s1, g2, s2, b_down)]
    lines += [up[:, j * rows : (j + 1) * rows] for j in range(wide)]
    table = jnp.zeros((128, rows), F32)
    for i, line in enumerate(lines):
        table = jnp.where(place == i, line, table)
    across = lax.broadcasted_iota(jnp.int32, (rows, rows), 0) == lax.broadcasted_iota(jnp.int32, (rows, rows), 1)
    lead[:, :total] = w_qkv[...]
    lead[:, total:] = dot_nt(jnp.where(across, 1.0, 0.0).astype(BF), table.astype(BF)).astype(BF)
    body[:rows] = w_out[...]
    for j in range(wide):
        body[rows * (1 + j) : rows * (2 + j)] = w_up[:, j * d : (j + 1) * d]
    body[rows * (1 + wide) :] = w_down[...]


def final_kernel(rows, wide, count, *refs):
    parts, outs = refs[:count], refs[2 * count :]
    wout, wup, wdown, wqkv, *lines = outs
    d = wout.shape[1]
    add = lambda refs: functools.reduce(lambda a, b: a + b, [v[...].astype(F32) for v in refs])
    total = add(refs[count : 2 * count])
    for j in range(wide):
        wup[:, j * d : (j + 1) * d] = total[rows * j : rows * (j + 1)]
    wout[...] = total[rows * wide : rows * (1 + wide)]
    wdown[...] = total[rows * (1 + wide) :]
    total = add(parts)
    cols = wqkv.shape[1]
    wqkv[...] = total[:, :cols]
    table = total[:, cols:].T
    for i in range(5):
        lines[i][...] = table[i]
    lines[5][...] = jnp.concatenate([table[5 + j : 6 + j] for j in range(wide)], 1)[0]


def run_final(lead_parts, body_parts, rows, wide):
    d = body_parts[0].shape[1]
    return pl.pallas_call(
        functools.partial(final_kernel, rows, wide, len(lead_parts)),
        in_specs=[VM] * (2 * len(lead_parts)),
        out_specs=[VM] * 10,
        out_shape=[
            shape(rows, d, kind=F32), shape(rows, wide * d, kind=F32), shape(rows * wide, d, kind=F32),
            shape(rows, 3 * d, kind=F32),
        ]
        + [shape(rows, kind=F32)] * 5
        + [shape(rows * wide, kind=F32)],
        name="final",
    )(*lead_parts, *body_parts)


def local(dp, fsdp, tokens, bounds, padding, bank, ln1_gain, ln1_bias, w_qkv, w_out, ln2_gain, ln2_bias,
          w_up, b_up, w_down, b_down, cotangent):
    ndev = dp * fsdp
    x = tokens[0]
    dy = cotangent[0]
    n, d = x.shape
    ff = w_up.shape[1]
    cells = bounds.shape[1] - 1
    chips = fsdp // 2
    rows = d // ndev
    wide = ff // d
    frow = ff // ndev
    paired = dp == 4 and fsdp == 8

    shards = (w_qkv, ln1_gain, ln1_bias, w_out, ln2_gain, ln2_bias, w_up, b_up, w_down, b_down)
    if paired:
        lead, body = pl.pallas_call(
            functools.partial(pack_kernel, wide),
            in_specs=[VM] * len(shards),
            out_specs=[VM, VM],
            out_shape=[shape(rows, 3 * d + 128), shape(rows * (1 + wide) + frow, d)],
            name="pack",
        )(*shards)
    else:
        vecs = jnp.concatenate([ln1_gain, ln1_bias, ln2_gain, ln2_bias, b_down, b_up]).reshape(5 + wide, rows)
        lead = jnp.concatenate([w_qkv, jnp.pad(vecs, ((0, 128 - 5 - wide), (0, 0))).T], 1)
        body = jnp.concatenate([w_out] + [w_up[:, j * d : (j + 1) * d] for j in range(wide)] + [w_down], 0)
    cut = rows * (1 + wide)

    if paired:
        first = jnp.stack([lead] + [to_z(lead, fsdp, k) for k in (1, 2, 3)])
        lead_own = [first] + [flip(first, "dp", dp, k) for k in (1, 2, 3)]
        pair = jnp.stack([body, to_z(body, fsdp, 1)])
        pair, *lead_own = tie(pair, *lead_own)
        lead_pieces = lead_own + [to_core(v, fsdp) for v in lead_own]
        four = jnp.concatenate([pair, to_z(pair, fsdp, 2)])
        lead_places = tuple((m, 0, rows) for m in LEAD_MASKS)
    else:
        lead_pieces = [lax.all_gather(lead, AXES, axis=0, tiled=True)]
        parts = lax.all_gather(body, AXES, axis=0)
        take = lambda lo, size: parts[:, lo : lo + size].reshape(ndev * size, d)
        body_pieces = [
            take(0, rows), jnp.concatenate([take((1 + j) * rows, rows) for j in range(wide)], 1), take(cut, frow),
        ]
        lead_places = body_places = None

    def far_sums(out):
        return lax.all_to_all(out, "fsdp", 0, 0, axis_index_groups=chip_groups(fsdp), tiled=True)

    a1, sk, pk, vr, sums, vec, *w = run_keys(bounds, x, padding, bank, lead_pieces, lead_places, cells)
    w = w[0].reshape(d, -1) if paired else lead_pieces[0]
    if paired:
        sums, four = tie(sums, four)
        sums = [sums, to_core(sums, fsdp)]
        out = run_spread(bounds, *sums, chips, n, cells)
        a1_q, out = tie(a1, out)
        far = far_sums(out)
        up, down = four[:, :cut], four[:, cut:]
        up_x, down_y = flip(up, "dp", dp, 1), flip(down, "dp", dp, 2)
        up_y = flip(jnp.concatenate([up, up_x]), "dp", dp, 2)
        down_x = flip(jnp.concatenate([down, down_y]), "dp", dp, 1)
        sq, pq, up_line = run_queries(a1_q, w, bank, vec, rows, wide)
        early = [to_core(v, fsdp) for v in (four, up_x, down_y)]
        up_y, down_x, pq, up_line, *early = tie(up_y, down_x, pq, up_line, *early)
        body_pieces = [four, up_x, down_y, up_y, down_x] + early + [to_core(v, fsdp) for v in (up_y, down_x)]
        body_places = (
            (Z_ALL, 0, cut + frow), ((4, 5, 6, 7), 0, cut), ((8, 9, 10, 11), cut, cut + frow),
            ((8, 9, 10, 11, 12, 13, 14, 15), 0, cut), ((4, 5, 6, 7, 12, 13, 14, 15), cut, cut + frow),
        )
        sums = sums + [far, to_core(far, fsdp)]
    else:
        sums = [lax.psum(sums, "fsdp")]
        sq, pq, up_line = run_queries(a1, w, bank, vec, rows, wide)
    mixed, gr, dpre, a2, ar, do, dx2, grads, gvec, vup, sums, full = run_middle(
        bounds, x, dy, padding, pq, vec, up_line, sums, body_pieces, body_places, ff, cells
    )
    back = lambda gq, qsum, sums: run_key_back(
        bounds, a1, pk, vr, sk, gvec, vup, bank, w, gq, qsum, sums, rows, wide, paired, cells
    )
    if paired:
        top, top_sent, low, low_sent = run_weights(a2, dpre, gr, dy, ar, do, rows)
        got, top_sent, low_sent = tie(to_core(sums, fsdp), top_sent, low_sent)
        sums = [sums, got]
        out = run_spread(bounds, *sums, chips, n, cells)
        far = far_sums(out)
        plus = lambda *parts: functools.reduce(lambda a, b: a + b, [v.astype(F32) for v in parts]).astype(BF)
        pick = lambda value, at, dim: lax.dynamic_index_in_dim(value, at, dim, keepdims=False)
        folded = run_fold(top, to_core(top_sent, fsdp), low, to_core(low_sent, fsdp), dp)
        grads, *folded = tie(grads, *folded)
        spread = [flip(v, "dp", dp, k) for k, v in enumerate(folded) if k]
        dq, gq, qsum = run_query_back(bounds, grads, pq, sq, full, bank, a1, cells)
        far, gq, qsum = tie(far, gq, qsum)
        dk, dv, kept, sent = back(gq, qsum, sums + [far, to_core(far, fsdp)])
        kept, sent, *spread = tie(kept, sent, *spread)
        whole = plus(folded[0], *spread)
        zpos = lax.axis_index("fsdp") // 2
        parts = [pick(whole, zpos, 0)] + [to_z(pick(whole, zpos ^ k, 0), fsdp, k) for k in (1, 2, 3)]
        half = plus(kept, to_core(sent, fsdp)).reshape((dp, chips) + kept.shape[1:])
        dpos = lax.axis_index("dp")
        half = plus(pick(half, dpos, 0), *[flip(pick(half, dpos ^ k, 0), "dp", dp, k) for k in (1, 2, 3)])
        lead_parts = [pick(half, zpos, 0)] + [to_z(pick(half, zpos ^ k, 0), fsdp, k) for k in (1, 2, 3)]
        wout, wup, wdown, wqkv, *vecs = run_final(lead_parts, parts, rows, wide)
    else:
        dq, gq, qsum = run_query_back(bounds, grads, pq, sq, full, bank, a1, cells)
        dk, dv, glead = back(gq, qsum, [lax.psum(sums, "fsdp")])
        gup = dot_tn(a2, dpre)
        blocks = lambda g, size: g.reshape(ndev, size, d)
        gbody = jnp.concatenate(
            [blocks(dot_tn(ar, do), rows)]
            + [blocks(gup[:, j * d : (j + 1) * d], rows) for j in range(wide)]
            + [blocks(dot_tn(gr, dy), frow)], 1
        )
        gbody = lax.psum_scatter(gbody, AXES, scatter_dimension=0, tiled=True)[0]
        glead = lax.psum_scatter(glead.astype(F32), AXES, scatter_dimension=0, tiled=True)
        gvec = glead[:, 3 * d :].T
        vecs = [gvec[i] for i in range(5)] + [gvec[5 : 5 + wide].reshape(-1)]
        wqkv, wout, wdown = glead[:, : 3 * d], gbody[:rows], gbody[cut:]
        wup = jnp.concatenate([gbody[(1 + j) * rows : (2 + j) * rows] for j in range(wide)], 1)
    gt = run_token_back(x, dq, dk, dv, dx2, vec, w)
    return (
        mixed[None], gt[None], vecs[0], vecs[1], wqkv, wout, vecs[2], vecs[3], wup, vecs[5], wdown, vecs[4],
    )


def solution(mesh):
    both = P(("dp", "fsdp"))
    mat = P(("dp", "fsdp"), None)
    act = P("dp", "fsdp", None)
    return jax.shard_map(
        functools.partial(local, mesh.shape["dp"], mesh.shape["fsdp"]),
        mesh=mesh,
        in_specs=(act, P("dp", None), P("dp", "fsdp"), P(), both, both, mat, mat, both, both, mat, both, mat, both, act),
        out_specs=(act, act, both, both, mat, mat, both, both, mat, both, mat, both),
        check_vma=False,
    )
```
